32 devices in a mesh: row: 4 (over z), col: 8 (over y, x, core).
Axes of the slice: x: 2, y: 2, z: 4, core: 2. Of those that a mesh axis runs over, the one named last changes fastest.
Arguments:
- points: float32 [4096, 128], P('row'), may hold values from -6 to 6
- panel_pool: float32 [4096, 128], P('col'), may hold values from -6 to 6
- order: int32 [512], replicated, may hold values from 0 to 511, each once
- panel_index: int32 [1], replicated, may hold values from 0 to 7
- inv_factor: float32 [512, 512], replicated, as said below
- ard_weights: float32 [128], replicated, may hold values from 0.001 to 0.1
- noise: float32 [4096], P('row'), may hold values from 0.05 to 1
Outputs:
- schur: float32 [4096, 4096], P('row', 'col')
The draws below stay inside these ranges and needn't reach their ends.
Inputs may be any that keep to these rules, and one draw needn't show every extreme that they name: `order`: a permutation of 0 to 511. `inv_factor`: lower triangular: zero above the diagonal.
All inputs are finite; a program needn't handle non-finite values.
Results may differ from the reference program's by a relative error of at most 0.0003.
Values sent between devices are 32-bit elements; how exact they have to be, the bound alone decides.
No kernel may reach another device: no remote copies, remote signals or barrier semaphores. Data moves between devices by JAX's collectives and lax.ppermute only.
A program may use at most 64 MiB of HBM per device.

```python
import math
import jax
import jax.numpy as jnp
from jax import lax

FEATURES = 128
PANEL = 512
ROWS_DEV = 1024
TRAIL = 4096
PANELS = 8
POOL = 4096
N_ROW = 4


def draw_inv_factor(key, part):
    first_key, second_key = jax.random.split(jax.random.fold_in(key, 17))
    row_ids = lax.broadcasted_iota(jnp.int32, (PANEL, PANEL), 0)
    col_ids = lax.broadcasted_iota(jnp.int32, (PANEL, PANEL), 1)
    below = jax.random.normal(first_key, (PANEL, PANEL), jnp.float32) * (6.0 / PANEL)
    diagonal = jnp.exp(jax.random.uniform(second_key, (PANEL,), jnp.float32, math.log(0.1), math.log(0.4)))
    lower = jnp.where(row_ids > col_ids, below, jnp.float32(0.0))
    return lower + jnp.where(row_ids == col_ids, diagonal[:, None], jnp.float32(0.0))


def levels(stream_key, dims, shards, low, top_value):
    level, own = 1.0, jax.random.fold_in(stream_key, 6)
    for dim, parts in shards:
        draws = jnp.exp(jax.random.uniform(jax.random.fold_in(own, dim), (parts,), jnp.float32, low / len(shards), top_value / len(shards)))
        level = level * jnp.repeat(draws, dims[dim] // parts).reshape([-1 if axis == dim else 1 for axis in range(len(dims))])
    return level


def normal_values(own_key, extent, deviation, bound, pieces=(), kind=jnp.bfloat16):
    array = deviation * jax.random.normal(own_key, extent, jnp.float32)
    if pieces:
        array = array * levels(own_key, extent, pieces, -0.22, 0.18)
    return jnp.clip(array, -bound, bound).astype(kind)


def setup_inputs(seed: int = 0) -> dict:
    seeds = jax.random.split(jax.random.key(seed), 8)
    points = normal_values(seeds[0], (TRAIL, FEATURES), 1.0, 6.0, ((0, 4),), jnp.float32)
    panel_pool = normal_values(seeds[1], (POOL, FEATURES), 1.0, 6.0, ((0, 8),), jnp.float32)
    order = jax.random.permutation(seeds[2], PANEL).astype(jnp.int32)
    panel_index = jax.random.randint(seeds[3], (1,), 0, PANELS).astype(jnp.int32)
    inv_factor = draw_inv_factor(jax.random.fold_in(seeds[7], 71), 0)
    ard_weights = jnp.clip(jnp.exp(jax.random.uniform(seeds[5], (FEATURES,), jnp.float32, math.log(0.001), math.log(0.1))), 0.001, 0.1)
    noise = jnp.clip(jnp.exp(math.log(1.0) - 2.9957323 * jax.random.uniform(seeds[6], (TRAIL,), jnp.float32) ** levels(seeds[6], (TRAIL,), ((0, 4),), -0.2, 0.2)), 0.05, 1.0)
    return {"points": points, "panel_pool": panel_pool, "order": order, "panel_index": panel_index, "inv_factor": inv_factor, "ard_weights": ard_weights, "noise": noise}


amplitude = 2.0


def kernel_block(left_side, right_side, weights):
    scaled = left_side * weights[None, :]
    left_square = jnp.sum(scaled * left_side, axis=1)
    right_square = jnp.sum(right_side * right_side * weights[None, :], axis=1)
    cross_term = lax.dot_general(scaled, right_side, (((1,), (1,)), ((), ())), precision=lax.Precision.HIGHEST, preferred_element_type=jnp.float32)
    return amplitude * jnp.exp(-0.5 * (left_square[:, None] + right_square[None, :] - 2.0 * cross_term))


def factor_rows(row_points, chosen, inv_factor, weights):
    kernel_part = kernel_block(row_points, chosen, weights)
    return lax.dot_general(kernel_part, inv_factor, (((1,), (1,)), ((), ())), precision=lax.Precision.HIGHEST, preferred_element_type=jnp.float32)


def reference(points, panel_pool, order, panel_index, inv_factor, ard_weights, noise):
    start = (panel_index[0] * PANEL).astype(jnp.int32)
    block_points = lax.dynamic_slice_in_dim(panel_pool, start, PANEL, 0)
    chosen = jnp.take(block_points, order, axis=0)
    factored = factor_rows(points, chosen, inv_factor, ard_weights)

    def one_block(block_number):
        first = (block_number * ROWS_DEV).astype(jnp.int32)
        row_points = lax.dynamic_slice_in_dim(points, first, ROWS_DEV, 0)
        panel_part = lax.dynamic_slice_in_dim(factored, first, ROWS_DEV, 0)
        noise_part = lax.dynamic_slice_in_dim(noise, first, ROWS_DEV, 0)
        kernel_tile = kernel_block(row_points, points, ard_weights)
        row_ids = lax.broadcasted_iota(jnp.int32, (ROWS_DEV, TRAIL), 0) + first
        col_ids = lax.broadcasted_iota(jnp.int32, (ROWS_DEV, TRAIL), 1)
        kernel_tile = kernel_tile + jnp.where(row_ids == col_ids, noise_part[:, None], jnp.float32(0.0))
        update = lax.dot_general(panel_part, factored, (((1,), (1,)), ((), ())), precision=lax.Precision.HIGHEST, preferred_element_type=jnp.float32)
        return kernel_tile - update

    blocks = lax.map(one_block, jnp.arange(N_ROW, dtype=jnp.int32))
    return blocks.reshape(TRAIL, TRAIL)
```

```python
import jax
import jax.numpy as jnp
from jax import lax
from jax.sharding import PartitionSpec as P

amplitude = 2.0


def kernel_block(left_side, right_side, weights):
    scaled = left_side * weights[None, :]
    left_square = jnp.sum(scaled * left_side, axis=1)
    right_square = jnp.sum(right_side * right_side * weights[None, :], axis=1)
    cross_term = lax.dot_general(
        scaled,
        right_side,
        (((1,), (1,)), ((), ())),
        precision=lax.Precision.HIGHEST,
        preferred_element_type=jnp.float32,
    )
    return amplitude * jnp.exp(
        -0.5 * (left_square[:, None] + right_square[None, :] - 2.0 * cross_term)
    )


def factor_rows(row_points, chosen, inv_factor, weights):
    kernel_part = kernel_block(row_points, chosen, weights)
    return lax.dot_general(
        kernel_part,
        inv_factor,
        (((1,), (1,)), ((), ())),
        precision=lax.Precision.HIGHEST,
        preferred_element_type=jnp.float32,
    )


def column_pairs(rows, cols):
    halves = cols // rows
    pairs = []
    for group in range(rows):
        for place in range(rows):
            target_row = group ^ place
            if target_row == group:
                continue
            for half in range(halves):
                source = group * cols + place * halves + half
                target = target_row * cols + group * halves + half
                pairs.append((source, target))
    return pairs


def swap(value, bit, cols):
    return lax.ppermute(value, "col", [(i, i ^ bit) for i in range(cols)])


def gather_panel(panel_pool, panel_block, cols):
    col_place = lax.axis_index("col")
    half_rows = panel_pool.shape[0] // 2
    core = col_place % 2
    mine = lax.dynamic_slice_in_dim(panel_pool, core * half_rows, half_rows, 0)
    others = lax.dynamic_slice_in_dim(panel_pool, (1 - core) * half_rows, half_rows, 0)
    got = swap(others, 1, cols)
    held = jnp.where(panel_block % 2 == core, mine, got)
    bit = 2
    while bit < cols:
        got = swap(held, bit, cols)
        held = jnp.where((panel_block ^ col_place) & bit == 0, held, got)
        bit *= 2
    got = swap(held, 1, cols)
    low = jnp.where(core == 0, held, got)
    high = jnp.where(core == 0, got, held)
    return jnp.concatenate([low, high], axis=0)


def on_device(points, panel_pool, order, panel_index, inv_factor, ard_weights, noise):
    row_count = points.shape[0]
    rows = lax.axis_size("row")
    cols = lax.axis_size("col")
    col_count = row_count * rows // cols
    halves = cols // rows
    row_place = lax.axis_index("row")
    col_place = lax.axis_index("col")
    own_half = lax.dynamic_slice_in_dim(points, col_place % halves * col_count, col_count, 0)
    sent = lax.ppermute(own_half, ("row", "col"), column_pairs(rows, cols))
    block = gather_panel(panel_pool, panel_index[0], cols)
    chosen = jnp.take(block, order, axis=0)
    col_points = jnp.where(row_place == col_place // halves, own_half, sent)
    kernel_tile = kernel_block(points, col_points, ard_weights)
    row_ids = lax.broadcasted_iota(jnp.int32, (row_count, col_count), 0) + row_place * row_count
    col_ids = lax.broadcasted_iota(jnp.int32, (row_count, col_count), 1) + col_place * col_count
    kernel_tile = kernel_tile + jnp.where(row_ids == col_ids, noise[:, None], jnp.float32(0.0))
    rows_panel = factor_rows(points, chosen, inv_factor, ard_weights)
    cols_panel = factor_rows(col_points, chosen, inv_factor, ard_weights)
    update = lax.dot_general(
        rows_panel,
        cols_panel,
        (((1,), (1,)), ((), ())),
        precision=lax.Precision.HIGHEST,
        preferred_element_type=jnp.float32,
    )
    return kernel_tile - update


def solution(mesh):
    in_specs = (P("row", None), P("col", None), P(), P(), P(), P(), P("row"))
    out_specs = P("row", "col")
    return jax.shard_map(
        on_device, mesh=mesh, in_specs=in_specs, out_specs=out_specs, check_vma=False
    )
```

```python
import functools

import jax
import jax.numpy as jnp
from jax import lax
from jax.experimental import pallas as pl
from jax.experimental.pallas import tpu as pltpu
from jax.sharding import PartitionSpec as P

log2_e = 1.4426950408889634
vmem_bytes = 32 * 1024 * 1024
f32, bf16 = jnp.float32, jnp.bfloat16


def halves_of(value):
    high = value.astype(bf16)
    low = (value - high.astype(f32)).astype(bf16)
    return high, low


def thirds_of(value):
    high = value.astype(bf16)
    rest = value - high.astype(f32)
    middle = rest.astype(bf16)
    low = (rest - middle.astype(f32)).astype(bf16)
    return high, middle, low


def pack_left(value):
    high, middle, low = thirds_of(value)
    return jnp.concatenate([high, middle, high, middle, high, low], axis=1)


def pack_right(value):
    high, middle, low = thirds_of(value)
    return jnp.concatenate([high, middle, middle, high, low, high], axis=0)


def product(left, right):
    return lax.dot_general(left, right, (((1,), (0,)), ((), ())), preferred_element_type=f32)


def product_of_halves(left, right):
    (left_high, left_low), (right_high, right_low) = left, right
    return (
        product(left_high, right_low) + product(left_low, right_high)
    ) + product(left_high, right_high)


def kern(left, left_half, right, right_half):
    return jnp.exp2((product(left, right) - left_half) - right_half + 1.0)


def factor_kernel(factor_ref, order_ref, high_ref, low_ref, turned_high_ref, turned_low_ref, pick_ref):
    factor = factor_ref[...]
    high_ref[...], low_ref[...] = halves_of(factor)
    turned_high_ref[...], turned_low_ref[...] = halves_of(jnp.transpose(factor))
    panel = factor.shape[0]
    core = lax.axis_index("col") % 2
    place = lax.broadcasted_iota(jnp.int32, (panel, panel), 0) + core * (panel // 2)
    place = jnp.where(place >= panel, place - panel, place)
    hit = jnp.where(place == order_ref[...], 1.0, 0.0).astype(f32)
    pick_ref[...] = jnp.transpose(hit).astype(bf16)


def tile_kernel(rows, cols, points_ref, sent_ref, scale_ref, noise_ref, tile_ref, right_ref, half_ref):
    row_place, col_place = lax.axis_index("row"), lax.axis_index("col")
    halves = cols // rows
    count = sent_ref.shape[0]
    part = col_place % halves
    start = pl.multiple_of(part * count, count)
    own = row_place == col_place // halves
    scale = scale_ref[...]
    col_points = jnp.where(own, points_ref[pl.ds(start, count), :], sent_ref[...])
    col_turned = jnp.transpose(col_points * scale)
    right = pack_right(col_turned)
    right_half = 0.5 * jnp.sum(col_turned * col_turned, axis=0, keepdims=True)
    right_ref[...] = right
    half_ref[...] = right_half
    scaled = points_ref[...] * scale
    left_half = 0.5 * jnp.sum(scaled * scaled, axis=1, keepdims=True)
    tile = kern(pack_left(scaled), left_half, right, right_half)
    tile_ref[...] = tile

    @pl.when(own)
    def _():
        square = tile_ref[pl.ds(start, count), :]
        ids = (count, count)
        on_diagonal = lax.broadcasted_iota(jnp.int32, ids, 0) == lax.broadcasted_iota(jnp.int32, ids, 1)
        noise = noise_ref[pl.ds(part, 1), :]
        tile_ref[pl.ds(start, count), :] = square + jnp.where(on_diagonal, noise, 0.0)


def update_kernel(
    own_ref, own_next_ref, other_ref, other_next_ref, scale_ref, high_ref, low_ref, turned_high_ref,
    turned_low_ref, pick_ref, right_ref, half_ref, points_ref, tile_ref, out_ref,
    chosen_ref, chosen_half_ref, cols_high_ref, cols_low_ref,
):
    panel = high_ref.shape[0]
    mid = panel // 2
    scale = scale_ref[...]

    @pl.when(pl.program_id(0) == 0)
    def _():
        block = jnp.concatenate(
            [own_ref[...], own_next_ref[...], other_ref[...], other_next_ref[...]], axis=0
        ) * scale
        features = block.shape[1]
        parts = product(pick_ref[...], jnp.concatenate(thirds_of(block), axis=1))
        chosen = (parts[:, :features] + parts[:, features : 2 * features]) + parts[:, 2 * features :]
        turned = jnp.transpose(chosen)
        chosen_ref[...] = pack_right(turned)
        chosen_half_ref[...] = 0.5 * jnp.sum(turned * turned, axis=0, keepdims=True)
        left_half = 0.5 * jnp.sum(chosen * chosen, axis=1, keepdims=True)
        cols_kern = kern(pack_left(chosen), left_half, right_ref[...], half_ref[...])
        kern_high, kern_low = halves_of(cols_kern)
        high, low = high_ref[...], low_ref[...]
        upper = product_of_halves(
            (high[:mid, :mid], low[:mid, :mid]), (kern_high[:mid], kern_low[:mid])
        )
        lower = product_of_halves((high[mid:], low[mid:]), (kern_high, kern_low))
        cols_high_ref[:mid, :], cols_low_ref[:mid, :] = halves_of(upper)
        cols_high_ref[mid:, :], cols_low_ref[mid:, :] = halves_of(lower)

    scaled = points_ref[...] * scale
    left_half = 0.5 * jnp.sum(scaled * scaled, axis=1, keepdims=True)
    rows_kern = kern(pack_left(scaled), left_half, chosen_ref[...], chosen_half_ref[...])
    kern_high, kern_low = halves_of(rows_kern)
    turned_high, turned_low = turned_high_ref[...], turned_low_ref[...]
    first = product_of_halves(
        (kern_high[:, :mid], kern_low[:, :mid]), (turned_high[:mid, :mid], turned_low[:mid, :mid])
    )
    second = product_of_halves((kern_high, kern_low), (turned_high[:, mid:], turned_low[:, mid:]))
    rows_panel = jnp.concatenate([first, second], axis=1)
    update = product_of_halves(halves_of(rows_panel), (cols_high_ref[...], cols_low_ref[...]))
    out_ref[...] = tile_ref[...] - update


def shape(dims, kind=f32):
    return jax.ShapeDtypeStruct(dims, kind)


def compute_params(flops, moved):
    return dict(
        compiler_params=pltpu.CompilerParams(vmem_limit_bytes=vmem_bytes),
        cost_estimate=pl.CostEstimate(flops=flops, bytes_accessed=moved, transcendentals=0),
    )


def source_places(rows):
    load = {}
    places = [[-1] * rows for _ in range(rows)]
    taken = [set() for _ in range(rows)]
    flows = sorted(
        ((g, r) for g in range(rows) for r in range(rows) if g != r),
        key=lambda flow: (-abs(flow[0] - flow[1]), flow),
    )
    for g, r in flows:
        step = 1 if r > g else -1
        links = [(z, step) for z in range(g, r, step)]

        def cost(place):
            loads = [load.get((place, link), 0) for link in links]
            return (max(loads), sum(loads), bin(place ^ g).count("1"), place)

        place = min((p for p in range(rows) if p not in taken[g]), key=cost)
        places[g][r] = place
        taken[g].add(place)
        for link in links:
            load[place, link] = load.get((place, link), 0) + 1
    return places


def column_pairs(rows, cols):
    halves = cols // rows
    places = source_places(rows)
    return [
        (g * cols + places[g][r] * halves + h, r * cols + g * halves + h)
        for g in range(rows)
        for r in range(rows)
        if r != g
        for h in range(halves)
    ]


def swap(value, bit, cols):
    return lax.ppermute(value, "col", [(i, i ^ bit) for i in range(cols)])


def gather_panel(panel_pool, panel_block, cols):
    col_place = lax.axis_index("col")
    half_rows = panel_pool.shape[0] // 2
    core = col_place % 2
    others = lax.dynamic_slice_in_dim(panel_pool, (1 - core) * half_rows, half_rows, 0)
    mine = lax.dynamic_slice_in_dim(panel_pool, core * half_rows, half_rows, 0)
    got, mine = lax.optimization_barrier((swap(others, 1, cols), mine))
    held = jnp.where(panel_block % 2 == core, mine, got)
    parts = [held[: half_rows // 2], held[half_rows // 2 :]]
    bits = [2**k for k in range(1, cols.bit_length() - 1)]
    turn = len(bits) // 2
    orders = [bits, bits[turn:] + bits[:turn]]
    for step in range(len(bits)):
        for path in range(2):
            bit = orders[path][step]
            got = swap(parts[path], bit, cols)
            parts[path] = jnp.where((panel_block ^ col_place) & bit == 0, parts[path], got)
    return parts + [swap(part, 1, cols) for part in parts]


def on_device(points, panel_pool, order, panel_index, inv_factor, ard_weights, noise):
    row_count, features = points.shape
    panel = inv_factor.shape[0]
    rows = lax.axis_size("row")
    cols = lax.axis_size("col")
    col_count = row_count * rows // cols
    halves = cols // rows
    col_place = lax.axis_index("col")

    pieces = gather_panel(panel_pool, panel_index[0], cols)
    own_half = lax.dynamic_slice_in_dim(points, col_place % halves * col_count, col_count, 0)
    sent = lax.ppermute(own_half, ("row", "col"), column_pairs(rows, cols))
    scale = jnp.sqrt(ard_weights * log2_e)[None, :]

    square = shape((panel, panel), bf16)
    factor_parts = pl.pallas_call(
        factor_kernel, out_shape=[square] * 5, **compute_params(10**8, 4 * 10**6)
    )(inv_factor, order[None, :])

    tile, right, right_half = pl.pallas_call(
        functools.partial(tile_kernel, rows, cols),
        out_shape=[
            shape((row_count, col_count)),
            shape((6 * features, col_count), bf16),
            shape((1, col_count)),
        ],
        **compute_params(12 * row_count * col_count * features, 4 * 10**6),
    )(points, sent, scale, noise.reshape(halves, col_count))

    step_rows = 256
    steps = row_count // step_rows
    quarter = panel_pool.shape[0] // 4

    def whole(*dims):
        return pl.BlockSpec(dims, lambda i: (0,) * len(dims))

    def row_block(width):
        return pl.BlockSpec((step_rows, width), lambda i: (i, 0))

    return pl.pallas_call(
        update_kernel,
        grid=(steps,),
        in_specs=[whole(quarter, features)] * 4
        + [whole(1, features)]
        + [whole(panel, panel)] * 5
        + [whole(6 * features, col_count), whole(1, col_count), row_block(features), row_block(col_count)],
        out_specs=row_block(col_count),
        out_shape=shape((row_count, col_count)),
        scratch_shapes=[
            pltpu.VMEM((6 * features, panel), bf16),
            pltpu.VMEM((1, panel), f32),
            pltpu.VMEM((panel, col_count), bf16),
            pltpu.VMEM((panel, col_count), bf16),
        ],
        **compute_params(4 * 10**9, 8 * 10**6),
    )(*pieces, scale, *factor_parts, right, right_half, points, tile)


def solution(mesh):
    in_specs = (P("row", None), P("col", None), P(), P(), P(), P(), P("row"))
    out_specs = P("row", "col")
    return jax.shard_map(
        on_device, mesh=mesh, in_specs=in_specs, out_specs=out_specs, check_vma=False
    )
```

```python
import functools

import jax
import jax.numpy as jnp
from jax import lax
from jax.experimental import pallas as pl
from jax.experimental.pallas import tpu as pltpu
from jax.sharding import PartitionSpec as P

log2_e = 1.4426950408889634
vmem_bytes = 32 * 1024 * 1024
f32, bf16 = jnp.float32, jnp.bfloat16


def halves_of(value):
    high = value.astype(bf16)
    low = (value - high.astype(f32)).astype(bf16)
    return high, low


def thirds_of(value):
    high = value.astype(bf16)
    rest = value - high.astype(f32)
    middle = rest.astype(bf16)
    low = (rest - middle.astype(f32)).astype(bf16)
    return high, middle, low


def pack_left(value):
    high, middle, low = thirds_of(value)
    return jnp.concatenate([high, middle, high, middle, high, low], axis=1)


def pack_right(value):
    high, middle, low = thirds_of(value)
    return jnp.concatenate([high, middle, middle, high, low, high], axis=0)


def product(left, right):
    return lax.dot_general(left, right, (((1,), (0,)), ((), ())), preferred_element_type=f32)


def product_of_halves(left, right):
    (left_high, left_low), (right_high, right_low) = left, right
    return (
        product(left_high, right_low) + product(left_low, right_high)
    ) + product(left_high, right_high)


def kern(left, left_half, right, right_half):
    return jnp.exp2((product(left, right) - left_half) - right_half + 1.0)


def factor_kernel(factor_ref, order_ref, high_ref, low_ref, turned_high_ref, turned_low_ref, pick_ref):
    factor = factor_ref[...]
    high_ref[...], low_ref[...] = halves_of(factor)
    turned_high_ref[...], turned_low_ref[...] = halves_of(jnp.transpose(factor))
    panel = factor.shape[0]
    place = lax.broadcasted_iota(jnp.int32, (panel, panel), 0)
    hit = jnp.where(place == order_ref[...], 1.0, 0.0).astype(f32)
    pick_ref[...] = jnp.transpose(hit).astype(bf16)


def tile_kernel(rows, cols, points_ref, sent_ref, scale_ref, noise_ref, tile_ref, right_ref, half_ref):
    row_place, col_place = lax.axis_index("row"), lax.axis_index("col")
    halves = cols // rows
    count = sent_ref.shape[0]
    part = col_place % halves
    start = pl.multiple_of(part * count, count)
    own = row_place == col_place // halves
    scale = scale_ref[...]
    col_points = jnp.where(own, points_ref[pl.ds(start, count), :], sent_ref[...])
    col_turned = jnp.transpose(col_points * scale)
    right = pack_right(col_turned)
    right_half = 0.5 * jnp.sum(col_turned * col_turned, axis=0, keepdims=True)
    right_ref[...] = right
    half_ref[...] = right_half
    scaled = points_ref[...] * scale
    left_half = 0.5 * jnp.sum(scaled * scaled, axis=1, keepdims=True)
    tile = kern(pack_left(scaled), left_half, right, right_half)
    tile_ref[...] = tile

    @pl.when(own)
    def _():
        square = tile_ref[pl.ds(start, count), :]
        ids = (count, count)
        on_diagonal = lax.broadcasted_iota(jnp.int32, ids, 0) == lax.broadcasted_iota(jnp.int32, ids, 1)
        noise = noise_ref[pl.ds(part, 1), :]
        tile_ref[pl.ds(start, count), :] = square + jnp.where(on_diagonal, noise, 0.0)


def update_kernel(
    block_ref, scale_ref, high_ref, low_ref, turned_high_ref,
    turned_low_ref, pick_ref, right_ref, half_ref, points_ref, tile_ref, out_ref,
    chosen_ref, chosen_half_ref, cols_high_ref, cols_low_ref,
):
    panel = high_ref.shape[0]
    mid = panel // 2
    scale = scale_ref[...]

    @pl.when(pl.program_id(0) == 0)
    def _():
        block = block_ref[...] * scale
        features = block.shape[1]
        parts = product(pick_ref[...], jnp.concatenate(thirds_of(block), axis=1))
        chosen = (parts[:, :features] + parts[:, features : 2 * features]) + parts[:, 2 * features :]
        turned = jnp.transpose(chosen)
        chosen_ref[...] = pack_right(turned)
        chosen_half_ref[...] = 0.5 * jnp.sum(turned * turned, axis=0, keepdims=True)
        left_half = 0.5 * jnp.sum(chosen * chosen, axis=1, keepdims=True)
        cols_kern = kern(pack_left(chosen), left_half, right_ref[...], half_ref[...])
        kern_high, kern_low = halves_of(cols_kern)
        high, low = high_ref[...], low_ref[...]
        upper = product_of_halves(
            (high[:mid, :mid], low[:mid, :mid]), (kern_high[:mid], kern_low[:mid])
        )
        lower = product_of_halves((high[mid:], low[mid:]), (kern_high, kern_low))
        cols_high_ref[:mid, :], cols_low_ref[:mid, :] = halves_of(upper)
        cols_high_ref[mid:, :], cols_low_ref[mid:, :] = halves_of(lower)

    scaled = points_ref[...] * scale
    left_half = 0.5 * jnp.sum(scaled * scaled, axis=1, keepdims=True)
    rows_kern = kern(pack_left(scaled), left_half, chosen_ref[...], chosen_half_ref[...])
    kern_high, kern_low = halves_of(rows_kern)
    turned_high, turned_low = turned_high_ref[...], turned_low_ref[...]
    first = product_of_halves(
        (kern_high[:, :mid], kern_low[:, :mid]), (turned_high[:mid, :mid], turned_low[:mid, :mid])
    )
    second = product_of_halves((kern_high, kern_low), (turned_high[:, mid:], turned_low[:, mid:]))
    rows_panel = jnp.concatenate([first, second], axis=1)
    update = product_of_halves(halves_of(rows_panel), (cols_high_ref[...], cols_low_ref[...]))
    out_ref[...] = tile_ref[...] - update


def shape(dims, kind=f32):
    return jax.ShapeDtypeStruct(dims, kind)


def compute_params(flops, moved):
    return dict(
        compiler_params=pltpu.CompilerParams(vmem_limit_bytes=vmem_bytes),
        cost_estimate=pl.CostEstimate(flops=flops, bytes_accessed=moved, transcendentals=0),
    )


def source_places(rows):
    load = {}
    places = [[-1] * rows for _ in range(rows)]
    taken = [set() for _ in range(rows)]
    flows = sorted(
        ((g, r) for g in range(rows) for r in range(rows) if g != r),
        key=lambda flow: (-abs(flow[0] - flow[1]), flow),
    )
    for g, r in flows:
        step = 1 if r > g else -1
        links = [(z, step) for z in range(g, r, step)]

        def cost(place):
            loads = [load.get((place, link), 0) for link in links]
            return (max(loads), sum(loads), bin(place ^ g).count("1"), place)

        place = min((p for p in range(rows) if p not in taken[g]), key=cost)
        places[g][r] = place
        taken[g].add(place)
        for link in links:
            load[place, link] = load.get((place, link), 0) + 1
    return places


def column_pairs(rows, cols):
    halves = cols // rows
    places = source_places(rows)
    return [
        (g * cols + places[g][r] * halves + h, r * cols + g * halves + h)
        for g in range(rows)
        for r in range(rows)
        if r != g
        for h in range(halves)
    ]


def gather_panel(panel_pool, panel_block, cols):
    rows, features = panel_pool.shape
    shares = lax.all_to_all(panel_pool.reshape(cols, rows // cols, features), "col", 0, 0)
    share = lax.dynamic_index_in_dim(shares, panel_block, 0, keepdims=True)
    whole = lax.all_to_all(jnp.broadcast_to(share, shares.shape), "col", 0, 0)
    return whole.reshape(rows, features)


def on_device(points, panel_pool, order, panel_index, inv_factor, ard_weights, noise):
    row_count, features = points.shape
    panel = inv_factor.shape[0]
    rows = lax.axis_size("row")
    cols = lax.axis_size("col")
    col_count = row_count * rows // cols
    halves = cols // rows
    col_place = lax.axis_index("col")

    block = gather_panel(panel_pool, panel_index[0], cols)
    own_half = lax.dynamic_slice_in_dim(points, col_place % halves * col_count, col_count, 0)
    sent = lax.ppermute(own_half, ("row", "col"), column_pairs(rows, cols))
    scale = jnp.sqrt(ard_weights * log2_e)[None, :]

    square = shape((panel, panel), bf16)
    factor_parts = pl.pallas_call(
        factor_kernel, out_shape=[square] * 5, **compute_params(10**8, 4 * 10**6)
    )(inv_factor, order[None, :])

    tile, right, right_half = pl.pallas_call(
        functools.partial(tile_kernel, rows, cols),
        out_shape=[
            shape((row_count, col_count)),
            shape((6 * features, col_count), bf16),
            shape((1, col_count)),
        ],
        **compute_params(12 * row_count * col_count * features, 4 * 10**6),
    )(points, sent, scale, noise.reshape(halves, col_count))

    step_rows = 256
    steps = row_count // step_rows

    def whole(*dims):
        return pl.BlockSpec(dims, lambda i: (0,) * len(dims))

    def row_block(width):
        return pl.BlockSpec((step_rows, width), lambda i: (i, 0))

    return pl.pallas_call(
        update_kernel,
        grid=(steps,),
        in_specs=[whole(panel, features), whole(1, features)]
        + [whole(panel, panel)] * 5
        + [whole(6 * features, col_count), whole(1, col_count), row_block(features), row_block(col_count)],
        out_specs=row_block(col_count),
        out_shape=shape((row_count, col_count)),
        scratch_shapes=[
            pltpu.VMEM((6 * features, panel), bf16),
            pltpu.VMEM((1, panel), f32),
            pltpu.VMEM((panel, col_count), bf16),
            pltpu.VMEM((panel, col_count), bf16),
        ],
        **compute_params(4 * 10**9, 8 * 10**6),
    )(block, scale, *factor_parts, right, right_half, points, tile)


def solution(mesh):
    in_specs = (P("row", None), P("col", None), P(), P(), P(), P(), P("row"))
    out_specs = P("row", "col")
    return jax.shard_map(
        on_device, mesh=mesh, in_specs=in_specs, out_specs=out_specs, check_vma=False
    )
```

```python
import functools

import jax
import jax.numpy as jnp
from jax import lax
from jax.experimental import pallas as pl
from jax.experimental.pallas import tpu as pltpu
from jax.sharding import PartitionSpec as P

log2_e = 1.4426950408889634
vmem_bytes = 32 * 1024 * 1024
f32, bf16 = jnp.float32, jnp.bfloat16


def halves_of(value):
    high = value.astype(bf16)
    low = (value - high.astype(f32)).astype(bf16)
    return high, low


def thirds_of(value):
    high = value.astype(bf16)
    rest = value - high.astype(f32)
    middle = rest.astype(bf16)
    low = (rest - middle.astype(f32)).astype(bf16)
    return high, middle, low


def pack_left(value):
    high, middle, low = thirds_of(value)
    return jnp.concatenate([high, middle, high, middle, high, low], axis=1)


def pack_right(value):
    high, middle, low = thirds_of(value)
    return jnp.concatenate([high, middle, middle, high, low, high], axis=0)


def product(left, right):
    return lax.dot_general(left, right, (((1,), (0,)), ((), ())), preferred_element_type=f32)


def join_left(high, low):
    return jnp.concatenate([high, high, low], axis=1)


def join_right(high, low):
    return jnp.concatenate([high, low, high], axis=0)


def kern(left, left_half, right, right_half):
    return jnp.exp2((product(left, right) - left_half) - right_half + 1.0)


def factor_kernel(factor_ref, order_ref, high_ref, low_ref, turned_high_ref, turned_low_ref, pick_ref):
    factor = factor_ref[...]
    high_ref[...], low_ref[...] = halves_of(factor)
    turned_high_ref[...], turned_low_ref[...] = halves_of(jnp.transpose(factor))
    panel = factor.shape[0]
    core = lax.axis_index("col") % 2
    place = lax.broadcasted_iota(jnp.int32, (panel, panel), 0) + core * (panel // 2)
    place = jnp.where(place >= panel, place - panel, place)
    hit = jnp.where(place == order_ref[...], 1.0, 0.0).astype(f32)
    pick_ref[...] = jnp.transpose(hit).astype(bf16)


def tile_kernel(
    rows, cols, points_ref, sent_ref, scale_ref, noise_ref, tile_ref, left_ref, left_half_ref, right_ref, half_ref
):
    row_place, col_place = lax.axis_index("row"), lax.axis_index("col")
    halves = cols // rows
    count = sent_ref.shape[0]
    part = col_place % halves
    start = pl.multiple_of(part * count, count)
    own = row_place == col_place // halves
    scale = scale_ref[...]
    col_points = jnp.where(own, points_ref[pl.ds(start, count), :], sent_ref[...])
    col_turned = jnp.transpose(col_points * scale)
    right = pack_right(col_turned)
    right_half = 0.5 * jnp.sum(col_turned * col_turned, axis=0, keepdims=True)
    right_ref[...] = right
    half_ref[...] = right_half
    scaled = points_ref[...] * scale
    left_half = 0.5 * jnp.sum(scaled * scaled, axis=1, keepdims=True)
    left = pack_left(scaled)
    left_ref[...] = left
    left_half_ref[...] = left_half
    tile_ref[...] = kern(left, left_half, right, right_half)

    @pl.when(own)
    def _():
        square = tile_ref[pl.ds(start, count), :]
        ids = (count, count)
        on_diagonal = lax.broadcasted_iota(jnp.int32, ids, 0) == lax.broadcasted_iota(jnp.int32, ids, 1)
        noise = noise_ref[pl.ds(part, 1), :]
        tile_ref[pl.ds(start, count), :] = square + jnp.where(on_diagonal, noise, 0.0)


def update_kernel(
    own_ref, own_next_ref, other_ref, other_next_ref, scale_ref, high_ref, low_ref, turned_high_ref,
    turned_low_ref, pick_ref, right_ref, half_ref, left_ref, left_half_ref, tile_ref, out_ref,
    block_ref, sems,
):
    panel = high_ref.shape[0]
    mid = panel // 2
    block = jnp.concatenate(
        [own_ref[...], own_next_ref[...], other_ref[...], other_next_ref[...]], axis=0
    ) * scale_ref[...]
    features = block.shape[1]
    parts = product(pick_ref[...], jnp.concatenate(thirds_of(block), axis=1))
    chosen = (parts[:, :features] + parts[:, features : 2 * features]) + parts[:, 2 * features :]
    turned = jnp.transpose(chosen)
    chosen_right = pack_right(turned)
    chosen_half = 0.5 * jnp.sum(turned * turned, axis=0, keepdims=True)
    chosen_left_half = 0.5 * jnp.sum(chosen * chosen, axis=1, keepdims=True)
    cols_kern = kern(pack_left(chosen), chosen_left_half, right_ref[...], half_ref[...])
    kern_high, kern_low = halves_of(cols_kern)
    upper = product(
        join_left(high_ref[:mid, :mid], low_ref[:mid, :mid]), join_right(kern_high[:mid], kern_low[:mid])
    )
    lower = product(join_left(high_ref[mid:, :], low_ref[mid:, :]), join_right(kern_high, kern_low))
    cols_panel = join_right(*halves_of(jnp.concatenate([upper, lower], axis=0)))
    first_right = join_right(turned_high_ref[:mid, :mid], turned_low_ref[:mid, :mid])
    second_right = join_right(turned_high_ref[:, mid:], turned_low_ref[:, mid:])

    chunks, chunk = block_ref.shape[:2]
    copies = []
    for number in range(chunks):
        rows = slice(number * chunk, (number + 1) * chunk)
        rows_kern = kern(left_ref[rows, :], left_half_ref[rows, :], chosen_right, chosen_half)
        kern_high, kern_low = halves_of(rows_kern)
        first = product(join_left(kern_high[:, :mid], kern_low[:, :mid]), first_right)
        second = product(join_left(kern_high, kern_low), second_right)
        rows_panel = join_left(*halves_of(jnp.concatenate([first, second], axis=1)))
        block_ref[number] = tile_ref[rows, :] - product(rows_panel, cols_panel)
        copy = pltpu.make_async_copy(block_ref.at[number], out_ref.at[pl.ds(number * chunk, chunk)], sems.at[number])
        copy.start()
        copies.append(copy)
    for copy in copies:
        copy.wait()


def shape(dims, kind=f32):
    return jax.ShapeDtypeStruct(dims, kind)


def compute_params(flops, moved):
    return dict(
        compiler_params=pltpu.CompilerParams(vmem_limit_bytes=vmem_bytes),
        cost_estimate=pl.CostEstimate(flops=flops, bytes_accessed=moved, transcendentals=0),
    )


def source_places(rows):
    load = {}
    places = [[-1] * rows for _ in range(rows)]
    taken = [set() for _ in range(rows)]
    flows = sorted(
        ((g, r) for g in range(rows) for r in range(rows) if g != r),
        key=lambda flow: (-abs(flow[0] - flow[1]), flow),
    )
    for g, r in flows:
        step = 1 if r > g else -1
        links = [(z, step) for z in range(g, r, step)]

        def cost(place):
            loads = [load.get((place, link), 0) for link in links]
            return (max(loads), sum(loads), bin(place ^ g).count("1"), place)

        place = min((p for p in range(rows) if p not in taken[g]), key=cost)
        places[g][r] = place
        taken[g].add(place)
        for link in links:
            load[place, link] = load.get((place, link), 0) + 1
    return places


def column_pairs(rows, cols):
    halves = cols // rows
    places = source_places(rows)
    return [
        (g * cols + places[g][r] * halves + h, r * cols + g * halves + h)
        for g in range(rows)
        for r in range(rows)
        if r != g
        for h in range(halves)
    ]


def swap(value, bit, cols):
    return lax.ppermute(value, "col", [(i, i ^ bit) for i in range(cols)])


def gather_panel(panel_pool, panel_block, cols):
    col_place = lax.axis_index("col")
    half_rows = panel_pool.shape[0] // 2
    core = col_place % 2
    others = lax.dynamic_slice_in_dim(panel_pool, (1 - core) * half_rows, half_rows, 0)
    mine = lax.dynamic_slice_in_dim(panel_pool, core * half_rows, half_rows, 0)
    got, mine = lax.optimization_barrier((swap(others, 1, cols), mine))
    held = jnp.where(panel_block % 2 == core, mine, got)
    parts = [held[: half_rows // 2], held[half_rows // 2 :]]
    bits = [2**k for k in range(1, cols.bit_length() - 1)]
    turn = len(bits) // 2
    orders = [bits, bits[turn:] + bits[:turn]]
    for step in range(len(bits)):
        for path in range(2):
            bit = orders[path][step]
            got = swap(parts[path], bit, cols)
            parts[path] = jnp.where((panel_block ^ col_place) & bit == 0, parts[path], got)
    return parts + [swap(part, 1, cols) for part in parts]


def on_device(points, panel_pool, order, panel_index, inv_factor, ard_weights, noise):
    row_count, features = points.shape
    panel = inv_factor.shape[0]
    rows = lax.axis_size("row")
    cols = lax.axis_size("col")
    col_count = row_count * rows // cols
    halves = cols // rows
    col_place = lax.axis_index("col")

    pieces = gather_panel(panel_pool, panel_index[0], cols)
    own_half = lax.dynamic_slice_in_dim(points, col_place % halves * col_count, col_count, 0)
    sent = lax.ppermute(own_half, ("row", "col"), column_pairs(rows, cols))
    scale = jnp.sqrt(ard_weights * log2_e)[None, :]

    square = shape((panel, panel), bf16)
    factor_parts = pl.pallas_call(
        factor_kernel, out_shape=[square] * 5, **compute_params(10**8, 4 * 10**6)
    )(inv_factor, order[None, :])

    tile, left, left_half, right, right_half = pl.pallas_call(
        functools.partial(tile_kernel, rows, cols),
        out_shape=[
            shape((row_count, col_count)),
            shape((row_count, 6 * features), bf16),
            shape((row_count, 1)),
            shape((6 * features, col_count), bf16),
            shape((1, col_count)),
        ],
        **compute_params(12 * row_count * col_count * features, 4 * 10**6),
    )(points, sent, scale, noise.reshape(halves, col_count))

    chunks = 4
    return pl.pallas_call(
        update_kernel,
        out_shape=shape((row_count, col_count)),
        out_specs=pl.BlockSpec(memory_space=pl.ANY),
        scratch_shapes=[
            pltpu.VMEM((chunks, row_count // chunks, col_count), f32),
            pltpu.SemaphoreType.DMA((chunks,)),
        ],
        **compute_params(4 * 10**9, 8 * 10**6),
    )(*pieces, scale, *factor_parts, right, right_half, left, left_half, tile)


def solution(mesh):
    in_specs = (P("row", None), P("col", None), P(), P(), P(), P(), P("row"))
    out_specs = P("row", "col")
    return jax.shard_map(
        on_device, mesh=mesh, in_specs=in_specs, out_specs=out_specs, check_vma=False
    )
```

```python
import collections
import functools
import math
import random

import jax
import jax.numpy as jnp
from jax import lax
from jax.experimental import pallas as pl
from jax.experimental.pallas import tpu as pltpu
from jax.sharding import PartitionSpec as P

log2_e = 1.4426950408889634
vmem_bytes = 32 * 1024 * 1024
f32, bf16 = jnp.float32, jnp.bfloat16


def halves_of(value):
    high = value.astype(bf16)
    low = (value - high.astype(f32)).astype(bf16)
    return high, low


def thirds_of(value):
    high = value.astype(bf16)
    rest = value - high.astype(f32)
    middle = rest.astype(bf16)
    low = (rest - middle.astype(f32)).astype(bf16)
    return high, middle, low


def pack_left(value):
    high, middle, low = thirds_of(value)
    return jnp.concatenate([high, middle, high, middle, high, low], axis=1)


def pack_right(value):
    high, middle, low = thirds_of(value)
    return jnp.concatenate([high, middle, middle, high, low, high], axis=0)


def product(left, right):
    return lax.dot_general(left, right, (((1,), (0,)), ((), ())), preferred_element_type=f32)


def join_left(high, low):
    return jnp.concatenate([high, high, low], axis=1)


def join_right(high, low):
    return jnp.concatenate([high, low, high], axis=0)


def kern(left, left_half, right, right_half):
    return jnp.exp2((product(left, right) - left_half) - right_half + 1.0)


def factor_kernel(factor_ref, order_ref, high_ref, low_ref, turned_high_ref, turned_low_ref, pick_ref):
    factor = factor_ref[...]
    high_ref[...], low_ref[...] = halves_of(factor)
    turned_high_ref[...], turned_low_ref[...] = halves_of(jnp.transpose(factor))
    panel = factor.shape[0]
    core = lax.axis_index("col") % 2
    place = lax.broadcasted_iota(jnp.int32, (panel, panel), 0) + core * (panel // 2)
    place = jnp.where(place >= panel, place - panel, place)
    hit = jnp.where(place == order_ref[...], 1.0, 0.0).astype(f32)
    pick_ref[...] = jnp.transpose(hit).astype(bf16)


def tile_kernel(
    rows, cols, points_ref, sent_ref, scale_ref, noise_ref, tile_ref, left_ref, left_half_ref, right_ref, half_ref
):
    row_place, col_place = lax.axis_index("row"), lax.axis_index("col")
    halves = cols // rows
    count = sent_ref.shape[0]
    part = col_place % halves
    start = pl.multiple_of(part * count, count)
    own = row_place == col_place // halves
    scale = scale_ref[...]
    col_turned = jnp.transpose(sent_ref[...] * scale)
    right = pack_right(col_turned)
    right_half = 0.5 * jnp.sum(col_turned * col_turned, axis=0, keepdims=True)
    right_ref[...] = right
    half_ref[...] = right_half
    scaled = points_ref[...] * scale
    left_half = 0.5 * jnp.sum(scaled * scaled, axis=1, keepdims=True)
    left = pack_left(scaled)
    left_ref[...] = left
    left_half_ref[...] = left_half
    tile_ref[...] = kern(left, left_half, right, right_half)

    @pl.when(own)
    def _():
        square = tile_ref[pl.ds(start, count), :]
        ids = (count, count)
        on_diagonal = lax.broadcasted_iota(jnp.int32, ids, 0) == lax.broadcasted_iota(jnp.int32, ids, 1)
        noise = noise_ref[pl.ds(part, 1), :]
        tile_ref[pl.ds(start, count), :] = square + jnp.where(on_diagonal, noise, 0.0)


def update_kernel(
    own_ref, own_next_ref, other_ref, other_next_ref, scale_ref, high_ref, low_ref, turned_high_ref,
    turned_low_ref, pick_ref, right_ref, half_ref, left_ref, left_half_ref, tile_ref, out_ref,
    block_ref, sems,
):
    panel = high_ref.shape[0]
    mid = panel // 2
    block = jnp.concatenate(
        [own_ref[...], own_next_ref[...], other_ref[...], other_next_ref[...]], axis=0
    ) * scale_ref[...]
    features = block.shape[1]
    parts = product(pick_ref[...], jnp.concatenate(thirds_of(block), axis=1))
    chosen = (parts[:, :features] + parts[:, features : 2 * features]) + parts[:, 2 * features :]
    turned = jnp.transpose(chosen)
    chosen_right = pack_right(turned)
    chosen_half = 0.5 * jnp.sum(turned * turned, axis=0, keepdims=True)
    chosen_left_half = 0.5 * jnp.sum(chosen * chosen, axis=1, keepdims=True)
    cols_kern = kern(pack_left(chosen), chosen_left_half, right_ref[...], half_ref[...])
    kern_high, kern_low = halves_of(cols_kern)
    upper = product(
        join_left(high_ref[:mid, :mid], low_ref[:mid, :mid]), join_right(kern_high[:mid], kern_low[:mid])
    )
    lower = product(join_left(high_ref[mid:, :], low_ref[mid:, :]), join_right(kern_high, kern_low))
    cols_panel = join_right(*halves_of(jnp.concatenate([upper, lower], axis=0)))
    first_right = join_right(turned_high_ref[:mid, :mid], turned_low_ref[:mid, :mid])
    second_right = join_right(turned_high_ref[:, mid:], turned_low_ref[:, mid:])

    chunks, chunk = block_ref.shape[:2]
    copies = []
    for number in range(chunks):
        rows = slice(number * chunk, (number + 1) * chunk)
        rows_kern = kern(left_ref[rows, :], left_half_ref[rows, :], chosen_right, chosen_half)
        kern_high, kern_low = halves_of(rows_kern)
        first = product(join_left(kern_high[:, :mid], kern_low[:, :mid]), first_right)
        second = product(join_left(kern_high, kern_low), second_right)
        rows_panel = join_left(*halves_of(jnp.concatenate([first, second], axis=1)))
        block_ref[number] = tile_ref[rows, :] - product(rows_panel, cols_panel)
        copy = pltpu.make_async_copy(block_ref.at[number], out_ref.at[pl.ds(number * chunk, chunk)], sems.at[number])
        copy.start()
        copies.append(copy)
    for copy in copies:
        copy.wait()


def shape(dims, kind=f32):
    return jax.ShapeDtypeStruct(dims, kind)


def compute_params(flops, moved):
    return dict(
        compiler_params=pltpu.CompilerParams(vmem_limit_bytes=vmem_bytes),
        cost_estimate=pl.CostEstimate(flops=flops, bytes_accessed=moved, transcendentals=0),
    )


def links_of(place, group, target_row, across):
    links = []
    step = 1 if target_row > group else -1
    links += [(0, place, z, step) for z in range(group, target_row, step)]
    (x, y), (end_x, end_y) = (place % across, place // across), (group % across, group // across)
    step = 1 if end_x > x else -1
    links += [(1, target_row, y, at, step) for at in range(x, end_x, step)]
    step = 1 if end_y > y else -1
    links += [(2, target_row, end_x, at, step) for at in range(y, end_y, step)]
    return links


def source_places(rows, halves):
    draw = random.Random(5)
    across = math.isqrt(rows)
    places = {}
    load = collections.Counter()

    def move(key, r, sign):
        change = 0
        for link in links_of(places[key][r], key[1], r, across):
            old = load[link]
            load[link] = old + sign
            change += (old + sign) ** 4 - old**4
        return change

    for h in range(halves):
        for g in range(rows):
            places[h, g] = draw.sample(range(rows), rows)
            for r in range(rows):
                move((h, g), r, 1)
    best, total, kept = 0, 0, {key: list(value) for key, value in places.items()}
    tries = 20000
    for number in range(tries):
        key = draw.randrange(halves), draw.randrange(rows)
        one, two = draw.sample(range(rows), 2)
        own = places[key]
        change = move(key, one, -1) + move(key, two, -1)
        own[one], own[two] = own[two], own[one]
        change += move(key, one, 1) + move(key, two, 1)
        heat = 30.0 * (1 - number / tries) + 0.01
        if change <= 0 or draw.random() < math.exp(-change / heat):
            total += change
            if total < best:
                best, kept = total, {key: list(value) for key, value in places.items()}
        else:
            move(key, one, -1), move(key, two, -1)
            own[one], own[two] = own[two], own[one]
            move(key, one, 1), move(key, two, 1)
    return kept


def column_pairs(rows, cols):
    halves = cols // rows
    places = source_places(rows, halves)
    return [
        (g * cols + places[h, g][r] * halves + h, r * cols + g * halves + h)
        for h in range(halves)
        for g in range(rows)
        for r in range(rows)
    ]


def swap(value, bit, cols):
    return lax.ppermute(value, "col", [(i, i ^ bit) for i in range(cols)])


def gather_panel(others, mine, panel_block, cols):
    col_place = lax.axis_index("col")
    half_rows = mine.shape[0]
    core = col_place % 2
    got, mine = lax.optimization_barrier((swap(others, 1, cols), mine))
    held = jnp.where(panel_block % 2 == core, mine, got)
    parts = [held[: half_rows // 2], held[half_rows // 2 :]]
    bits = [2**k for k in range(1, cols.bit_length() - 1)]
    turn = len(bits) // 2
    orders = [bits, bits[turn:] + bits[:turn]]
    for step in range(len(bits)):
        for path in range(2):
            bit = orders[path][step]
            got = swap(parts[path], bit, cols)
            parts[path] = jnp.where((panel_block ^ col_place) & bit == 0, parts[path], got)
    return parts + [swap(part, 1, cols) for part in parts]


def on_device(points, panel_pool, order, panel_index, inv_factor, ard_weights, noise):
    row_count, features = points.shape
    panel = inv_factor.shape[0]
    rows = lax.axis_size("row")
    cols = lax.axis_size("col")
    col_count = row_count * rows // cols
    halves = cols // rows
    half_rows = panel_pool.shape[0] // 2
    col_place = lax.axis_index("col")

    core = col_place % 2
    own_half = lax.dynamic_slice_in_dim(points, col_place % halves * col_count, col_count, 0)
    others = lax.dynamic_slice_in_dim(panel_pool, (1 - core) * half_rows, half_rows, 0)
    mine = lax.dynamic_slice_in_dim(panel_pool, core * half_rows, half_rows, 0)
    sent = lax.ppermute(own_half, ("row", "col"), column_pairs(rows, cols))
    pieces = gather_panel(others, mine, panel_index[0], cols)
    scale = jnp.sqrt(ard_weights * log2_e)[None, :]

    square = shape((panel, panel), bf16)
    factor_parts = pl.pallas_call(
        factor_kernel, out_shape=[square] * 5, **compute_params(10**8, 4 * 10**6)
    )(inv_factor, order[None, :])

    tile, left, left_half, right, right_half = pl.pallas_call(
        functools.partial(tile_kernel, rows, cols),
        out_shape=[
            shape((row_count, col_count)),
            shape((row_count, 6 * features), bf16),
            shape((row_count, 1)),
            shape((6 * features, col_count), bf16),
            shape((1, col_count)),
        ],
        **compute_params(12 * row_count * col_count * features, 4 * 10**6),
    )(points, sent, scale, noise.reshape(halves, col_count))

    chunks = 4
    return pl.pallas_call(
        update_kernel,
        out_shape=shape((row_count, col_count)),
        out_specs=pl.BlockSpec(memory_space=pl.ANY),
        scratch_shapes=[
            pltpu.VMEM((chunks, row_count // chunks, col_count), f32),
            pltpu.SemaphoreType.DMA((chunks,)),
        ],
        **compute_params(4 * 10**9, 8 * 10**6),
    )(*pieces, scale, *factor_parts, right, right_half, left, left_half, tile)


def solution(mesh):
    in_specs = (P("row", None), P("col", None), P(), P(), P(), P(), P("row"))
    out_specs = P("row", "col")
    return jax.shard_map(
        on_device, mesh=mesh, in_specs=in_specs, out_specs=out_specs, check_vma=False
    )
```

```python
import collections
import functools
import math
import random

import jax
import jax.numpy as jnp
from jax import lax
from jax.experimental import pallas as pl
from jax.experimental.pallas import tpu as pltpu
from jax.sharding import PartitionSpec as P

log2_e = 1.4426950408889634
vmem_bytes = 32 * 1024 * 1024
f32, bf16 = jnp.float32, jnp.bfloat16


def halves_of(value):
    high = value.astype(bf16)
    low = (value - high.astype(f32)).astype(bf16)
    return high, low


def thirds_of(value):
    high = value.astype(bf16)
    rest = value - high.astype(f32)
    middle = rest.astype(bf16)
    low = (rest - middle.astype(f32)).astype(bf16)
    return high, middle, low


def pack_left(value):
    high, middle, low = thirds_of(value)
    return jnp.concatenate([high, middle, high, middle, high, low], axis=1)


def pack_right(value):
    high, middle, low = thirds_of(value)
    return jnp.concatenate([high, middle, middle, high, low, high], axis=0)


def product(left, right):
    return lax.dot_general(left, right, (((1,), (0,)), ((), ())), preferred_element_type=f32)


def join_left(high, low):
    return jnp.concatenate([high, high, low], axis=1)


def join_right(high, low):
    return jnp.concatenate([high, low, high], axis=0)


def kern(left, left_half, right, right_half):
    return jnp.exp2((product(left, right) - left_half) - right_half + 1.0)


def factor_kernel(factor_ref, order_ref, high_ref, low_ref, turned_high_ref, turned_low_ref, pick_ref):
    factor = factor_ref[...]
    high_ref[...], low_ref[...] = halves_of(factor)
    turned_high_ref[...], turned_low_ref[...] = halves_of(jnp.transpose(factor))
    panel = factor.shape[0]
    core = lax.axis_index("col") % 2
    place = lax.broadcasted_iota(jnp.int32, (panel, panel), 0) + core * (panel // 2)
    place = jnp.where(place >= panel, place - panel, place)
    hit = jnp.where(place == order_ref[...], 1.0, 0.0).astype(f32)
    pick_ref[...] = jnp.transpose(hit).astype(bf16)


def tile_kernel(
    rows, cols, points_ref, sent_ref, scale_ref, noise_ref, tile_ref, left_ref, left_half_ref, right_ref, half_ref
):
    row_place, col_place = lax.axis_index("row"), lax.axis_index("col")
    halves = cols // rows
    count = sent_ref.shape[0]
    part = col_place % halves
    start = pl.multiple_of(part * count, count)
    own = row_place == col_place // halves
    scale = scale_ref[...]
    col_turned = jnp.transpose(sent_ref[...] * scale)
    right = pack_right(col_turned)
    right_half = 0.5 * jnp.sum(col_turned * col_turned, axis=0, keepdims=True)
    right_ref[...] = right
    half_ref[...] = right_half
    scaled = points_ref[...] * scale
    left_half = 0.5 * jnp.sum(scaled * scaled, axis=1, keepdims=True)
    left = pack_left(scaled)
    left_ref[...] = left
    left_half_ref[...] = left_half
    tile_ref[...] = kern(left, left_half, right, right_half)

    @pl.when(own)
    def _():
        square = tile_ref[pl.ds(start, count), :]
        ids = (count, count)
        on_diagonal = lax.broadcasted_iota(jnp.int32, ids, 0) == lax.broadcasted_iota(jnp.int32, ids, 1)
        noise = noise_ref[pl.ds(part, 1), :]
        tile_ref[pl.ds(start, count), :] = square + jnp.where(on_diagonal, noise, 0.0)


def update_kernel(
    own_ref, own_next_ref, other_ref, other_next_ref, scale_ref, high_ref, low_ref, turned_high_ref,
    turned_low_ref, pick_ref, right_ref, half_ref, left_ref, left_half_ref, tile_ref, out_ref,
    block_ref, sems,
):
    panel = high_ref.shape[0]
    mid = panel // 2
    block = jnp.concatenate(
        [own_ref[...], own_next_ref[...], other_ref[...], other_next_ref[...]], axis=0
    ) * scale_ref[...]
    features = block.shape[1]
    parts = product(pick_ref[...], jnp.concatenate(thirds_of(block), axis=1))
    chosen = (parts[:, :features] + parts[:, features : 2 * features]) + parts[:, 2 * features :]
    turned = jnp.transpose(chosen)
    chosen_right = pack_right(turned)
    chosen_half = 0.5 * jnp.sum(turned * turned, axis=0, keepdims=True)
    chosen_left_half = 0.5 * jnp.sum(chosen * chosen, axis=1, keepdims=True)
    cols_kern = kern(pack_left(chosen), chosen_left_half, right_ref[...], half_ref[...])
    kern_high, kern_low = halves_of(cols_kern)
    upper = product(
        join_left(high_ref[:mid, :mid], low_ref[:mid, :mid]), join_right(kern_high[:mid], kern_low[:mid])
    )
    lower = product(join_left(high_ref[mid:, :], low_ref[mid:, :]), join_right(kern_high, kern_low))
    cols_panel = join_right(*halves_of(jnp.concatenate([upper, lower], axis=0)))
    first_right = join_right(turned_high_ref[:mid, :mid], turned_low_ref[:mid, :mid])
    second_right = join_right(turned_high_ref[:, mid:], turned_low_ref[:, mid:])

    chunks, chunk = block_ref.shape[:2]
    copies = []
    for number in range(chunks):
        rows = slice(number * chunk, (number + 1) * chunk)
        rows_kern = kern(left_ref[rows, :], left_half_ref[rows, :], chosen_right, chosen_half)
        kern_high, kern_low = halves_of(rows_kern)
        first = product(join_left(kern_high[:, :mid], kern_low[:, :mid]), first_right)
        second = product(join_left(kern_high, kern_low), second_right)
        rows_panel = join_left(*halves_of(jnp.concatenate([first, second], axis=1)))
        block_ref[number] = tile_ref[rows, :] - product(rows_panel, cols_panel)
        copy = pltpu.make_async_copy(block_ref.at[number], out_ref.at[pl.ds(number * chunk, chunk)], sems.at[number])
        copy.start()
        copies.append(copy)
    for copy in copies:
        copy.wait()


def shape(dims, kind=f32):
    return jax.ShapeDtypeStruct(dims, kind)


def compute_params(flops, moved):
    return dict(
        compiler_params=pltpu.CompilerParams(vmem_limit_bytes=vmem_bytes),
        cost_estimate=pl.CostEstimate(flops=flops, bytes_accessed=moved, transcendentals=0),
    )


def links_of(place, group, target_row, across):
    links = []
    step = 1 if target_row > group else -1
    links += [(0, place, z, step) for z in range(group, target_row, step)]
    (x, y), (end_x, end_y) = (place % across, place // across), (group % across, group // across)
    step = 1 if end_x > x else -1
    links += [(1, target_row, y, at, step) for at in range(x, end_x, step)]
    step = 1 if end_y > y else -1
    links += [(2, target_row, end_x, at, step) for at in range(y, end_y, step)]
    return links


def source_places(rows, halves):
    draw = random.Random(5)
    across = math.isqrt(rows)
    places = {}
    load = collections.Counter()

    def move(key, r, sign):
        change = 0
        for link in links_of(places[key][r], key[1], r, across):
            old = load[link]
            load[link] = old + sign
            change += (old + sign) ** 4 - old**4
        return change

    for h in range(halves):
        for g in range(rows):
            places[h, g] = draw.sample(range(rows), rows)
            for r in range(rows):
                move((h, g), r, 1)
    best, total, kept = 0, 0, {key: list(value) for key, value in places.items()}
    tries = 20000
    for number in range(tries):
        key = draw.randrange(halves), draw.randrange(rows)
        one, two = draw.sample(range(rows), 2)
        own = places[key]
        change = move(key, one, -1) + move(key, two, -1)
        own[one], own[two] = own[two], own[one]
        change += move(key, one, 1) + move(key, two, 1)
        heat = 30.0 * (1 - number / tries) + 0.01
        if change <= 0 or draw.random() < math.exp(-change / heat):
            total += change
            if total < best:
                best, kept = total, {key: list(value) for key, value in places.items()}
        else:
            move(key, one, -1), move(key, two, -1)
            own[one], own[two] = own[two], own[one]
            move(key, one, 1), move(key, two, 1)
    return kept


def column_pairs(rows, cols):
    halves = cols // rows
    places = source_places(rows, halves)
    return [
        (g * cols + places[h, g][r] * halves + h, r * cols + g * halves + h)
        for h in range(halves)
        for g in range(rows)
        for r in range(rows)
    ]


def swap(value, bit, cols):
    return lax.ppermute(value, "col", [(i, i ^ bit) for i in range(cols)])


def gather_panel(others, mine, panel_block, cols):
    col_place = lax.axis_index("col")
    half_rows = mine.shape[0]
    core = col_place % 2
    got, mine = lax.optimization_barrier((swap(others, 1, cols), mine))
    held = jnp.where(panel_block % 2 == core, mine, got)
    parts = [held[: half_rows // 2], held[half_rows // 2 :]]
    bits = [2**k for k in range(1, cols.bit_length() - 1)]
    turn = len(bits) // 2
    orders = [bits, bits[turn:] + bits[:turn]]
    for step in range(len(bits)):
        for path in range(2):
            bit = orders[path][step]
            got = swap(parts[path], bit, cols)
            parts[path] = jnp.where((panel_block ^ col_place) & bit == 0, parts[path], got)
    return parts + [swap(part, 1, cols) for part in parts]


def on_device(points, panel_pool, order, panel_index, inv_factor, ard_weights, noise):
    row_count, features = points.shape
    panel = inv_factor.shape[0]
    rows = lax.axis_size("row")
    cols = lax.axis_size("col")
    col_count = row_count * rows // cols
    halves = cols // rows
    half_rows = panel_pool.shape[0] // 2
    col_place = lax.axis_index("col")

    core = col_place % 2
    own_half = lax.dynamic_slice_in_dim(points, col_place % halves * col_count, col_count, 0)
    others = lax.dynamic_slice_in_dim(panel_pool, (1 - core) * half_rows, half_rows, 0)
    mine = lax.dynamic_slice_in_dim(panel_pool, core * half_rows, half_rows, 0)
    sent = lax.ppermute(own_half, ("row", "col"), column_pairs(rows, cols))
    pieces = gather_panel(others, mine, panel_index[0], cols)
    scale = jnp.sqrt(ard_weights * log2_e)[None, :]

    square = shape((panel, panel), bf16)
    factor_parts = pl.pallas_call(
        factor_kernel, out_shape=[square] * 5, **compute_params(10**10, 4 * 10**6)
    )(inv_factor, order[None, :])

    tile, left, left_half, right, right_half = pl.pallas_call(
        functools.partial(tile_kernel, rows, cols),
        out_shape=[
            shape((row_count, col_count)),
            shape((row_count, 6 * features), bf16),
            shape((row_count, 1)),
            shape((6 * features, col_count), bf16),
            shape((1, col_count)),
        ],
        **compute_params(12 * row_count * col_count * features, 4 * 10**6),
    )(points, sent, scale, noise.reshape(halves, col_count))

    chunks = 4
    return pl.pallas_call(
        update_kernel,
        out_shape=shape((row_count, col_count)),
        out_specs=pl.BlockSpec(memory_space=pl.ANY),
        scratch_shapes=[
            pltpu.VMEM((chunks, row_count // chunks, col_count), f32),
            pltpu.SemaphoreType.DMA((chunks,)),
        ],
        **compute_params(4 * 10**9, 8 * 10**6),
    )(*pieces, scale, *factor_parts, right, right_half, left, left_half, tile)


def solution(mesh):
    in_specs = (P("row", None), P("col", None), P(), P(), P(), P(), P("row"))
    out_specs = P("row", "col")
    return jax.shard_map(
        on_device, mesh=mesh, in_specs=in_specs, out_specs=out_specs, check_vma=False
    )
```

```python
import collections
import functools
import math
import random

import jax
import jax.numpy as jnp
from jax import lax
from jax.experimental import pallas as pl
from jax.experimental.pallas import tpu as pltpu
from jax.sharding import PartitionSpec as P

log2_e = 1.4426950408889634
vmem_bytes = 32 * 1024 * 1024
f32, bf16 = jnp.float32, jnp.bfloat16


def halves_of(value):
    high = value.astype(bf16)
    low = (value - high.astype(f32)).astype(bf16)
    return high, low


def thirds_of(value):
    high = value.astype(bf16)
    rest = value - high.astype(f32)
    middle = rest.astype(bf16)
    low = (rest - middle.astype(f32)).astype(bf16)
    return high, middle, low


def pack_left(value):
    high, middle, low = thirds_of(value)
    return jnp.concatenate([high, middle, high, middle, high, low], axis=1)


def pack_right(value):
    high, middle, low = thirds_of(value)
    return jnp.concatenate([high, middle, middle, high, low, high], axis=0)


def product(left, right):
    return lax.dot_general(left, right, (((1,), (0,)), ((), ())), preferred_element_type=f32)


def join_left(high, low):
    return jnp.concatenate([high, high, low], axis=1)


def join_right(high, low):
    return jnp.concatenate([high, low, high], axis=0)


def kern(left, left_half, right, right_half):
    return jnp.exp2((product(left, right) - left_half) - right_half + 1.0)


def factor_kernel(factor_ref, order_ref, high_ref, low_ref, turned_high_ref, turned_low_ref, pick_ref):
    factor = factor_ref[...]
    high_ref[...], low_ref[...] = halves_of(factor)
    turned_high_ref[...], turned_low_ref[...] = halves_of(jnp.transpose(factor))
    panel = factor.shape[0]
    core = lax.axis_index("col") % 2
    place = lax.broadcasted_iota(jnp.int32, (panel, panel), 0) + core * (panel // 2)
    place = jnp.where(place >= panel, place - panel, place)
    hit = jnp.where(place == order_ref[...], 1.0, 0.0).astype(f32)
    pick_ref[...] = jnp.transpose(hit).astype(bf16)


def tile_kernel(
    rows, cols, points_ref, sent_ref, scale_ref, noise_ref, tile_ref, left_ref, left_half_ref, right_ref, half_ref
):
    row_place, col_place = lax.axis_index("row"), lax.axis_index("col")
    halves = cols // rows
    count = sent_ref.shape[0]
    part = col_place % halves
    start = pl.multiple_of(part * count, count)
    own = row_place == col_place // halves
    scale = scale_ref[...]
    col_turned = jnp.transpose(sent_ref[...] * scale)
    right = pack_right(col_turned)
    right_half = 0.5 * jnp.sum(col_turned * col_turned, axis=0, keepdims=True)
    right_ref[...] = right
    half_ref[...] = right_half
    scaled = points_ref[...] * scale
    left_half = 0.5 * jnp.sum(scaled * scaled, axis=1, keepdims=True)
    left = pack_left(scaled)
    left_ref[...] = left
    left_half_ref[...] = left_half
    tile_ref[...] = kern(left, left_half, right, right_half)

    @pl.when(own)
    def _():
        square = tile_ref[pl.ds(start, count), :]
        ids = (count, count)
        on_diagonal = lax.broadcasted_iota(jnp.int32, ids, 0) == lax.broadcasted_iota(jnp.int32, ids, 1)
        noise = noise_ref[pl.ds(part, 1), :]
        tile_ref[pl.ds(start, count), :] = square + jnp.where(on_diagonal, noise, 0.0)


def update_kernel(
    own_ref, other_ref, scale_ref, high_ref, low_ref, turned_high_ref,
    turned_low_ref, pick_ref, right_ref, half_ref, left_ref, left_half_ref, tile_ref, out_ref,
    block_ref, sems,
):
    panel = high_ref.shape[0]
    mid = panel // 2
    block = jnp.concatenate([own_ref[...], other_ref[...]], axis=0) * scale_ref[...]
    features = block.shape[1]
    parts = product(pick_ref[...], jnp.concatenate(thirds_of(block), axis=1))
    chosen = (parts[:, :features] + parts[:, features : 2 * features]) + parts[:, 2 * features :]
    turned = jnp.transpose(chosen)
    chosen_right = pack_right(turned)
    chosen_half = 0.5 * jnp.sum(turned * turned, axis=0, keepdims=True)
    chosen_left_half = 0.5 * jnp.sum(chosen * chosen, axis=1, keepdims=True)
    cols_kern = kern(pack_left(chosen), chosen_left_half, right_ref[...], half_ref[...])
    kern_high, kern_low = halves_of(cols_kern)
    upper = product(
        join_left(high_ref[:mid, :mid], low_ref[:mid, :mid]), join_right(kern_high[:mid], kern_low[:mid])
    )
    lower = product(join_left(high_ref[mid:, :], low_ref[mid:, :]), join_right(kern_high, kern_low))
    cols_panel = join_right(*halves_of(jnp.concatenate([upper, lower], axis=0)))
    first_right = join_right(turned_high_ref[:mid, :mid], turned_low_ref[:mid, :mid])
    second_right = join_right(turned_high_ref[:, mid:], turned_low_ref[:, mid:])

    chunks, chunk = block_ref.shape[:2]
    copies = []
    for number in range(chunks):
        rows = slice(number * chunk, (number + 1) * chunk)
        rows_kern = kern(left_ref[rows, :], left_half_ref[rows, :], chosen_right, chosen_half)
        kern_high, kern_low = halves_of(rows_kern)
        first = product(join_left(kern_high[:, :mid], kern_low[:, :mid]), first_right)
        second = product(join_left(kern_high, kern_low), second_right)
        rows_panel = join_left(*halves_of(jnp.concatenate([first, second], axis=1)))
        block_ref[number] = tile_ref[rows, :] - product(rows_panel, cols_panel)
        copy = pltpu.make_async_copy(block_ref.at[number], out_ref.at[pl.ds(number * chunk, chunk)], sems.at[number])
        copy.start()
        copies.append(copy)
    for copy in copies:
        copy.wait()


def shape(dims, kind=f32):
    return jax.ShapeDtypeStruct(dims, kind)


def compute_params(flops, moved):
    return dict(
        compiler_params=pltpu.CompilerParams(vmem_limit_bytes=vmem_bytes),
        cost_estimate=pl.CostEstimate(flops=flops, bytes_accessed=moved, transcendentals=0),
    )


def links_of(place, group, target_row, across):
    links = []
    step = 1 if target_row > group else -1
    links += [(0, place, z, step) for z in range(group, target_row, step)]
    (x, y), (end_x, end_y) = (place % across, place // across), (group % across, group // across)
    step = 1 if end_x > x else -1
    links += [(1, target_row, y, at, step) for at in range(x, end_x, step)]
    step = 1 if end_y > y else -1
    links += [(2, target_row, end_x, at, step) for at in range(y, end_y, step)]
    return links


def source_places(rows, halves):
    draw = random.Random(5)
    across = math.isqrt(rows)
    places = {}
    load = collections.Counter()

    def move(key, r, sign):
        change = 0
        for link in links_of(places[key][r], key[1], r, across):
            old = load[link]
            load[link] = old + sign
            change += (old + sign) ** 4 - old**4
        return change

    for h in range(halves):
        for g in range(rows):
            places[h, g] = draw.sample(range(rows), rows)
            if g == 0:
                places[h, g].remove(0)
                places[h, g].insert(0, 0)
            for r in range(rows):
                move((h, g), r, 1)
    best, total, kept = 0, 0, {key: list(value) for key, value in places.items()}
    tries = 20000
    for number in range(tries):
        key = draw.randrange(halves), draw.randrange(rows)
        one, two = draw.sample(range(key[1] == 0, rows), 2)
        own = places[key]
        change = move(key, one, -1) + move(key, two, -1)
        own[one], own[two] = own[two], own[one]
        change += move(key, one, 1) + move(key, two, 1)
        heat = 30.0 * (1 - number / tries) + 0.01
        if change <= 0 or draw.random() < math.exp(-change / heat):
            total += change
            if total < best:
                best, kept = total, {key: list(value) for key, value in places.items()}
        else:
            move(key, one, -1), move(key, two, -1)
            own[one], own[two] = own[two], own[one]
            move(key, one, 1), move(key, two, 1)
    return kept


def column_pairs(rows, cols):
    halves = cols // rows
    places = source_places(rows, halves)
    return [
        (g * cols + places[h, g][r] * halves + h, r * cols + g * halves + h)
        for h in range(halves)
        for g in range(rows)
        for r in range(rows)
    ]


def swap(value, bit, cols):
    return lax.ppermute(value, "col", [(i, i ^ bit) for i in range(cols)])


def gather_panel(others, mine, panel_block, cols):
    col_place = lax.axis_index("col")
    core = col_place % 2
    got, mine = lax.optimization_barrier((swap(others, 1, cols), mine))
    held = jnp.where(panel_block % 2 == core, mine, got)
    apart = panel_block ^ col_place
    low = 2
    while low < cols:
        high = min(4 * low, cols)
        away = apart & (high - low)
        received = [swap(held, bits, cols) for bits in range(low, high, low)]
        for bits, value in zip(range(low, high, low), received):
            held = jnp.where(away == bits, value, held)
        low = high
    return [held, swap(held, 1, cols)]


def on_device(points, panel_pool, order, panel_index, inv_factor, ard_weights, noise):
    row_count, features = points.shape
    panel = inv_factor.shape[0]
    rows = lax.axis_size("row")
    cols = lax.axis_size("col")
    col_count = row_count * rows // cols
    halves = cols // rows
    half_rows = panel_pool.shape[0] // 2
    col_place = lax.axis_index("col")

    core = col_place % 2
    own_half = lax.dynamic_slice_in_dim(points, col_place % halves * col_count, col_count, 0)
    others = lax.dynamic_slice_in_dim(panel_pool, (1 - core) * half_rows, half_rows, 0)
    mine = lax.dynamic_slice_in_dim(panel_pool, core * half_rows, half_rows, 0)
    sent = lax.ppermute(own_half, ("row", "col"), column_pairs(rows, cols))
    pieces = gather_panel(others, mine, panel_index[0], cols)
    scale = jnp.sqrt(ard_weights * log2_e)[None, :]

    square = shape((panel, panel), bf16)
    factor_parts = pl.pallas_call(
        factor_kernel, out_shape=[square] * 5, **compute_params(10**8, 4 * 10**6)
    )(inv_factor, order[None, :])

    tile, left, left_half, right, right_half = pl.pallas_call(
        functools.partial(tile_kernel, rows, cols),
        out_shape=[
            shape((row_count, col_count)),
            shape((row_count, 6 * features), bf16),
            shape((row_count, 1)),
            shape((6 * features, col_count), bf16),
            shape((1, col_count)),
        ],
        **compute_params(12 * row_count * col_count * features, 4 * 10**6),
    )(points, sent, scale, noise.reshape(halves, col_count))

    chunks = 2
    return pl.pallas_call(
        update_kernel,
        out_shape=shape((row_count, col_count)),
        out_specs=pl.BlockSpec(memory_space=pl.ANY),
        scratch_shapes=[
            pltpu.VMEM((chunks, row_count // chunks, col_count), f32),
            pltpu.SemaphoreType.DMA((chunks,)),
        ],
        **compute_params(4 * 10**9, 8 * 10**6),
    )(*pieces, scale, *factor_parts, right, right_half, left, left_half, tile)


def solution(mesh):
    in_specs = (P("row", None), P("col", None), P(), P(), P(), P(), P("row"))
    out_specs = P("row", "col")
    return jax.shard_map(
        on_device, mesh=mesh, in_specs=in_specs, out_specs=out_specs, check_vma=False
    )
```

```python
import collections
import functools
import math
import random

import jax
import jax.numpy as jnp
from jax import lax
from jax.experimental import pallas as pl
from jax.experimental.pallas import tpu as pltpu
from jax.sharding import PartitionSpec as P

log2_e = 1.4426950408889634
vmem_bytes = 32 * 1024 * 1024
f32, bf16 = jnp.float32, jnp.bfloat16


def halves_of(value):
    high = value.astype(bf16)
    low = (value - high.astype(f32)).astype(bf16)
    return high, low


def thirds_of(value):
    high = value.astype(bf16)
    rest = value - high.astype(f32)
    middle = rest.astype(bf16)
    low = (rest - middle.astype(f32)).astype(bf16)
    return high, middle, low


def pack_left(value):
    high, middle, low = thirds_of(value)
    return jnp.concatenate([high, middle, high, middle, high, low], axis=1)


def pack_right(value):
    high, middle, low = thirds_of(value)
    return jnp.concatenate([high, middle, middle, high, low, high], axis=0)


def product(left, right):
    return lax.dot_general(left, right, (((1,), (0,)), ((), ())), preferred_element_type=f32)


def join_left(high, low):
    return jnp.concatenate([high, high, low], axis=1)


def join_right(high, low):
    return jnp.concatenate([high, low, high], axis=0)


def kern(left, left_half, right, right_half):
    return jnp.exp2((product(left, right) - left_half) - right_half + 1.0)


def factor_kernel(factor_ref, order_ref, high_ref, low_ref, turned_high_ref, turned_low_ref, pick_ref):
    factor = factor_ref[...]
    high_ref[...], low_ref[...] = halves_of(factor)
    turned_high_ref[...], turned_low_ref[...] = halves_of(jnp.transpose(factor))
    panel = factor.shape[0]
    core = lax.axis_index("col") % 2
    place = lax.broadcasted_iota(jnp.int32, (panel, panel), 0) + core * (panel // 2)
    place = jnp.where(place >= panel, place - panel, place)
    hit = jnp.where(place == order_ref[...], 1.0, 0.0).astype(f32)
    pick_ref[...] = jnp.transpose(hit).astype(bf16)


def tile_kernel(
    rows, cols, points_ref, sent_ref, scale_ref, noise_ref, tile_ref, left_ref, left_half_ref, right_ref, half_ref
):
    row_place, col_place = lax.axis_index("row"), lax.axis_index("col")
    halves = cols // rows
    count = sent_ref.shape[0]
    part = col_place % halves
    start = pl.multiple_of(part * count, count)
    own = row_place == col_place // halves
    scale = scale_ref[...]
    col_turned = jnp.transpose(sent_ref[...] * scale)
    right = pack_right(col_turned)
    right_half = 0.5 * jnp.sum(col_turned * col_turned, axis=0, keepdims=True)
    right_ref[...] = right
    half_ref[...] = right_half
    scaled = points_ref[...] * scale
    left_half = 0.5 * jnp.sum(scaled * scaled, axis=1, keepdims=True)
    left = pack_left(scaled)
    left_ref[...] = left
    left_half_ref[...] = left_half
    tile_ref[...] = kern(left, left_half, right, right_half)

    @pl.when(own)
    def _():
        square = tile_ref[pl.ds(start, count), :]
        ids = (count, count)
        on_diagonal = lax.broadcasted_iota(jnp.int32, ids, 0) == lax.broadcasted_iota(jnp.int32, ids, 1)
        noise = noise_ref[pl.ds(part, 1), :]
        tile_ref[pl.ds(start, count), :] = square + jnp.where(on_diagonal, noise, 0.0)


def update_kernel(
    own_ref, other_ref, scale_ref, high_ref, low_ref, turned_high_ref,
    turned_low_ref, pick_ref, right_ref, half_ref, left_ref, left_half_ref, tile_ref, out_ref,
    block_ref, sems,
):
    panel = high_ref.shape[0]
    mid = panel // 2
    block = jnp.concatenate([own_ref[...], other_ref[...]], axis=0) * scale_ref[...]
    features = block.shape[1]
    parts = product(pick_ref[...], jnp.concatenate(thirds_of(block), axis=1))
    chosen = (parts[:, :features] + parts[:, features : 2 * features]) + parts[:, 2 * features :]
    turned = jnp.transpose(chosen)
    chosen_right = pack_right(turned)
    chosen_half = 0.5 * jnp.sum(turned * turned, axis=0, keepdims=True)
    chosen_left_half = 0.5 * jnp.sum(chosen * chosen, axis=1, keepdims=True)
    cols_kern = kern(pack_left(chosen), chosen_left_half, right_ref[...], half_ref[...])
    kern_high, kern_low = halves_of(cols_kern)
    upper = product(
        join_left(high_ref[:mid, :mid], low_ref[:mid, :mid]), join_right(kern_high[:mid], kern_low[:mid])
    )
    lower = product(join_left(high_ref[mid:, :], low_ref[mid:, :]), join_right(kern_high, kern_low))
    cols_panel = join_right(*halves_of(jnp.concatenate([upper, lower], axis=0)))
    first_right = join_right(turned_high_ref[:mid, :mid], turned_low_ref[:mid, :mid])
    second_right = join_right(turned_high_ref[:, mid:], turned_low_ref[:, mid:])

    chunks, chunk = block_ref.shape[:2]
    copies = []
    for number in range(chunks):
        rows = slice(number * chunk, (number + 1) * chunk)
        rows_kern = kern(left_ref[rows, :], left_half_ref[rows, :], chosen_right, chosen_half)
        kern_high, kern_low = halves_of(rows_kern)
        first = product(join_left(kern_high[:, :mid], kern_low[:, :mid]), first_right)
        second = product(join_left(kern_high, kern_low), second_right)
        rows_panel = join_left(*halves_of(jnp.concatenate([first, second], axis=1)))
        block_ref[number] = tile_ref[rows, :] - product(rows_panel, cols_panel)
        copy = pltpu.make_async_copy(block_ref.at[number], out_ref.at[pl.ds(number * chunk, chunk)], sems.at[number])
        copy.start()
        copies.append(copy)
    for copy in copies:
        copy.wait()


def shape(dims, kind=f32):
    return jax.ShapeDtypeStruct(dims, kind)


def compute_params(flops, moved):
    return dict(
        compiler_params=pltpu.CompilerParams(vmem_limit_bytes=vmem_bytes),
        cost_estimate=pl.CostEstimate(flops=flops, bytes_accessed=moved, transcendentals=0),
    )


def links_of(place, group, target_row, across):
    links = []
    step = 1 if target_row > group else -1
    links += [(0, place, z, step) for z in range(group, target_row, step)]
    (x, y), (end_x, end_y) = (place % across, place // across), (group % across, group // across)
    step = 1 if end_x > x else -1
    links += [(1, target_row, y, at, step) for at in range(x, end_x, step)]
    step = 1 if end_y > y else -1
    links += [(2, target_row, end_x, at, step) for at in range(y, end_y, step)]
    return links


def source_places(rows, halves):
    draw = random.Random(5)
    across = math.isqrt(rows)
    places = {}
    load = collections.Counter()

    def move(key, r, sign):
        change = 0
        for link in links_of(places[key][r], key[1], r, across):
            old = load[link]
            load[link] = old + sign
            change += (old + sign) ** 4 - old**4
        return change

    for h in range(halves):
        for g in range(rows):
            places[h, g] = draw.sample(range(rows), rows)
            if g == 0:
                places[h, g].remove(0)
                places[h, g].insert(0, 0)
            for r in range(rows):
                move((h, g), r, 1)
    best, total, kept = 0, 0, {key: list(value) for key, value in places.items()}
    tries = 20000
    for number in range(tries):
        key = draw.randrange(halves), draw.randrange(rows)
        one, two = draw.sample(range(key[1] == 0, rows), 2)
        own = places[key]
        change = move(key, one, -1) + move(key, two, -1)
        own[one], own[two] = own[two], own[one]
        change += move(key, one, 1) + move(key, two, 1)
        heat = 30.0 * (1 - number / tries) + 0.01
        if change <= 0 or draw.random() < math.exp(-change / heat):
            total += change
            if total < best:
                best, kept = total, {key: list(value) for key, value in places.items()}
        else:
            move(key, one, -1), move(key, two, -1)
            own[one], own[two] = own[two], own[one]
            move(key, one, 1), move(key, two, 1)
    return kept


def column_pairs(rows, cols):
    halves = cols // rows
    places = source_places(rows, halves)
    return [
        (g * cols + places[h, g][r] * halves + h, r * cols + g * halves + h)
        for h in range(halves)
        for g in range(rows)
        for r in range(rows)
    ]


def swap(value, bit, cols):
    return lax.ppermute(value, "col", [(i, i ^ bit) for i in range(cols)])


def gather_panel(others, mine, panel_block, cols):
    col_place = lax.axis_index("col")
    core = col_place % 2
    got, mine = lax.optimization_barrier((swap(others, 1, cols), mine))
    held = jnp.where(panel_block % 2 == core, mine, got)
    apart = panel_block ^ col_place
    low = 2
    while low < cols:
        high = min(4 * low, cols)
        away = apart & (high - low)
        received = [swap(held, bits, cols) for bits in range(low, high, low)]
        for bits, value in zip(range(low, high, low), received):
            held = jnp.where(away == bits, value, held)
        low = high
    return [held, swap(held, 1, cols)]


def on_device(points, panel_pool, order, panel_index, inv_factor, ard_weights, noise):
    row_count, features = points.shape
    panel = inv_factor.shape[0]
    rows = lax.axis_size("row")
    cols = lax.axis_size("col")
    col_count = row_count * rows // cols
    halves = cols // rows
    half_rows = panel_pool.shape[0] // 2
    col_place = lax.axis_index("col")

    core = col_place % 2
    own_half = lax.dynamic_slice_in_dim(points, col_place % halves * col_count, col_count, 0)
    others = lax.dynamic_slice_in_dim(panel_pool, (1 - core) * half_rows, half_rows, 0)
    mine = lax.dynamic_slice_in_dim(panel_pool, core * half_rows, half_rows, 0)
    sent = lax.ppermute(own_half, ("row", "col"), column_pairs(rows, cols))
    pieces = gather_panel(others, mine, panel_index[0], cols)
    scale = jnp.sqrt(ard_weights * log2_e)[None, :]

    square = shape((panel, panel), bf16)
    factor_parts = pl.pallas_call(
        factor_kernel, out_shape=[square] * 5, **compute_params(10**10, 4 * 10**6)
    )(inv_factor, order[None, :])

    tile, left, left_half, right, right_half = pl.pallas_call(
        functools.partial(tile_kernel, rows, cols),
        out_shape=[
            shape((row_count, col_count)),
            shape((row_count, 6 * features), bf16),
            shape((row_count, 1)),
            shape((6 * features, col_count), bf16),
            shape((1, col_count)),
        ],
        **compute_params(12 * row_count * col_count * features, 4 * 10**6),
    )(points, sent, scale, noise.reshape(halves, col_count))

    chunks = 2
    return pl.pallas_call(
        update_kernel,
        out_shape=shape((row_count, col_count)),
        out_specs=pl.BlockSpec(memory_space=pl.ANY),
        scratch_shapes=[
            pltpu.VMEM((chunks, row_count // chunks, col_count), f32),
            pltpu.SemaphoreType.DMA((chunks,)),
        ],
        **compute_params(4 * 10**9, 8 * 10**6),
    )(*pieces, scale, *factor_parts, right, right_half, left, left_half, tile)


def solution(mesh):
    in_specs = (P("row", None), P("col", None), P(), P(), P(), P(), P("row"))
    out_specs = P("row", "col")
    return jax.shard_map(
        on_device, mesh=mesh, in_specs=in_specs, out_specs=out_specs, check_vma=False
    )
```

```python
import collections
import functools
import math
import random

import jax
import jax.numpy as jnp
from jax import lax
from jax.experimental import pallas as pl
from jax.experimental.pallas import tpu as pltpu
from jax.sharding import PartitionSpec as P

log2_e = 1.4426950408889634
vmem_bytes = 32 * 1024 * 1024
f32, bf16 = jnp.float32, jnp.bfloat16


def halves_of(value):
    high = value.astype(bf16)
    low = (value - high.astype(f32)).astype(bf16)
    return high, low


def thirds_of(value):
    high = value.astype(bf16)
    rest = value - high.astype(f32)
    middle = rest.astype(bf16)
    low = (rest - middle.astype(f32)).astype(bf16)
    return high, middle, low


def pack_left(value):
    high, middle, low = thirds_of(value)
    return jnp.concatenate([high, middle, high, middle, high, low], axis=1)


def pack_right(value):
    high, middle, low = thirds_of(value)
    return jnp.concatenate([high, middle, middle, high, low, high], axis=0)


def product(left, right):
    return lax.dot_general(left, right, (((1,), (0,)), ((), ())), preferred_element_type=f32)


def join_left(high, low):
    return jnp.concatenate([high, high, low], axis=1)


def join_right(high, low):
    return jnp.concatenate([high, low, high], axis=0)


def kern(left, left_half, right, right_half):
    return jnp.exp2((product(left, right) - left_half) - right_half + 1.0)


def parts_kernel(
    factor_ref, order_ref, points_ref, scale_ref, high_ref, low_ref, turned_high_ref, turned_low_ref, pick_ref,
    left_ref, left_half_ref,
):
    factor = factor_ref[...]
    high_ref[...], low_ref[...] = halves_of(factor)
    turned_high_ref[...], turned_low_ref[...] = halves_of(jnp.transpose(factor))
    panel = factor.shape[0]
    core = lax.axis_index("col") % 2
    place = lax.broadcasted_iota(jnp.int32, (panel, panel), 0) + core * (panel // 2)
    place = jnp.where(place >= panel, place - panel, place)
    hit = jnp.where(place == order_ref[...], 1.0, 0.0).astype(f32)
    pick_ref[...] = jnp.transpose(hit).astype(bf16)
    scaled = points_ref[...] * scale_ref[...]
    left_ref[...] = pack_left(scaled)
    left_half_ref[...] = 0.5 * jnp.sum(scaled * scaled, axis=1, keepdims=True)


def rows_kernel(
    own_ref, other_ref, scale_ref, turned_high_ref, turned_low_ref, pick_ref, left_ref, left_half_ref,
    rows_high_ref, rows_low_ref, chosen_ref, chosen_half_ref,
):
    panel = pick_ref.shape[0]
    mid = panel // 2
    block = jnp.concatenate([own_ref[...], other_ref[...]], axis=0) * scale_ref[...]
    features = block.shape[1]
    parts = product(pick_ref[...], jnp.concatenate(thirds_of(block), axis=1))
    chosen = (parts[:, :features] + parts[:, features : 2 * features]) + parts[:, 2 * features :]
    turned = jnp.transpose(chosen)
    right = pack_right(turned)
    right_half = 0.5 * jnp.sum(turned * turned, axis=0, keepdims=True)
    chosen_ref[...] = pack_left(chosen)
    chosen_half_ref[...] = 0.5 * jnp.sum(chosen * chosen, axis=1, keepdims=True)
    first_right = join_right(turned_high_ref[:mid, :mid], turned_low_ref[:mid, :mid])
    second_right = join_right(turned_high_ref[:, mid:], turned_low_ref[:, mid:])
    count = left_ref.shape[0] // 2
    for number in range(2):
        rows = slice(number * count, (number + 1) * count)
        kern_high, kern_low = halves_of(kern(left_ref[rows, :], left_half_ref[rows, :], right, right_half))
        first = product(join_left(kern_high[:, :mid], kern_low[:, :mid]), first_right)
        second = product(join_left(kern_high, kern_low), second_right)
        rows_high_ref[rows, :mid], rows_low_ref[rows, :mid] = halves_of(first)
        rows_high_ref[rows, mid:], rows_low_ref[rows, mid:] = halves_of(second)


def update_kernel(
    rows, cols, sent_ref, scale_ref, noise_ref, high_ref, low_ref, left_ref, left_half_ref, rows_high_ref,
    rows_low_ref, chosen_ref, chosen_half_ref, out_ref, block_ref, sems,
):
    row_place, col_place = lax.axis_index("row"), lax.axis_index("col")
    halves = cols // rows
    count = sent_ref.shape[0]
    part = col_place % halves
    own = row_place == col_place // halves
    panel = high_ref.shape[0]
    mid = panel // 2

    turned = jnp.transpose(sent_ref[...] * scale_ref[...])
    right = pack_right(turned)
    right_half = 0.5 * jnp.sum(turned * turned, axis=0, keepdims=True)
    cols_kern = kern(chosen_ref[...], chosen_half_ref[...], right, right_half)
    kern_high, kern_low = halves_of(cols_kern)
    upper = product(
        join_left(high_ref[:mid, :mid], low_ref[:mid, :mid]), join_right(kern_high[:mid], kern_low[:mid])
    )
    lower = product(join_left(high_ref[mid:, :], low_ref[mid:, :]), join_right(kern_high, kern_low))
    cols_panel = join_right(*halves_of(jnp.concatenate([upper, lower], axis=0)))

    noise = jnp.where(own, noise_ref[pl.ds(part, 1), :], 0.0)
    chunks, chunk = block_ref.shape[:2]
    ids = (chunk, count)
    below = lax.broadcasted_iota(jnp.int32, ids, 0) - lax.broadcasted_iota(jnp.int32, ids, 1)
    copies = []
    for number in range(chunks):
        place = slice(number * chunk, (number + 1) * chunk)
        tile = kern(left_ref[place, :], left_half_ref[place, :], right, right_half)
        tile = tile + jnp.where(below == part * count - number * chunk, noise, 0.0)
        update = product(join_left(rows_high_ref[place, :], rows_low_ref[place, :]), cols_panel)
        block_ref[number] = tile - update
        copy = pltpu.make_async_copy(block_ref.at[number], out_ref.at[pl.ds(number * chunk, chunk)], sems.at[number])
        copy.start()
        copies.append(copy)
    for copy in copies:
        copy.wait()


def shape(dims, kind=f32):
    return jax.ShapeDtypeStruct(dims, kind)


def compute_params(flops, moved):
    return dict(
        compiler_params=pltpu.CompilerParams(vmem_limit_bytes=vmem_bytes),
        cost_estimate=pl.CostEstimate(flops=flops, bytes_accessed=moved, transcendentals=0),
    )


def links_of(place, group, target_row, across):
    links = []
    step = 1 if target_row > group else -1
    links += [(0, place, z, step) for z in range(group, target_row, step)]
    (x, y), (end_x, end_y) = (place % across, place // across), (group % across, group // across)
    step = 1 if end_x > x else -1
    links += [(1, target_row, y, at, step) for at in range(x, end_x, step)]
    step = 1 if end_y > y else -1
    links += [(2, target_row, end_x, at, step) for at in range(y, end_y, step)]
    return links


def source_places(rows, halves):
    draw = random.Random(5)
    across = math.isqrt(rows)
    places = {}
    load = collections.Counter()

    def move(key, r, sign):
        change = 0
        for link in links_of(places[key][r], key[1], r, across):
            old = load[link]
            load[link] = old + sign
            change += (old + sign) ** 4 - old**4
        return change

    for h in range(halves):
        for g in range(rows):
            places[h, g] = draw.sample(range(rows), rows)
            if g == 0:
                places[h, g].remove(0)
                places[h, g].insert(0, 0)
            for r in range(rows):
                move((h, g), r, 1)
    best, total, kept = 0, 0, {key: list(value) for key, value in places.items()}
    tries = 20000
    for number in range(tries):
        key = draw.randrange(halves), draw.randrange(rows)
        one, two = draw.sample(range(key[1] == 0, rows), 2)
        own = places[key]
        change = move(key, one, -1) + move(key, two, -1)
        own[one], own[two] = own[two], own[one]
        change += move(key, one, 1) + move(key, two, 1)
        heat = 30.0 * (1 - number / tries) + 0.01
        if change <= 0 or draw.random() < math.exp(-change / heat):
            total += change
            if total < best:
                best, kept = total, {key: list(value) for key, value in places.items()}
        else:
            move(key, one, -1), move(key, two, -1)
            own[one], own[two] = own[two], own[one]
            move(key, one, 1), move(key, two, 1)
    return kept


def column_pairs(rows, cols):
    halves = cols // rows
    places = source_places(rows, halves)
    return [
        (g * cols + places[h, g][r] * halves + h, r * cols + g * halves + h)
        for h in range(halves)
        for g in range(rows)
        for r in range(rows)
    ]


def swap(value, bit, cols):
    return lax.ppermute(value, "col", [(i, i ^ bit) for i in range(cols)])


def gather_panel(others, mine, panel_block, cols):
    col_place = lax.axis_index("col")
    core = col_place % 2
    got, mine = lax.optimization_barrier((swap(others, 1, cols), mine))
    held = jnp.where(panel_block % 2 == core, mine, got)
    apart = panel_block ^ col_place
    low = 2
    while low < cols:
        high = min(4 * low, cols)
        away = apart & (high - low)
        received = [swap(held, bits, cols) for bits in range(low, high, low)]
        for bits, value in zip(range(low, high, low), received):
            held = jnp.where(away == bits, value, held)
        low = high
    return [held, swap(held, 1, cols)]


def on_device(points, panel_pool, order, panel_index, inv_factor, ard_weights, noise):
    row_count, features = points.shape
    panel = inv_factor.shape[0]
    rows = lax.axis_size("row")
    cols = lax.axis_size("col")
    col_count = row_count * rows // cols
    halves = cols // rows
    half_rows = panel_pool.shape[0] // 2
    col_place = lax.axis_index("col")

    core = col_place % 2
    own_half = lax.dynamic_slice_in_dim(points, col_place % halves * col_count, col_count, 0)
    others = lax.dynamic_slice_in_dim(panel_pool, (1 - core) * half_rows, half_rows, 0)
    mine = lax.dynamic_slice_in_dim(panel_pool, core * half_rows, half_rows, 0)
    sent = lax.ppermute(own_half, ("row", "col"), column_pairs(rows, cols))
    pieces = gather_panel(others, mine, panel_index[0], cols)
    scale = jnp.sqrt(ard_weights * log2_e)[None, :]

    square = shape((panel, panel), bf16)
    high, low, turned_high, turned_low, pick, left, left_half = pl.pallas_call(
        parts_kernel,
        out_shape=[square] * 5 + [shape((row_count, 6 * features), bf16), shape((row_count, 1))],
        **compute_params(10**8, 4 * 10**6),
    )(inv_factor, order[None, :], points, scale)

    rows_high, rows_low, chosen, chosen_half = pl.pallas_call(
        rows_kernel,
        out_shape=[shape((row_count, panel), bf16)] * 2
        + [shape((panel, 6 * features), bf16), shape((panel, 1))],
        **compute_params(1, 1),
    )(*pieces, scale, turned_high, turned_low, pick, left, left_half)

    chunks = 2
    return pl.pallas_call(
        functools.partial(update_kernel, rows, cols),
        out_shape=shape((row_count, col_count)),
        out_specs=pl.BlockSpec(memory_space=pl.ANY),
        scratch_shapes=[
            pltpu.VMEM((chunks, row_count // chunks, col_count), f32),
            pltpu.SemaphoreType.DMA((chunks,)),
        ],
        **compute_params(4 * 10**9, 8 * 10**6),
    )(
        sent, scale, noise.reshape(halves, col_count), high, low, left, left_half, rows_high, rows_low,
        chosen, chosen_half,
    )


def solution(mesh):
    in_specs = (P("row", None), P("col", None), P(), P(), P(), P(), P("row"))
    out_specs = P("row", "col")
    return jax.shard_map(
        on_device, mesh=mesh, in_specs=in_specs, out_specs=out_specs, check_vma=False
    )
```

```python
import collections
import functools
import math
import random

import jax
import jax.numpy as jnp
from jax import lax
from jax.experimental import pallas as pl
from jax.experimental.pallas import tpu as pltpu
from jax.sharding import PartitionSpec as P

log2_e = 1.4426950408889634
vmem_bytes = 32 * 1024 * 1024
f32, bf16 = jnp.float32, jnp.bfloat16


def halves_of(value):
    high = value.astype(bf16)
    low = (value - high.astype(f32)).astype(bf16)
    return high, low


def thirds_of(value):
    high = value.astype(bf16)
    rest = value - high.astype(f32)
    middle = rest.astype(bf16)
    low = (rest - middle.astype(f32)).astype(bf16)
    return high, middle, low


def pack_left(value):
    high, middle, low = thirds_of(value)
    return jnp.concatenate([high, middle, high, middle, high, low], axis=1)


def pack_right(value):
    high, middle, low = thirds_of(value)
    return jnp.concatenate([high, middle, middle, high, low, high], axis=0)


def product(left, right):
    return lax.dot_general(left, right, (((1,), (0,)), ((), ())), preferred_element_type=f32)


def join_left(high, low):
    return jnp.concatenate([high, high, low], axis=1)


def join_right(high, low):
    return jnp.concatenate([high, low, high], axis=0)


def kern(crossed, left_half, right_half):
    return jnp.exp2((crossed - left_half) - (right_half - 1.0))


def scale_of(weights_ref):
    return jnp.sqrt(weights_ref[...] * log2_e)


def parts_kernel(
    factor_ref, order_ref, points_ref, weights_ref, high_ref, low_ref, turned_high_ref, turned_low_ref, pick_ref,
    left_ref, left_half_ref,
):
    factor = factor_ref[...]
    high_ref[...], low_ref[...] = halves_of(factor)
    turned_high_ref[...], turned_low_ref[...] = halves_of(jnp.transpose(factor))
    panel = factor.shape[0]
    core = lax.axis_index("col") % 2
    place = lax.broadcasted_iota(jnp.int32, (panel, panel), 0) + core * (panel // 2)
    place = jnp.where(place >= panel, place - panel, place)
    hit = jnp.where(place == order_ref[...], 1.0, 0.0).astype(f32)
    pick_ref[...] = jnp.transpose(hit).astype(bf16)
    scaled = points_ref[...] * scale_of(weights_ref)
    left_ref[...] = pack_left(scaled)
    left_half_ref[...] = 0.5 * jnp.sum(scaled * scaled, axis=1, keepdims=True)


def rows_kernel(
    own_ref, other_ref, weights_ref, turned_high_ref, turned_low_ref, pick_ref, left_ref, left_half_ref,
    rows_high_ref, rows_low_ref, chosen_ref, chosen_half_ref,
):
    panel = pick_ref.shape[0]
    mid = panel // 2
    block = jnp.concatenate([own_ref[...], other_ref[...]], axis=0) * scale_of(weights_ref)
    features = block.shape[1]
    parts = product(pick_ref[...], jnp.concatenate(thirds_of(block), axis=1))
    chosen = (parts[:, :features] + parts[:, features : 2 * features]) + parts[:, 2 * features :]
    turned = jnp.transpose(chosen)
    right = pack_right(turned)
    right_half = 0.5 * jnp.sum(turned * turned, axis=0, keepdims=True)
    chosen_ref[...] = pack_left(chosen)
    chosen_half_ref[...] = 0.5 * jnp.sum(chosen * chosen, axis=1, keepdims=True)
    first_right = join_right(turned_high_ref[:mid, :mid], turned_low_ref[:mid, :mid])
    second_right = join_right(turned_high_ref[:, mid:], turned_low_ref[:, mid:])
    chunks = 4
    count = left_ref.shape[0] // chunks
    places = [slice(number * count, (number + 1) * count) for number in range(chunks)]
    crossed = product(left_ref[places[0], :], right)
    for number, place in enumerate(places):
        now = crossed
        if number + 1 < chunks:
            crossed = product(left_ref[places[number + 1], :], right)
        kern_high, kern_low = halves_of(kern(now, left_half_ref[place, :], right_half))
        first = product(join_left(kern_high[:, :mid], kern_low[:, :mid]), first_right)
        second = product(join_left(kern_high, kern_low), second_right)
        rows_high_ref[place, :mid], rows_low_ref[place, :mid] = halves_of(first)
        rows_high_ref[place, mid:], rows_low_ref[place, mid:] = halves_of(second)


def update_kernel(
    rows, cols, sent_ref, weights_ref, noise_ref, high_ref, low_ref, left_ref, left_half_ref, rows_high_ref,
    rows_low_ref, chosen_ref, chosen_half_ref, out_ref, block_ref, sems,
):
    row_place, col_place = lax.axis_index("row"), lax.axis_index("col")
    halves = cols // rows
    count = sent_ref.shape[0]
    part = col_place % halves
    own = row_place == col_place // halves
    panel = high_ref.shape[0]
    mid = panel // 2

    turned = jnp.transpose(sent_ref[...] * scale_of(weights_ref))
    right = pack_right(turned)
    right_half = 0.5 * jnp.sum(turned * turned, axis=0, keepdims=True)
    chunks, chunk = block_ref.shape[:2]
    places = [slice(number * chunk, (number + 1) * chunk) for number in range(chunks)]
    noise = jnp.where(own, noise_ref[:, pl.ds(pl.multiple_of(part * count, count), count)], 0.0)
    ids = (chunk, count)
    below = lax.broadcasted_iota(jnp.int32, ids, 0) - lax.broadcasted_iota(jnp.int32, ids, 1)

    crossed = product(chosen_ref[...], right)
    tiles = [product(left_ref[place, :], right) for place in places]
    kern_high, kern_low = halves_of(kern(crossed, chosen_half_ref[...], right_half))
    upper = product(
        join_left(high_ref[:mid, :mid], low_ref[:mid, :mid]), join_right(kern_high[:mid], kern_low[:mid])
    )
    lower = product(join_left(high_ref[mid:, :], low_ref[mid:, :]), join_right(kern_high, kern_low))
    for number, place in enumerate(places):
        tile = kern(tiles[number], left_half_ref[place, :], right_half)
        block_ref[number] = tile + jnp.where(below == part * count - number * chunk, noise, 0.0)
    cols_panel = join_right(*halves_of(jnp.concatenate([upper, lower], axis=0)))

    copies = []
    for number, place in enumerate(places):
        update = product(join_left(rows_high_ref[place, :], rows_low_ref[place, :]), cols_panel)
        block_ref[number] = block_ref[number] - update
        copy = pltpu.make_async_copy(block_ref.at[number], out_ref.at[pl.ds(number * chunk, chunk)], sems.at[number])
        copy.start()
        copies.append(copy)
    for copy in copies:
        copy.wait()


def shape(dims, kind=f32):
    return jax.ShapeDtypeStruct(dims, kind)


def compute_params(flops, moved):
    return dict(
        compiler_params=pltpu.CompilerParams(vmem_limit_bytes=vmem_bytes),
        cost_estimate=pl.CostEstimate(flops=flops, bytes_accessed=moved, transcendentals=0),
    )


def links_of(place, group, target_row, across):
    links = []
    step = 1 if target_row > group else -1
    links += [(0, place, z, step) for z in range(group, target_row, step)]
    (x, y), (end_x, end_y) = (place % across, place // across), (group % across, group // across)
    step = 1 if end_x > x else -1
    links += [(1, target_row, y, at, step) for at in range(x, end_x, step)]
    step = 1 if end_y > y else -1
    links += [(2, target_row, end_x, at, step) for at in range(y, end_y, step)]
    return links


def source_places(rows, halves):
    draw = random.Random(5)
    across = math.isqrt(rows)
    places = {}
    load = collections.Counter()

    def move(key, r, sign):
        change = 0
        for link in links_of(places[key][r], key[1], r, across):
            old = load[link]
            load[link] = old + sign
            change += (old + sign) ** 4 - old**4
        return change

    for h in range(halves):
        for g in range(rows):
            places[h, g] = draw.sample(range(rows), rows)
            if g == 0:
                places[h, g].remove(0)
                places[h, g].insert(0, 0)
            for r in range(rows):
                move((h, g), r, 1)
    best, total, kept = 0, 0, {key: list(value) for key, value in places.items()}
    tries = 20000
    for number in range(tries):
        key = draw.randrange(halves), draw.randrange(rows)
        one, two = draw.sample(range(key[1] == 0, rows), 2)
        own = places[key]
        change = move(key, one, -1) + move(key, two, -1)
        own[one], own[two] = own[two], own[one]
        change += move(key, one, 1) + move(key, two, 1)
        heat = 30.0 * (1 - number / tries) + 0.01
        if change <= 0 or draw.random() < math.exp(-change / heat):
            total += change
            if total < best:
                best, kept = total, {key: list(value) for key, value in places.items()}
        else:
            move(key, one, -1), move(key, two, -1)
            own[one], own[two] = own[two], own[one]
            move(key, one, 1), move(key, two, 1)
    return kept


def column_pairs(rows, cols):
    halves = cols // rows
    places = source_places(rows, halves)
    return [
        (g * cols + places[h, g][r] * halves + h, r * cols + g * halves + h)
        for h in range(halves)
        for g in range(rows)
        for r in range(rows)
    ]


def swap(value, bit, cols):
    return lax.ppermute(value, "col", [(i, i ^ bit) for i in range(cols)])


def gather_panel(panel_pool, panel_block, cols):
    col_place = lax.axis_index("col")
    core = col_place % 2
    half_rows = panel_pool.shape[0] // 2
    others = lax.dynamic_slice_in_dim(panel_pool, (1 - core) * half_rows, half_rows, 0)
    mine = lax.dynamic_slice_in_dim(panel_pool, core * half_rows, half_rows, 0)
    got, mine = lax.optimization_barrier((swap(others, 1, cols), mine))
    held = jnp.where(panel_block % 2 == core, mine, got)
    apart = panel_block ^ col_place
    low = 2
    while low < cols:
        high = min(4 * low, cols)
        away = apart & (high - low)
        received = [swap(held, bits, cols) for bits in range(low, high, low)]
        for bits, value in zip(range(low, high, low), received):
            held = jnp.where(away == bits, value, held)
        low = high
    return [held, swap(held, 1, cols)]


def on_device(points, panel_pool, order, panel_index, inv_factor, ard_weights, noise):
    row_count, features = points.shape
    panel = inv_factor.shape[0]
    rows = lax.axis_size("row")
    cols = lax.axis_size("col")
    col_count = row_count * rows // cols
    halves = cols // rows
    col_place = lax.axis_index("col")
    own_half = lax.dynamic_slice_in_dim(points, col_place % halves * col_count, col_count, 0)
    sent = lax.ppermute(own_half, ("row", "col"), column_pairs(rows, cols))
    pieces = gather_panel(panel_pool, panel_index[0], cols)
    weights = ard_weights[None, :]

    square = shape((panel, panel), bf16)
    high, low, turned_high, turned_low, pick, left, left_half = pl.pallas_call(
        parts_kernel,
        out_shape=[square] * 5 + [shape((row_count, 6 * features), bf16), shape((row_count, 1))],
        **compute_params(10**8, 4 * 10**6),
    )(inv_factor, order[None, :], points, weights)

    rows_high, rows_low, chosen, chosen_half = pl.pallas_call(
        rows_kernel,
        out_shape=[shape((row_count, panel), bf16)] * 2
        + [shape((panel, 6 * features), bf16), shape((panel, 1))],
        **compute_params(1, 1),
    )(*pieces, weights, turned_high, turned_low, pick, left, left_half)

    chunks = 4
    return pl.pallas_call(
        functools.partial(update_kernel, rows, cols),
        out_shape=shape((row_count, col_count)),
        out_specs=pl.BlockSpec(memory_space=pl.ANY),
        scratch_shapes=[
            pltpu.VMEM((chunks, row_count // chunks, col_count), f32),
            pltpu.SemaphoreType.DMA((chunks,)),
        ],
        **compute_params(4 * 10**9, 8 * 10**6),
    )(
        sent, weights, noise[None, :], high, low, left, left_half, rows_high, rows_low,
        chosen, chosen_half,
    )


def solution(mesh):
    in_specs = (P("row", None), P("col", None), P(), P(), P(), P(), P("row"))
    out_specs = P("row", "col")
    return jax.shard_map(
        on_device, mesh=mesh, in_specs=in_specs, out_specs=out_specs, check_vma=False
    )
```

```python
import collections
import functools
import math
import random

import jax
import jax.numpy as jnp
from jax import lax
from jax.experimental import pallas as pl
from jax.experimental.pallas import tpu as pltpu
from jax.sharding import PartitionSpec as P

log2_e = 1.4426950408889634
vmem_bytes = 32 * 1024 * 1024
f32, bf16 = jnp.float32, jnp.bfloat16
block = 256


def halves_of(value):
    high = value.astype(bf16)
    low = (value - high.astype(f32)).astype(bf16)
    return high, low


def pack_left(high, low):
    return jnp.concatenate([high, low, high, low], axis=1)


def pack_right(high, low):
    return jnp.concatenate([high, low, low, high], axis=0)


def half_square(high, low, axis):
    value = high.astype(f32) + low.astype(f32)
    return 0.5 * jnp.sum(value * value, axis=axis, keepdims=True)


def product(left, right):
    return lax.dot_general(left, right, (((1,), (0,)), ((), ())), preferred_element_type=f32)


def store_left(ref, rows, first, value):
    high, low = halves_of(value)
    for start in range(0, value.shape[1], block):
        now, at = slice(start, start + block), 3 * (first + start)
        ref[rows, at : at + block] = high[:, now]
        ref[rows, at + block : at + 2 * block] = high[:, now]
        ref[rows, at + 2 * block : at + 3 * block] = low[:, now]


def store_right(ref, first, value):
    high, low = halves_of(value)
    for start in range(0, value.shape[0], block):
        now, at = slice(start, start + block), 3 * (first + start)
        ref[at : at + block, :] = high[now]
        ref[at + block : at + 2 * block, :] = low[now]
        ref[at + 2 * block : at + 3 * block, :] = high[now]


def kern(crossed, left_half, right_half):
    return jnp.exp2((crossed - left_half) - (right_half - 1.0))


def scale_of(weights_ref):
    return jnp.sqrt(weights_ref[...] * log2_e)


def parts_kernel(
    factor_ref, order_ref, points_ref, weights_ref, factor_left_ref, factor_right_ref, pick_ref, left_ref,
    left_half_ref,
):
    factor = factor_ref[...]
    store_left(factor_left_ref, slice(None), 0, factor)
    store_right(factor_right_ref, 0, jnp.transpose(factor))
    panel = factor.shape[0]
    core = lax.axis_index("col") % 2
    place = lax.broadcasted_iota(jnp.int32, (panel, panel), 0) + core * (panel // 2)
    place = jnp.where(place >= panel, place - panel, place)
    hit = jnp.where(place == order_ref[...], 1.0, 0.0).astype(f32)
    pick_ref[...] = jnp.transpose(hit).astype(bf16)
    high, low = halves_of(points_ref[...] * scale_of(weights_ref))
    left_ref[...] = pack_left(high, low)
    left_half_ref[...] = half_square(high, low, 1)


def rows_kernel(
    own_ref, other_ref, weights_ref, factor_right_ref, pick_ref, left_ref, left_half_ref,
    rows_ref, chosen_ref, chosen_half_ref, kern_ref,
):
    panel = pick_ref.shape[0]
    features = own_ref.shape[1]
    held = jnp.concatenate([own_ref[...], other_ref[...]], axis=0) * scale_of(weights_ref)
    chosen = product(pick_ref[...], jnp.concatenate(halves_of(held), axis=1))
    high, low = chosen[:, :features].astype(bf16), chosen[:, features:].astype(bf16)
    chosen_ref[...] = pack_left(high, low)
    chosen_half_ref[...] = half_square(high, low, 1)
    turned = jnp.transpose(chosen)
    high, low = turned[:features].astype(bf16), turned[features:].astype(bf16)
    right = pack_right(high, low)
    right_half = half_square(high, low, 0)
    chunks = 2
    count = left_ref.shape[0] // chunks
    places = [slice(number * count, (number + 1) * count) for number in range(chunks)]
    crossed = [product(left_ref[place, :], right) for place in places]
    for number, place in enumerate(places):
        store_left(kern_ref, place, 0, kern(crossed[number], left_half_ref[place, :], right_half))
        for first in range(0, panel, block):
            last = first + block
            part = product(kern_ref[place, : 3 * last], factor_right_ref[: 3 * last, first:last])
            store_left(rows_ref, place, first, part)


def update_kernel(
    rows, cols, sent_ref, weights_ref, noise_ref, factor_left_ref, left_ref, left_half_ref, rows_ref, chosen_ref,
    chosen_half_ref, out_ref, block_ref, kern_ref, cols_ref, sems,
):
    row_place, col_place = lax.axis_index("row"), lax.axis_index("col")
    halves = cols // rows
    count = sent_ref.shape[0]
    part = col_place % halves
    own = row_place == col_place // halves
    panel = factor_left_ref.shape[0]

    high, low = halves_of(jnp.transpose(sent_ref[...] * scale_of(weights_ref)))
    right = pack_right(high, low)
    right_half = half_square(high, low, 0)
    chunks, chunk = block_ref.shape[:2]
    places = [slice(number * chunk, (number + 1) * chunk) for number in range(chunks)]
    noise = jnp.where(own, noise_ref[:, pl.ds(pl.multiple_of(part * count, count), count)], 0.0)
    ids = (chunk, count)
    below = lax.broadcasted_iota(jnp.int32, ids, 0) - lax.broadcasted_iota(jnp.int32, ids, 1)

    crossed = product(chosen_ref[...], right)
    tiles = [product(left_ref[place, :], right) for place in places]
    store_right(kern_ref, 0, kern(crossed, chosen_half_ref[...], right_half))
    for first in range(0, panel, block):
        last = first + block
        store_right(cols_ref, first, product(factor_left_ref[first:last, : 3 * last], kern_ref[: 3 * last, :]))
    for number, place in enumerate(places):
        tile = kern(tiles[number], left_half_ref[place, :], right_half)
        block_ref[number] = tile + jnp.where(below == part * count - number * chunk, noise, 0.0)

    copies = []
    for number, place in enumerate(places):
        block_ref[number] = block_ref[number] - product(rows_ref[place, :], cols_ref[...])
        copy = pltpu.make_async_copy(block_ref.at[number], out_ref.at[pl.ds(number * chunk, chunk)], sems.at[number])
        copy.start()
        copies.append(copy)
    for copy in copies:
        copy.wait()


def shape(dims, kind=f32):
    return jax.ShapeDtypeStruct(dims, kind)


def compute_params(flops, moved):
    return dict(
        compiler_params=pltpu.CompilerParams(vmem_limit_bytes=vmem_bytes),
        cost_estimate=pl.CostEstimate(flops=flops, bytes_accessed=moved, transcendentals=0),
    )


def links_of(place, group, target_row, across):
    links = []
    step = 1 if target_row > group else -1
    links += [(0, place, z, step) for z in range(group, target_row, step)]
    (x, y), (end_x, end_y) = (place % across, place // across), (group % across, group // across)
    step = 1 if end_x > x else -1
    links += [(1, target_row, y, at, step) for at in range(x, end_x, step)]
    step = 1 if end_y > y else -1
    links += [(2, target_row, end_x, at, step) for at in range(y, end_y, step)]
    return links


def source_places(rows, halves):
    draw = random.Random(5)
    across = math.isqrt(rows)
    places = {}
    load = collections.Counter()

    def move(key, r, sign):
        change = 0
        for link in links_of(places[key][r], key[1], r, across):
            old = load[link]
            load[link] = old + sign
            change += (old + sign) ** 4 - old**4
        return change

    for h in range(halves):
        for g in range(rows):
            places[h, g] = draw.sample(range(rows), rows)
            if g == 0:
                places[h, g].remove(0)
                places[h, g].insert(0, 0)
            for r in range(rows):
                move((h, g), r, 1)
    best, total, kept = 0, 0, {key: list(value) for key, value in places.items()}
    tries = 20000
    for number in range(tries):
        key = draw.randrange(halves), draw.randrange(rows)
        one, two = draw.sample(range(key[1] == 0, rows), 2)
        own = places[key]
        change = move(key, one, -1) + move(key, two, -1)
        own[one], own[two] = own[two], own[one]
        change += move(key, one, 1) + move(key, two, 1)
        heat = 30.0 * (1 - number / tries) + 0.01
        if change <= 0 or draw.random() < math.exp(-change / heat):
            total += change
            if total < best:
                best, kept = total, {key: list(value) for key, value in places.items()}
        else:
            move(key, one, -1), move(key, two, -1)
            own[one], own[two] = own[two], own[one]
            move(key, one, 1), move(key, two, 1)
    return kept


def column_pairs(rows, cols):
    halves = cols // rows
    places = source_places(rows, halves)
    return [
        (g * cols + places[h, g][r] * halves + h, r * cols + g * halves + h)
        for h in range(halves)
        for g in range(rows)
        for r in range(rows)
    ]


def swap(value, bit, cols):
    return lax.ppermute(value, "col", [(i, i ^ bit) for i in range(cols)])


def gather_panel(panel_pool, panel_block, cols):
    col_place = lax.axis_index("col")
    core = col_place % 2
    half_rows = panel_pool.shape[0] // 2
    others = lax.dynamic_slice_in_dim(panel_pool, (1 - core) * half_rows, half_rows, 0)
    mine = lax.dynamic_slice_in_dim(panel_pool, core * half_rows, half_rows, 0)
    got, mine = lax.optimization_barrier((swap(others, 1, cols), mine))
    held = jnp.where(panel_block % 2 == core, mine, got)
    apart = panel_block ^ col_place
    low = 2
    while low < cols:
        high = min(4 * low, cols)
        away = apart & (high - low)
        received = [swap(held, bits, cols) for bits in range(low, high, low)]
        for bits, value in zip(range(low, high, low), received):
            held = jnp.where(away == bits, value, held)
        low = high
    return [held, swap(held, 1, cols)]


def on_device(points, panel_pool, order, panel_index, inv_factor, ard_weights, noise):
    row_count, features = points.shape
    panel = inv_factor.shape[0]
    rows = lax.axis_size("row")
    cols = lax.axis_size("col")
    col_count = row_count * rows // cols
    halves = cols // rows
    col_place = lax.axis_index("col")
    own_half = lax.dynamic_slice_in_dim(points, col_place % halves * col_count, col_count, 0)
    sent = lax.ppermute(own_half, ("row", "col"), column_pairs(rows, cols))
    pieces = gather_panel(panel_pool, panel_index[0], cols)
    weights = ard_weights[None, :]

    packed = 4 * features
    factor_left, factor_right, pick, left, left_half = pl.pallas_call(
        parts_kernel,
        out_shape=[
            shape((panel, 3 * panel), bf16),
            shape((3 * panel, panel), bf16),
            shape((panel, panel), bf16),
            shape((row_count, packed), bf16),
            shape((row_count, 1)),
        ],
        **compute_params(10**8, 4 * 10**6),
    )(inv_factor, order[None, :], points, weights)

    rows_left, chosen, chosen_half = pl.pallas_call(
        rows_kernel,
        out_shape=[shape((row_count, 3 * panel), bf16), shape((panel, packed), bf16), shape((panel, 1))],
        scratch_shapes=[pltpu.VMEM((row_count, 3 * panel), bf16)],
        **compute_params(1, 1),
    )(*pieces, weights, factor_right, pick, left, left_half)

    chunks = 2
    return pl.pallas_call(
        functools.partial(update_kernel, rows, cols),
        out_shape=shape((row_count, col_count)),
        out_specs=pl.BlockSpec(memory_space=pl.ANY),
        scratch_shapes=[
            pltpu.VMEM((chunks, row_count // chunks, col_count), f32),
            pltpu.VMEM((3 * panel, col_count), bf16),
            pltpu.VMEM((3 * panel, col_count), bf16),
            pltpu.SemaphoreType.DMA((chunks,)),
        ],
        **compute_params(4 * 10**9, 8 * 10**6),
    )(sent, weights, noise[None, :], factor_left, left, left_half, rows_left, chosen, chosen_half)


def solution(mesh):
    in_specs = (P("row", None), P("col", None), P(), P(), P(), P(), P("row"))
    out_specs = P("row", "col")
    return jax.shard_map(
        on_device, mesh=mesh, in_specs=in_specs, out_specs=out_specs, check_vma=False
    )
```

```python
import collections
import functools
import math
import random

import jax
import jax.numpy as jnp
from jax import lax
from jax.experimental import pallas as pl
from jax.experimental.pallas import tpu as pltpu
from jax.sharding import PartitionSpec as P

log2_e = 1.4426950408889634
vmem_bytes = 32 * 1024 * 1024
f32, bf16 = jnp.float32, jnp.bfloat16
block = 256


def halves_of(value):
    high = value.astype(bf16)
    low = (value - high.astype(f32)).astype(bf16)
    return high, low


def pack_left(high, low):
    return jnp.concatenate([high, low, high, low], axis=1)


def pack_right(high, low):
    return jnp.concatenate([high, low, low, high], axis=0)


def half_square(high, low, axis):
    value = high.astype(f32) + low.astype(f32)
    return 0.5 * jnp.sum(value * value, axis=axis, keepdims=True)


def product(left, right):
    return lax.dot_general(left, right, (((1,), (0,)), ((), ())), preferred_element_type=f32)


def store_left(ref, rows, first, value):
    high, low = halves_of(value)
    for start in range(0, value.shape[1], block):
        now, at = slice(start, start + block), 3 * (first + start)
        ref[rows, at : at + block] = high[:, now]
        ref[rows, at + block : at + 2 * block] = high[:, now]
        ref[rows, at + 2 * block : at + 3 * block] = low[:, now]


def store_right(ref, first, value):
    high, low = halves_of(value)
    for start in range(0, value.shape[0], block):
        now, at = slice(start, start + block), 3 * (first + start)
        ref[at : at + block, :] = high[now]
        ref[at + block : at + 2 * block, :] = low[now]
        ref[at + 2 * block : at + 3 * block, :] = high[now]


def kern(crossed, left_half, right_half):
    return jnp.exp2((crossed - left_half) - (right_half - 1.0))


def scale_of(weights_ref):
    return jnp.sqrt(weights_ref[...] * log2_e)


def parts_kernel(
    factor_ref, order_ref, points_ref, weights_ref, factor_left_ref, factor_right_ref, pick_ref, left_ref,
    left_half_ref,
):
    factor = factor_ref[...]
    store_left(factor_left_ref, slice(None), 0, factor)
    store_right(factor_right_ref, 0, jnp.transpose(factor))
    panel = factor.shape[0]
    core = lax.axis_index("col") % 2
    place = lax.broadcasted_iota(jnp.int32, (panel, panel), 0) + core * (panel // 2)
    place = jnp.where(place >= panel, place - panel, place)
    hit = jnp.where(place == order_ref[...], 1.0, 0.0).astype(f32)
    pick_ref[...] = jnp.transpose(hit).astype(bf16)
    high, low = halves_of(points_ref[...] * scale_of(weights_ref))
    left_ref[...] = pack_left(high, low)
    left_half_ref[...] = half_square(high, low, 1)


def rows_kernel(
    own_ref, other_ref, weights_ref, factor_right_ref, pick_ref, left_ref, left_half_ref,
    rows_ref, chosen_ref, chosen_half_ref, kern_ref,
):
    panel = pick_ref.shape[0]
    features = own_ref.shape[1]
    held = jnp.concatenate([own_ref[...], other_ref[...]], axis=0) * scale_of(weights_ref)
    chosen = product(pick_ref[...], jnp.concatenate(halves_of(held), axis=1))
    high, low = chosen[:, :features].astype(bf16), chosen[:, features:].astype(bf16)
    chosen_ref[...] = pack_left(high, low)
    chosen_half_ref[...] = half_square(high, low, 1)
    turned = jnp.transpose(chosen)
    high, low = turned[:features].astype(bf16), turned[features:].astype(bf16)
    right = pack_right(high, low)
    right_half = half_square(high, low, 0)
    chunks = 2
    count = left_ref.shape[0] // chunks
    places = [slice(number * count, (number + 1) * count) for number in range(chunks)]
    crossed = [product(left_ref[place, :], right) for place in places]
    for number, place in enumerate(places):
        store_left(kern_ref, place, 0, kern(crossed[number], left_half_ref[place, :], right_half))
        for first in range(0, panel, block):
            last = first + block
            part = product(kern_ref[place, : 3 * last], factor_right_ref[: 3 * last, first:last])
            store_left(rows_ref, place, first, part)


def update_kernel(
    rows, cols, sent_ref, weights_ref, noise_ref, factor_left_ref, left_ref, left_half_ref, rows_ref, chosen_ref,
    chosen_half_ref, out_ref, block_ref, kern_ref, cols_ref, sems,
):
    row_place, col_place = lax.axis_index("row"), lax.axis_index("col")
    halves = cols // rows
    count = sent_ref.shape[0]
    part = col_place % halves
    own = row_place == col_place // halves
    panel = factor_left_ref.shape[0]

    high, low = halves_of(jnp.transpose(sent_ref[...] * scale_of(weights_ref)))
    right = pack_right(high, low)
    right_half = half_square(high, low, 0)
    chunks, chunk = block_ref.shape[:2]
    places = [slice(number * chunk, (number + 1) * chunk) for number in range(chunks)]
    noise = jnp.where(own, noise_ref[:, pl.ds(pl.multiple_of(part * count, count), count)], 0.0)
    ids = (chunk, count)
    below = lax.broadcasted_iota(jnp.int32, ids, 0) - lax.broadcasted_iota(jnp.int32, ids, 1)

    crossed = product(chosen_ref[...], right)
    tiles = [product(left_ref[place, :], right) for place in places]
    store_right(kern_ref, 0, kern(crossed, chosen_half_ref[...], right_half))
    for first in range(0, panel, block):
        last = first + block
        store_right(cols_ref, first, product(factor_left_ref[first:last, : 3 * last], kern_ref[: 3 * last, :]))
    for number, place in enumerate(places):
        tile = kern(tiles[number], left_half_ref[place, :], right_half)
        block_ref[number] = tile + jnp.where(below == part * count - number * chunk, noise, 0.0)

    copies = []
    for number, place in enumerate(places):
        block_ref[number] = block_ref[number] - product(rows_ref[place, :], cols_ref[...])
        copy = pltpu.make_async_copy(block_ref.at[number], out_ref.at[pl.ds(number * chunk, chunk)], sems.at[number])
        copy.start()
        copies.append(copy)
    for copy in copies:
        copy.wait()


def shape(dims, kind=f32):
    return jax.ShapeDtypeStruct(dims, kind)


def compute_params(flops, moved):
    return dict(
        compiler_params=pltpu.CompilerParams(vmem_limit_bytes=vmem_bytes),
        cost_estimate=pl.CostEstimate(flops=flops, bytes_accessed=moved, transcendentals=0),
    )


def links_of(place, group, target_row, across):
    links = []
    step = 1 if target_row > group else -1
    links += [(0, place, z, step) for z in range(group, target_row, step)]
    (x, y), (end_x, end_y) = (place % across, place // across), (group % across, group // across)
    step = 1 if end_x > x else -1
    links += [(1, target_row, y, at, step) for at in range(x, end_x, step)]
    step = 1 if end_y > y else -1
    links += [(2, target_row, end_x, at, step) for at in range(y, end_y, step)]
    return links


def source_places(rows, halves):
    draw = random.Random(5)
    across = math.isqrt(rows)
    places = {}
    load = collections.Counter()

    def move(key, r, sign):
        change = 0
        for link in links_of(places[key][r], key[1], r, across):
            old = load[link]
            load[link] = old + sign
            change += (old + sign) ** 4 - old**4
        return change

    for h in range(halves):
        for g in range(rows):
            places[h, g] = draw.sample(range(rows), rows)
            if g == 0:
                places[h, g].remove(0)
                places[h, g].insert(0, 0)
            for r in range(rows):
                move((h, g), r, 1)
    best, total, kept = 0, 0, {key: list(value) for key, value in places.items()}
    tries = 20000
    for number in range(tries):
        key = draw.randrange(halves), draw.randrange(rows)
        one, two = draw.sample(range(key[1] == 0, rows), 2)
        own = places[key]
        change = move(key, one, -1) + move(key, two, -1)
        own[one], own[two] = own[two], own[one]
        change += move(key, one, 1) + move(key, two, 1)
        heat = 30.0 * (1 - number / tries) + 0.01
        if change <= 0 or draw.random() < math.exp(-change / heat):
            total += change
            if total < best:
                best, kept = total, {key: list(value) for key, value in places.items()}
        else:
            move(key, one, -1), move(key, two, -1)
            own[one], own[two] = own[two], own[one]
            move(key, one, 1), move(key, two, 1)
    return kept


def column_pairs(rows, cols):
    halves = cols // rows
    places = source_places(rows, halves)
    return [
        (g * cols + places[h, g][r] * halves + h, r * cols + g * halves + h)
        for h in range(halves)
        for g in range(rows)
        for r in range(rows)
    ]


def swap(value, bit, cols):
    return lax.ppermute(value, "col", [(i, i ^ bit) for i in range(cols)])


def gather_panel(panel_pool, own_points, panel_block, cols):
    col_place = lax.axis_index("col")
    core = col_place % 2
    half_rows = panel_pool.shape[0] // 2
    mine = lax.dynamic_slice_in_dim(panel_pool, core * half_rows, half_rows, 0)
    others = lax.dynamic_slice_in_dim(panel_pool, (1 - core) * half_rows, half_rows, 0)
    got, mine, own_points = lax.optimization_barrier((swap(others, 1, cols), mine, own_points))
    held = jnp.where(panel_block % 2 == core, mine, got)
    apart = panel_block ^ col_place
    low = 2
    while low < cols:
        high = min(4 * low, cols)
        away = apart & (high - low)
        received = [swap(held, bits, cols) for bits in range(low, high, low)]
        for bits, value in zip(range(low, high, low), received):
            held = jnp.where(away == bits, value, held)
        low = high
    return [held, swap(held, 1, cols)], own_points


def on_device(points, panel_pool, order, panel_index, inv_factor, ard_weights, noise):
    row_count, features = points.shape
    panel = inv_factor.shape[0]
    rows = lax.axis_size("row")
    cols = lax.axis_size("col")
    col_count = row_count * rows // cols
    halves = cols // rows
    col_place = lax.axis_index("col")
    own_points = lax.dynamic_slice_in_dim(points, col_place % halves * col_count, col_count, 0)
    pieces, own_points = gather_panel(panel_pool, own_points, panel_index[0], cols)
    sent = lax.ppermute(own_points, ("row", "col"), column_pairs(rows, cols))
    weights = ard_weights[None, :]

    packed = 4 * features
    factor_left, factor_right, pick, left, left_half = pl.pallas_call(
        parts_kernel,
        out_shape=[
            shape((panel, 3 * panel), bf16),
            shape((3 * panel, panel), bf16),
            shape((panel, panel), bf16),
            shape((row_count, packed), bf16),
            shape((row_count, 1)),
        ],
        **compute_params(10**8, 4 * 10**6),
    )(inv_factor, order[None, :], points, weights)

    rows_left, chosen, chosen_half = pl.pallas_call(
        rows_kernel,
        out_shape=[shape((row_count, 3 * panel), bf16), shape((panel, packed), bf16), shape((panel, 1))],
        scratch_shapes=[pltpu.VMEM((row_count, 3 * panel), bf16)],
        **compute_params(1, 1),
    )(*pieces, weights, factor_right, pick, left, left_half)

    chunks = 2
    return pl.pallas_call(
        functools.partial(update_kernel, rows, cols),
        out_shape=shape((row_count, col_count)),
        out_specs=pl.BlockSpec(memory_space=pl.ANY),
        scratch_shapes=[
            pltpu.VMEM((chunks, row_count // chunks, col_count), f32),
            pltpu.VMEM((3 * panel, col_count), bf16),
            pltpu.VMEM((3 * panel, col_count), bf16),
            pltpu.SemaphoreType.DMA((chunks,)),
        ],
        **compute_params(4 * 10**9, 8 * 10**6),
    )(sent, weights, noise[None, :], factor_left, left, left_half, rows_left, chosen, chosen_half)


def solution(mesh):
    in_specs = (P("row", None), P("col", None), P(), P(), P(), P(), P("row"))
    out_specs = P("row", "col")
    return jax.shard_map(
        on_device, mesh=mesh, in_specs=in_specs, out_specs=out_specs, check_vma=False
    )
```

```python
import collections
import functools
import math
import random

import jax
import jax.numpy as jnp
from jax import lax
from jax.experimental import pallas as pl
from jax.experimental.pallas import tpu as pltpu
from jax.sharding import PartitionSpec as P

log2_e = 1.4426950408889634
vmem_bytes = 32 * 1024 * 1024
f32, bf16 = jnp.float32, jnp.bfloat16
block = 256


def halves_of(value):
    high = value.astype(bf16)
    low = (value - high.astype(f32)).astype(bf16)
    return high, low


def pack_left(high, low):
    return jnp.concatenate([high, low, high, low], axis=1)


def pack_right(high, low):
    return jnp.concatenate([high, low, low, high], axis=0)


def half_square(high, low, axis):
    value = high.astype(f32) + low.astype(f32)
    return 0.5 * jnp.sum(value * value, axis=axis, keepdims=True)


def product(left, right):
    return lax.dot_general(left, right, (((1,), (0,)), ((), ())), preferred_element_type=f32)


def store_left(ref, rows, first, value):
    high, low = halves_of(value)
    for start in range(0, value.shape[1], block):
        now, at = slice(start, start + block), 3 * (first + start)
        ref[rows, at : at + block] = high[:, now]
        ref[rows, at + block : at + 2 * block] = high[:, now]
        ref[rows, at + 2 * block : at + 3 * block] = low[:, now]


def store_right(ref, first, value):
    high, low = halves_of(value)
    for start in range(0, value.shape[0], block):
        now, at = slice(start, start + block), 3 * (first + start)
        ref[at : at + block, :] = high[now]
        ref[at + block : at + 2 * block, :] = low[now]
        ref[at + 2 * block : at + 3 * block, :] = high[now]


def kern(crossed, left_half, right_half):
    return jnp.exp2((crossed - left_half) - (right_half - 1.0))


def scale_of(weights_ref):
    return jnp.sqrt(weights_ref[...] * log2_e)


def parts_kernel(
    factor_ref, order_ref, points_ref, weights_ref, factor_left_ref, factor_right_ref, pick_ref, left_ref,
    left_half_ref,
):
    factor = factor_ref[...]
    store_left(factor_left_ref, slice(None), 0, factor)
    store_right(factor_right_ref, 0, jnp.transpose(factor))
    panel = factor.shape[0]
    core = lax.axis_index("col") % 2
    place = lax.broadcasted_iota(jnp.int32, (panel, panel), 0) + core * (panel // 2)
    place = jnp.where(place >= panel, place - panel, place)
    hit = jnp.where(place == order_ref[...], 1.0, 0.0).astype(f32)
    pick_ref[...] = jnp.transpose(hit).astype(bf16)
    high, low = halves_of(points_ref[...] * scale_of(weights_ref))
    left_ref[...] = pack_left(high, low)
    left_half_ref[...] = half_square(high, low, 1)


def rows_kernel(
    own_ref, other_ref, weights_ref, factor_right_ref, pick_ref, left_ref, left_half_ref,
    rows_ref, chosen_ref, chosen_half_ref, kern_ref,
):
    panel = pick_ref.shape[0]
    features = own_ref.shape[1]
    held = jnp.concatenate([own_ref[...], other_ref[...]], axis=0) * scale_of(weights_ref)
    chosen = product(pick_ref[...], jnp.concatenate(halves_of(held), axis=1))
    high, low = chosen[:, :features].astype(bf16), chosen[:, features:].astype(bf16)
    chosen_ref[...] = pack_left(high, low)
    chosen_half_ref[...] = half_square(high, low, 1)
    turned = jnp.transpose(chosen)
    high, low = turned[:features].astype(bf16), turned[features:].astype(bf16)
    right = pack_right(high, low)
    right_half = half_square(high, low, 0)
    chunks = 2
    count = left_ref.shape[0] // chunks
    places = [slice(number * count, (number + 1) * count) for number in range(chunks)]
    crossed = [product(left_ref[place, :], right) for place in places]
    for number, place in enumerate(places):
        store_left(kern_ref, place, 0, kern(crossed[number], left_half_ref[place, :], right_half))
        for first in range(0, panel, block):
            last = first + block
            part = product(kern_ref[place, : 3 * last], factor_right_ref[: 3 * last, first:last])
            store_left(rows_ref, place, first, part)


def update_kernel(
    rows, cols, sent_ref, weights_ref, noise_ref, factor_left_ref, left_ref, left_half_ref, rows_ref, chosen_ref,
    chosen_half_ref, out_ref, block_ref, kern_ref, cols_ref, sems,
):
    row_place, col_place = lax.axis_index("row"), lax.axis_index("col")
    halves = cols // rows
    count = sent_ref.shape[0]
    part = col_place % halves
    own = row_place == col_place // halves
    panel = factor_left_ref.shape[0]

    high, low = halves_of(jnp.transpose(sent_ref[...] * scale_of(weights_ref)))
    right = pack_right(high, low)
    right_half = half_square(high, low, 0)
    chunks, chunk = block_ref.shape[:2]
    places = [slice(number * chunk, (number + 1) * chunk) for number in range(chunks)]
    noise = jnp.where(own, noise_ref[:, pl.ds(pl.multiple_of(part * count, count), count)], 0.0)
    ids = (chunk, count)
    below = lax.broadcasted_iota(jnp.int32, ids, 0) - lax.broadcasted_iota(jnp.int32, ids, 1)

    crossed = product(chosen_ref[...], right)
    tiles = [product(left_ref[place, :], right) for place in places]
    store_right(kern_ref, 0, kern(crossed, chosen_half_ref[...], right_half))
    for first in range(0, panel, block):
        last = first + block
        store_right(cols_ref, first, product(factor_left_ref[first:last, : 3 * last], kern_ref[: 3 * last, :]))
    for number, place in enumerate(places):
        tile = kern(tiles[number], left_half_ref[place, :], right_half)
        block_ref[number] = tile + jnp.where(below == part * count - number * chunk, noise, 0.0)

    copies = []
    for number, place in enumerate(places):
        block_ref[number] = block_ref[number] - product(rows_ref[place, :], cols_ref[...])
        copy = pltpu.make_async_copy(block_ref.at[number], out_ref.at[pl.ds(number * chunk, chunk)], sems.at[number])
        copy.start()
        copies.append(copy)
    for copy in copies:
        copy.wait()


def shape(dims, kind=f32):
    return jax.ShapeDtypeStruct(dims, kind)


def compute_params(flops, moved):
    return dict(
        compiler_params=pltpu.CompilerParams(vmem_limit_bytes=vmem_bytes),
        cost_estimate=pl.CostEstimate(flops=flops, bytes_accessed=moved, transcendentals=0),
    )


def links_of(place, group, target_row, across):
    links = []
    step = 1 if target_row > group else -1
    links += [(0, place, z, step) for z in range(group, target_row, step)]
    (x, y), (end_x, end_y) = (place % across, place // across), (group % across, group // across)
    step = 1 if end_x > x else -1
    links += [(1, target_row, y, at, step) for at in range(x, end_x, step)]
    step = 1 if end_y > y else -1
    links += [(2, target_row, end_x, at, step) for at in range(y, end_y, step)]
    return links


def source_places(rows, halves):
    draw = random.Random(5)
    across = math.isqrt(rows)
    places = {}
    load = collections.Counter()

    def move(key, r, sign):
        change = 0
        for link in links_of(places[key][r], key[1], r, across):
            old = load[link]
            load[link] = old + sign
            change += (old + sign) ** 4 - old**4
        return change

    for h in range(halves):
        for g in range(rows):
            places[h, g] = draw.sample(range(rows), rows)
            for r in range(rows):
                move((h, g), r, 1)
    best, total, kept = 0, 0, {key: list(value) for key, value in places.items()}
    tries = 20000
    for number in range(tries):
        key = draw.randrange(halves), draw.randrange(rows)
        one, two = draw.sample(range(rows), 2)
        own = places[key]
        change = move(key, one, -1) + move(key, two, -1)
        own[one], own[two] = own[two], own[one]
        change += move(key, one, 1) + move(key, two, 1)
        heat = 30.0 * (1 - number / tries) + 0.01
        if change <= 0 or draw.random() < math.exp(-change / heat):
            total += change
            if total < best:
                best, kept = total, {key: list(value) for key, value in places.items()}
        else:
            move(key, one, -1), move(key, two, -1)
            own[one], own[two] = own[two], own[one]
            move(key, one, 1), move(key, two, 1)
    return kept


def column_pairs(rows, cols):
    halves = cols // rows
    places = source_places(rows, halves)
    return [
        (g * cols + places[h, g][r] * halves + h, r * cols + g * halves + h)
        for h in range(halves)
        for g in range(rows)
        for r in range(rows)
    ]


def swap(value, bit, cols):
    return lax.ppermute(value, "col", [(i, i ^ bit) for i in range(cols)])


def gather_panel(panel_pool, own_points, panel_block, cols):
    col_place = lax.axis_index("col")
    core = col_place % 2
    half_rows = panel_pool.shape[0] // 2
    mine = lax.dynamic_slice_in_dim(panel_pool, core * half_rows, half_rows, 0)
    others = lax.dynamic_slice_in_dim(panel_pool, (1 - core) * half_rows, half_rows, 0)
    got, mine, own_points = lax.optimization_barrier((swap(others, 1, cols), mine, own_points))
    held = jnp.where(panel_block % 2 == core, mine, got)
    apart = panel_block ^ col_place
    low = 2
    while low < cols:
        high = min(4 * low, cols)
        away = apart & (high - low)
        received = [swap(held, bits, cols) for bits in range(low, high, low)]
        for bits, value in zip(range(low, high, low), received):
            held = jnp.where(away == bits, value, held)
        low = high
    return [held, swap(held, 1, cols)], own_points


def on_device(points, panel_pool, order, panel_index, inv_factor, ard_weights, noise):
    row_count, features = points.shape
    panel = inv_factor.shape[0]
    rows = lax.axis_size("row")
    cols = lax.axis_size("col")
    col_count = row_count * rows // cols
    halves = cols // rows
    col_place = lax.axis_index("col")
    own_points = lax.dynamic_slice_in_dim(points, col_place % halves * col_count, col_count, 0)
    pieces, own_points = gather_panel(panel_pool, own_points, panel_index[0], cols)
    sent = lax.ppermute(own_points, ("row", "col"), column_pairs(rows, cols))
    weights = ard_weights[None, :]

    packed = 4 * features
    factor_left, factor_right, pick, left, left_half = pl.pallas_call(
        parts_kernel,
        out_shape=[
            shape((panel, 3 * panel), bf16),
            shape((3 * panel, panel), bf16),
            shape((panel, panel), bf16),
            shape((row_count, packed), bf16),
            shape((row_count, 1)),
        ],
        **compute_params(10**8, 4 * 10**6),
    )(inv_factor, order[None, :], points, weights)

    rows_left, chosen, chosen_half = pl.pallas_call(
        rows_kernel,
        out_shape=[shape((row_count, 3 * panel), bf16), shape((panel, packed), bf16), shape((panel, 1))],
        scratch_shapes=[pltpu.VMEM((row_count, 3 * panel), bf16)],
        **compute_params(1, 1),
    )(*pieces, weights, factor_right, pick, left, left_half)

    chunks = 2
    return pl.pallas_call(
        functools.partial(update_kernel, rows, cols),
        out_shape=shape((row_count, col_count)),
        out_specs=pl.BlockSpec(memory_space=pl.ANY),
        scratch_shapes=[
            pltpu.VMEM((chunks, row_count // chunks, col_count), f32),
            pltpu.VMEM((3 * panel, col_count), bf16),
            pltpu.VMEM((3 * panel, col_count), bf16),
            pltpu.SemaphoreType.DMA((chunks,)),
        ],
        **compute_params(4 * 10**9, 8 * 10**6),
    )(sent, weights, noise[None, :], factor_left, left, left_half, rows_left, chosen, chosen_half)


def solution(mesh):
    in_specs = (P("row", None), P("col", None), P(), P(), P(), P(), P("row"))
    out_specs = P("row", "col")
    return jax.shard_map(
        on_device, mesh=mesh, in_specs=in_specs, out_specs=out_specs, check_vma=False
    )
```

```python
import collections
import functools
import math
import random

import jax
import jax.numpy as jnp
from jax import lax
from jax.experimental import pallas as pl
from jax.experimental.pallas import tpu as pltpu
from jax.sharding import PartitionSpec as P

log2_e = 1.4426950408889634
vmem_bytes = 32 * 1024 * 1024
f32, bf16 = jnp.float32, jnp.bfloat16
block = 256


def halves_of(value):
    high = value.astype(bf16)
    low = (value - high.astype(f32)).astype(bf16)
    return high, low


def pack_left(high, low):
    return jnp.concatenate([high, low, high, low], axis=1)


def pack_right(high, low):
    return jnp.concatenate([high, low, low, high], axis=0)


def half_square(high, low, axis):
    value = high.astype(f32) + low.astype(f32)
    return 0.5 * jnp.sum(value * value, axis=axis, keepdims=True)


def product(left, right):
    return lax.dot_general(left, right, (((1,), (0,)), ((), ())), preferred_element_type=f32)


def store_left(ref, rows, first, value):
    high, low = halves_of(value)
    for start in range(0, value.shape[1], block):
        now, at = slice(start, start + block), 3 * (first + start)
        ref[rows, at : at + block] = high[:, now]
        ref[rows, at + block : at + 2 * block] = high[:, now]
        ref[rows, at + 2 * block : at + 3 * block] = low[:, now]


def store_right(ref, first, value):
    high, low = halves_of(value)
    for start in range(0, value.shape[0], block):
        now, at = slice(start, start + block), 3 * (first + start)
        ref[at : at + block, :] = high[now]
        ref[at + block : at + 2 * block, :] = low[now]
        ref[at + 2 * block : at + 3 * block, :] = high[now]


def kern(crossed, left_half, right_half):
    return jnp.exp2((crossed - left_half) - (right_half - 1.0))


def scale_of(weights_ref):
    return jnp.sqrt(weights_ref[...] * log2_e)


def parts_kernel(
    factor_ref, order_ref, points_ref, weights_ref, factor_left_ref, factor_right_ref, pick_ref, left_ref,
    left_half_ref,
):
    factor = factor_ref[...]
    store_left(factor_left_ref, slice(None), 0, factor)
    store_right(factor_right_ref, 0, jnp.transpose(factor))
    panel = factor.shape[0]
    core = lax.axis_index("col") % 2
    place = lax.broadcasted_iota(jnp.int32, (panel, panel), 0) + core * (panel // 2)
    place = jnp.where(place >= panel, place - panel, place)
    hit = jnp.where(place == order_ref[...], 1.0, 0.0).astype(f32)
    pick_ref[...] = jnp.transpose(hit).astype(bf16)
    high, low = halves_of(points_ref[...] * scale_of(weights_ref))
    left_ref[...] = pack_left(high, low)
    left_half_ref[...] = half_square(high, low, 1)


def rows_kernel(
    own_ref, other_ref, weights_ref, factor_right_ref, pick_ref, left_ref, left_half_ref,
    rows_ref, chosen_ref, chosen_half_ref, kern_ref,
):
    panel = pick_ref.shape[0]
    features = own_ref.shape[1]
    held = jnp.concatenate([own_ref[...], other_ref[...]], axis=0) * scale_of(weights_ref)
    chosen = product(pick_ref[...], jnp.concatenate(halves_of(held), axis=1))
    high, low = chosen[:, :features].astype(bf16), chosen[:, features:].astype(bf16)
    chosen_ref[...] = pack_left(high, low)
    chosen_half_ref[...] = half_square(high, low, 1)
    turned = jnp.transpose(chosen)
    high, low = turned[:features].astype(bf16), turned[features:].astype(bf16)
    right = pack_right(high, low)
    right_half = half_square(high, low, 0)
    chunks = 2
    count = left_ref.shape[0] // chunks
    places = [slice(number * count, (number + 1) * count) for number in range(chunks)]
    crossed = [product(left_ref[place, :], right) for place in places]
    for number, place in enumerate(places):
        store_left(kern_ref, place, 0, kern(crossed[number], left_half_ref[place, :], right_half))
        for first in range(0, panel, block):
            last = first + block
            part = product(kern_ref[place, : 3 * last], factor_right_ref[: 3 * last, first:last])
            store_left(rows_ref, place, first, part)


def update_kernel(
    rows, cols, sent_ref, weights_ref, noise_ref, factor_left_ref, left_ref, left_half_ref, rows_ref, chosen_ref,
    chosen_half_ref, out_ref, block_ref, kern_ref, cols_ref, sems,
):
    row_place, col_place = lax.axis_index("row"), lax.axis_index("col")
    halves = cols // rows
    count = sent_ref.shape[0]
    part = col_place % halves
    own = row_place == col_place // halves
    panel = factor_left_ref.shape[0]

    high, low = halves_of(jnp.transpose(sent_ref[...] * scale_of(weights_ref)))
    right = pack_right(high, low)
    right_half = half_square(high, low, 0)
    chunks, chunk = block_ref.shape[:2]
    places = [slice(number * chunk, (number + 1) * chunk) for number in range(chunks)]
    noise = jnp.where(own, noise_ref[:, pl.ds(pl.multiple_of(part * count, count), count)], 0.0)
    ids = (chunk, count)
    below = lax.broadcasted_iota(jnp.int32, ids, 0) - lax.broadcasted_iota(jnp.int32, ids, 1)

    crossed = product(chosen_ref[...], right)
    tiles = [product(left_ref[place, :], right) for place in places]
    store_right(kern_ref, 0, kern(crossed, chosen_half_ref[...], right_half))
    for first in range(0, panel, block):
        last = first + block
        store_right(cols_ref, first, product(factor_left_ref[first:last, : 3 * last], kern_ref[: 3 * last, :]))
    for number, place in enumerate(places):
        tile = kern(tiles[number], left_half_ref[place, :], right_half)
        block_ref[number] = tile + jnp.where(below == part * count - number * chunk, noise, 0.0)

    copies = []
    for number, place in enumerate(places):
        block_ref[number] = block_ref[number] - product(rows_ref[place, :], cols_ref[...])
        copy = pltpu.make_async_copy(block_ref.at[number], out_ref.at[pl.ds(number * chunk, chunk)], sems.at[number])
        copy.start()
        copies.append(copy)
    for copy in copies:
        copy.wait()


def shape(dims, kind=f32):
    return jax.ShapeDtypeStruct(dims, kind)


def compute_params(flops, moved):
    return dict(
        compiler_params=pltpu.CompilerParams(vmem_limit_bytes=vmem_bytes),
        cost_estimate=pl.CostEstimate(flops=flops, bytes_accessed=moved, transcendentals=0),
    )


def links_of(place, group, target_row, across):
    links = []
    step = 1 if target_row > group else -1
    links += [(0, place, z, step) for z in range(group, target_row, step)]
    (x, y), (end_x, end_y) = (place % across, place // across), (group % across, group // across)
    step = 1 if end_x > x else -1
    links += [(1, target_row, y, at, step) for at in range(x, end_x, step)]
    step = 1 if end_y > y else -1
    links += [(2, target_row, end_x, at, step) for at in range(y, end_y, step)]
    return links


def source_places(rows, halves):
    draw = random.Random(5)
    across = math.isqrt(rows)
    places = {}
    load = collections.Counter()

    def move(key, r, sign):
        change = 0
        for link in links_of(places[key][r], key[1], r, across):
            old = load[link]
            load[link] = old + sign
            change += (old + sign) ** 4 - old**4
        return change

    for h in range(halves):
        for g in range(rows):
            places[h, g] = draw.sample(range(rows), rows)
            for r in range(rows):
                move((h, g), r, 1)
    best, total, kept = 0, 0, {key: list(value) for key, value in places.items()}
    tries = 20000
    for number in range(tries):
        key = draw.randrange(halves), draw.randrange(rows)
        one, two = draw.sample(range(rows), 2)
        own = places[key]
        change = move(key, one, -1) + move(key, two, -1)
        own[one], own[two] = own[two], own[one]
        change += move(key, one, 1) + move(key, two, 1)
        heat = 30.0 * (1 - number / tries) + 0.01
        if change <= 0 or draw.random() < math.exp(-change / heat):
            total += change
            if total < best:
                best, kept = total, {key: list(value) for key, value in places.items()}
        else:
            move(key, one, -1), move(key, two, -1)
            own[one], own[two] = own[two], own[one]
            move(key, one, 1), move(key, two, 1)
    return kept


def column_pairs(rows, cols):
    halves = cols // rows
    places = source_places(rows, halves)
    return [
        (g * cols + places[h, g][r] * halves + h, r * cols + g * halves + h)
        for h in range(halves)
        for g in range(rows)
        for r in range(rows)
    ]


def swap(value, bit, cols):
    return lax.ppermute(value, "col", [(i, i ^ bit) for i in range(cols)])


def gather_panel(panel_pool, panel_block, cols):
    col_place = lax.axis_index("col")
    core = col_place % 2
    half_rows = panel_pool.shape[0] // 2
    others = lax.dynamic_slice_in_dim(panel_pool, (1 - core) * half_rows, half_rows, 0)
    mine = lax.dynamic_slice_in_dim(panel_pool, core * half_rows, half_rows, 0)
    got, mine = lax.optimization_barrier((swap(others, 1, cols), mine))
    held = jnp.where(panel_block % 2 == core, mine, got)
    apart = panel_block ^ col_place
    low = 2
    while low < cols:
        high = min(4 * low, cols)
        away = apart & (high - low)
        received = [swap(held, bits, cols) for bits in range(low, high, low)]
        for bits, value in zip(range(low, high, low), received):
            held = jnp.where(away == bits, value, held)
        low = high
    return [held, swap(held, 1, cols)]


def on_device(points, panel_pool, order, panel_index, inv_factor, ard_weights, noise):
    row_count, features = points.shape
    panel = inv_factor.shape[0]
    rows = lax.axis_size("row")
    cols = lax.axis_size("col")
    col_count = row_count * rows // cols
    halves = cols // rows
    col_place = lax.axis_index("col")
    own_half = lax.dynamic_slice_in_dim(points, col_place % halves * col_count, col_count, 0)
    sent = lax.ppermute(own_half, ("row", "col"), column_pairs(rows, cols))
    pieces = gather_panel(panel_pool, panel_index[0], cols)
    weights = ard_weights[None, :]

    packed = 4 * features
    factor_left, factor_right, pick, left, left_half = pl.pallas_call(
        parts_kernel,
        out_shape=[
            shape((panel, 3 * panel), bf16),
            shape((3 * panel, panel), bf16),
            shape((panel, panel), bf16),
            shape((row_count, packed), bf16),
            shape((row_count, 1)),
        ],
        **compute_params(10**8, 4 * 10**6),
    )(inv_factor, order[None, :], points, weights)

    rows_left, chosen, chosen_half = pl.pallas_call(
        rows_kernel,
        out_shape=[shape((row_count, 3 * panel), bf16), shape((panel, packed), bf16), shape((panel, 1))],
        scratch_shapes=[pltpu.VMEM((row_count, 3 * panel), bf16)],
        **compute_params(1, 1),
    )(*pieces, weights, factor_right, pick, left, left_half)

    chunks = 4
    return pl.pallas_call(
        functools.partial(update_kernel, rows, cols),
        out_shape=shape((row_count, col_count)),
        out_specs=pl.BlockSpec(memory_space=pl.ANY),
        scratch_shapes=[
            pltpu.VMEM((chunks, row_count // chunks, col_count), f32),
            pltpu.VMEM((3 * panel, col_count), bf16),
            pltpu.VMEM((3 * panel, col_count), bf16),
            pltpu.SemaphoreType.DMA((chunks,)),
        ],
        **compute_params(4 * 10**9, 8 * 10**6),
    )(sent, weights, noise[None, :], factor_left, left, left_half, rows_left, chosen, chosen_half)


def solution(mesh):
    in_specs = (P("row", None), P("col", None), P(), P(), P(), P(), P("row"))
    out_specs = P("row", "col")
    return jax.shard_map(
        on_device, mesh=mesh, in_specs=in_specs, out_specs=out_specs, check_vma=False
    )
```

```python
import collections
import functools
import math
import random

import jax
import jax.numpy as jnp
from jax import lax
from jax.experimental import pallas as pl
from jax.experimental.pallas import tpu as pltpu
from jax.sharding import PartitionSpec as P

log2_e = 1.4426950408889634
vmem_bytes = 32 * 1024 * 1024
f32, bf16 = jnp.float32, jnp.bfloat16
block = 256


def halves_of(value):
    high = value.astype(bf16)
    low = (value - high.astype(f32)).astype(bf16)
    return high, low


def pack_left(high, low):
    return jnp.concatenate([high, low, high, low], axis=1)


def pack_right(high, low):
    return jnp.concatenate([high, low, low, high], axis=0)


def half_square(high, low, axis):
    value = high.astype(f32) + low.astype(f32)
    return 0.5 * jnp.sum(value * value, axis=axis, keepdims=True)


def product(left, right):
    return lax.dot_general(left, right, (((1,), (0,)), ((), ())), preferred_element_type=f32)


def store_left(ref, rows, first, value):
    high, low = halves_of(value)
    for start in range(0, value.shape[1], block):
        now, at = slice(start, start + block), 3 * (first + start)
        ref[rows, at : at + block] = high[:, now]
        ref[rows, at + block : at + 2 * block] = high[:, now]
        ref[rows, at + 2 * block : at + 3 * block] = low[:, now]


def store_right(ref, first, value):
    high, low = halves_of(value)
    for start in range(0, value.shape[0], block):
        now, at = slice(start, start + block), 3 * (first + start)
        ref[at : at + block, :] = high[now]
        ref[at + block : at + 2 * block, :] = low[now]
        ref[at + 2 * block : at + 3 * block, :] = high[now]


def kern(crossed, left_half, right_half):
    return jnp.exp2((crossed - left_half) - (right_half - 1.0))


def scale_of(weights_ref):
    return jnp.sqrt(weights_ref[...] * log2_e)


def parts_kernel(
    factor_ref, order_ref, points_ref, weights_ref, factor_left_ref, factor_right_ref, pick_ref, left_ref,
    left_half_ref,
):
    factor = factor_ref[...]
    store_left(factor_left_ref, slice(None), 0, factor)
    store_right(factor_right_ref, 0, jnp.transpose(factor))
    panel = factor.shape[0]
    core = lax.axis_index("col") % 2
    place = lax.broadcasted_iota(jnp.int32, (panel, panel), 0) + core * (panel // 2)
    place = jnp.where(place >= panel, place - panel, place)
    hit = jnp.where(place == order_ref[...], 1.0, 0.0).astype(f32)
    pick_ref[...] = jnp.transpose(hit).astype(bf16)
    high, low = halves_of(points_ref[...] * scale_of(weights_ref))
    left_ref[...] = pack_left(high, low)
    left_half_ref[...] = half_square(high, low, 1)


def rows_kernel(
    own_ref, other_ref, weights_ref, factor_right_ref, pick_ref, left_ref, left_half_ref,
    rows_ref, chosen_ref, chosen_half_ref, kern_ref,
):
    panel = pick_ref.shape[0]
    features = own_ref.shape[1]
    held = jnp.concatenate([own_ref[...], other_ref[...]], axis=0) * scale_of(weights_ref)
    chosen = product(pick_ref[...], jnp.concatenate(halves_of(held), axis=1))
    high, low = chosen[:, :features].astype(bf16), chosen[:, features:].astype(bf16)
    chosen_ref[...] = pack_left(high, low)
    chosen_half_ref[...] = half_square(high, low, 1)
    turned = jnp.transpose(chosen)
    high, low = turned[:features].astype(bf16), turned[features:].astype(bf16)
    right = pack_right(high, low)
    right_half = half_square(high, low, 0)
    chunks = 2
    count = left_ref.shape[0] // chunks
    places = [slice(number * count, (number + 1) * count) for number in range(chunks)]
    crossed = [product(left_ref[place, :], right) for place in places]
    for number, place in enumerate(places):
        store_left(kern_ref, place, 0, kern(crossed[number], left_half_ref[place, :], right_half))
        for first in range(0, panel, block):
            last = first + block
            part = product(kern_ref[place, : 3 * last], factor_right_ref[: 3 * last, first:last])
            store_left(rows_ref, place, first, part)


def update_kernel(
    rows, cols, sent_ref, weights_ref, noise_ref, factor_left_ref, left_ref, left_half_ref, rows_ref, chosen_ref,
    chosen_half_ref, out_ref, block_ref, kern_ref, cols_ref, sems,
):
    row_place, col_place = lax.axis_index("row"), lax.axis_index("col")
    halves = cols // rows
    count = sent_ref.shape[0]
    part = col_place % halves
    own = row_place == col_place // halves
    panel = factor_left_ref.shape[0]

    high, low = halves_of(jnp.transpose(sent_ref[...] * scale_of(weights_ref)))
    right = pack_right(high, low)
    right_half = half_square(high, low, 0)
    chunks, chunk = block_ref.shape[:2]
    places = [slice(number * chunk, (number + 1) * chunk) for number in range(chunks)]
    noise = jnp.where(own, noise_ref[:, pl.ds(pl.multiple_of(part * count, count), count)], 0.0)
    ids = (chunk, count)
    below = lax.broadcasted_iota(jnp.int32, ids, 0) - lax.broadcasted_iota(jnp.int32, ids, 1)

    crossed = product(chosen_ref[...], right)
    tiles = [product(left_ref[place, :], right) for place in places]
    store_right(kern_ref, 0, kern(crossed, chosen_half_ref[...], right_half))
    for first in range(0, panel, block):
        last = first + block
        store_right(cols_ref, first, product(factor_left_ref[first:last, : 3 * last], kern_ref[: 3 * last, :]))
    for number, place in enumerate(places):
        tile = kern(tiles[number], left_half_ref[place, :], right_half)
        block_ref[number] = tile + jnp.where(below == part * count - number * chunk, noise, 0.0)

    copies = []
    for number, place in enumerate(places):
        block_ref[number] = block_ref[number] - product(rows_ref[place, :], cols_ref[...])
        copy = pltpu.make_async_copy(block_ref.at[number], out_ref.at[pl.ds(number * chunk, chunk)], sems.at[number])
        copy.start()
        copies.append(copy)
    for copy in copies:
        copy.wait()


def shape(dims, kind=f32):
    return jax.ShapeDtypeStruct(dims, kind)


def compute_params(flops, moved):
    return dict(
        compiler_params=pltpu.CompilerParams(vmem_limit_bytes=vmem_bytes),
        cost_estimate=pl.CostEstimate(flops=flops, bytes_accessed=moved, transcendentals=0),
    )


def links_of(place, group, target_row, across):
    links = []
    step = 1 if target_row > group else -1
    links += [(0, place, z, step) for z in range(group, target_row, step)]
    (x, y), (end_x, end_y) = (place % across, place // across), (group % across, group // across)
    step = 1 if end_x > x else -1
    links += [(1, target_row, y, at, step) for at in range(x, end_x, step)]
    step = 1 if end_y > y else -1
    links += [(2, target_row, end_x, at, step) for at in range(y, end_y, step)]
    return links


def source_places(rows, halves):
    draw = random.Random(5)
    across = math.isqrt(rows)
    places = {}
    load = collections.Counter()

    def move(key, r, sign):
        change = 0
        for link in links_of(places[key][r], key[1], r, across):
            old = load[link]
            load[link] = old + sign
            change += (old + sign) ** 4 - old**4
        return change

    for h in range(halves):
        for g in range(rows):
            places[h, g] = draw.sample(range(rows), rows)
            for r in range(rows):
                move((h, g), r, 1)
    best, total, kept = 0, 0, {key: list(value) for key, value in places.items()}
    tries = 20000
    for number in range(tries):
        key = draw.randrange(halves), draw.randrange(rows)
        one, two = draw.sample(range(rows), 2)
        own = places[key]
        change = move(key, one, -1) + move(key, two, -1)
        own[one], own[two] = own[two], own[one]
        change += move(key, one, 1) + move(key, two, 1)
        heat = 30.0 * (1 - number / tries) + 0.01
        if change <= 0 or draw.random() < math.exp(-change / heat):
            total += change
            if total < best:
                best, kept = total, {key: list(value) for key, value in places.items()}
        else:
            move(key, one, -1), move(key, two, -1)
            own[one], own[two] = own[two], own[one]
            move(key, one, 1), move(key, two, 1)
    return kept


def column_pairs(rows, cols):
    halves = cols // rows
    places = source_places(rows, halves)
    return [
        (g * cols + places[h, g][r] * halves + h, r * cols + g * halves + h)
        for h in range(halves)
        for g in range(rows)
        for r in range(rows)
    ]


def swap(value, bit, cols):
    return lax.ppermute(value, "col", [(i, i ^ bit) for i in range(cols)])


def gather_panel(panel_pool, own_points, panel_block, cols):
    col_place = lax.axis_index("col")
    core = col_place % 2
    half_rows = panel_pool.shape[0] // 2
    mine = lax.dynamic_slice_in_dim(panel_pool, core * half_rows, half_rows, 0)
    others = lax.dynamic_slice_in_dim(panel_pool, (1 - core) * half_rows, half_rows, 0)
    got, mine, own_points = lax.optimization_barrier((swap(others, 1, cols), mine, own_points))
    held = jnp.where(panel_block % 2 == core, mine, got)
    apart = panel_block ^ col_place
    low = 2
    while low < cols:
        high = min(4 * low, cols)
        away = apart & (high - low)
        steps = range(high - low, 0, -low)
        received = [swap(held, bits, cols) for bits in steps]
        for bits, value in zip(steps, received):
            held = jnp.where(away == bits, value, held)
        low = high
    return [held, swap(held, 1, cols)], own_points


def on_device(points, panel_pool, order, panel_index, inv_factor, ard_weights, noise):
    row_count, features = points.shape
    panel = inv_factor.shape[0]
    rows = lax.axis_size("row")
    cols = lax.axis_size("col")
    col_count = row_count * rows // cols
    halves = cols // rows
    col_place = lax.axis_index("col")
    own_points = lax.dynamic_slice_in_dim(points, col_place % halves * col_count, col_count, 0)
    pieces, own_points = gather_panel(panel_pool, own_points, panel_index[0], cols)
    sent = lax.ppermute(own_points, ("row", "col"), column_pairs(rows, cols))
    weights = ard_weights[None, :]

    packed = 4 * features
    factor_left, factor_right, pick, left, left_half = pl.pallas_call(
        parts_kernel,
        out_shape=[
            shape((panel, 3 * panel), bf16),
            shape((3 * panel, panel), bf16),
            shape((panel, panel), bf16),
            shape((row_count, packed), bf16),
            shape((row_count, 1)),
        ],
        **compute_params(10**8, 4 * 10**6),
    )(inv_factor, order[None, :], points, weights)

    rows_left, chosen, chosen_half = pl.pallas_call(
        rows_kernel,
        out_shape=[shape((row_count, 3 * panel), bf16), shape((panel, packed), bf16), shape((panel, 1))],
        scratch_shapes=[pltpu.VMEM((row_count, 3 * panel), bf16)],
        **compute_params(1, 1),
    )(*pieces, weights, factor_right, pick, left, left_half)

    chunks = 4
    return pl.pallas_call(
        functools.partial(update_kernel, rows, cols),
        out_shape=shape((row_count, col_count)),
        out_specs=pl.BlockSpec(memory_space=pl.ANY),
        scratch_shapes=[
            pltpu.VMEM((chunks, row_count // chunks, col_count), f32),
            pltpu.VMEM((3 * panel, col_count), bf16),
            pltpu.VMEM((3 * panel, col_count), bf16),
            pltpu.SemaphoreType.DMA((chunks,)),
        ],
        **compute_params(4 * 10**9, 8 * 10**6),
    )(sent, weights, noise[None, :], factor_left, left, left_half, rows_left, chosen, chosen_half)


def solution(mesh):
    in_specs = (P("row", None), P("col", None), P(), P(), P(), P(), P("row"))
    out_specs = P("row", "col")
    return jax.shard_map(
        on_device, mesh=mesh, in_specs=in_specs, out_specs=out_specs, check_vma=False
    )
```

```python
import collections
import functools
import math
import random

import jax
import jax.numpy as jnp
from jax import lax
from jax.experimental import pallas as pl
from jax.experimental.pallas import tpu as pltpu
from jax.sharding import PartitionSpec as P

log2_e = 1.4426950408889634
vmem_bytes = 32 * 1024 * 1024
f32, bf16 = jnp.float32, jnp.bfloat16
block = 256


def halves_of(value):
    high = value.astype(bf16)
    low = (value - high.astype(f32)).astype(bf16)
    return high, low


def pack_left(high, low):
    return jnp.concatenate([high, low, high, low], axis=1)


def pack_right(high, low):
    return jnp.concatenate([high, low, low, high], axis=0)


def half_square(high, low, axis):
    value = high.astype(f32) + low.astype(f32)
    return 0.5 * jnp.sum(value * value, axis=axis, keepdims=True)


def product(left, right):
    return lax.dot_general(left, right, (((1,), (0,)), ((), ())), preferred_element_type=f32)


def store_left(ref, rows, first, value):
    high, low = halves_of(value)
    for start in range(0, value.shape[1], block):
        now, at = slice(start, start + block), 3 * (first + start)
        ref[rows, at : at + block] = high[:, now]
        ref[rows, at + block : at + 2 * block] = high[:, now]
        ref[rows, at + 2 * block : at + 3 * block] = low[:, now]


def store_right(ref, first, value):
    high, low = halves_of(value)
    for start in range(0, value.shape[0], block):
        now, at = slice(start, start + block), 3 * (first + start)
        ref[at : at + block, :] = high[now]
        ref[at + block : at + 2 * block, :] = low[now]
        ref[at + 2 * block : at + 3 * block, :] = high[now]


def kern(crossed, left_half, right_half):
    return jnp.exp2((crossed - left_half) - (right_half - 1.0))


def scale_of(weights_ref):
    return jnp.sqrt(weights_ref[...] * log2_e)


def parts_kernel(
    factor_ref, order_ref, points_ref, weights_ref, factor_left_ref, factor_right_ref, pick_ref, left_ref,
    left_half_ref,
):
    factor = factor_ref[...]
    store_left(factor_left_ref, slice(None), 0, factor)
    store_right(factor_right_ref, 0, jnp.transpose(factor))
    panel = factor.shape[0]
    core = lax.axis_index("col") % 2
    place = lax.broadcasted_iota(jnp.int32, (panel, panel), 0) + core * (panel // 2)
    place = jnp.where(place >= panel, place - panel, place)
    hit = jnp.where(place == order_ref[...], 1.0, 0.0).astype(f32)
    pick_ref[...] = jnp.transpose(hit).astype(bf16)
    high, low = halves_of(points_ref[...] * scale_of(weights_ref))
    left_ref[...] = pack_left(high, low)
    left_half_ref[...] = half_square(high, low, 1)


def rows_kernel(
    own_ref, other_ref, weights_ref, factor_right_ref, pick_ref, left_ref, left_half_ref,
    rows_ref, chosen_ref, chosen_half_ref, kern_ref,
):
    panel = pick_ref.shape[0]
    features = own_ref.shape[1]
    held = jnp.concatenate([own_ref[...], other_ref[...]], axis=0) * scale_of(weights_ref)
    chosen = product(pick_ref[...], jnp.concatenate(halves_of(held), axis=1))
    high, low = chosen[:, :features].astype(bf16), chosen[:, features:].astype(bf16)
    chosen_ref[...] = pack_left(high, low)
    chosen_half_ref[...] = half_square(high, low, 1)
    turned = jnp.transpose(chosen)
    high, low = turned[:features].astype(bf16), turned[features:].astype(bf16)
    right = pack_right(high, low)
    right_half = half_square(high, low, 0)
    chunks = 2
    count = left_ref.shape[0] // chunks
    places = [slice(number * count, (number + 1) * count) for number in range(chunks)]
    crossed = [product(left_ref[place, :], right) for place in places]
    for number, place in enumerate(places):
        store_left(kern_ref, place, 0, kern(crossed[number], left_half_ref[place, :], right_half))
        for first in range(0, panel, block):
            last = first + block
            part = product(kern_ref[place, : 3 * last], factor_right_ref[: 3 * last, first:last])
            store_left(rows_ref, place, first, part)


def update_kernel(
    rows, cols, sent_ref, weights_ref, noise_ref, factor_left_ref, left_ref, left_half_ref, rows_ref, chosen_ref,
    chosen_half_ref, out_ref, block_ref, kern_ref, cols_ref, sems,
):
    row_place, col_place = lax.axis_index("row"), lax.axis_index("col")
    halves = cols // rows
    count = sent_ref.shape[0]
    part = col_place % halves
    own = row_place == col_place // halves
    panel = factor_left_ref.shape[0]

    high, low = halves_of(jnp.transpose(sent_ref[...] * scale_of(weights_ref)))
    right = pack_right(high, low)
    right_half = half_square(high, low, 0)
    chunks, chunk = block_ref.shape[:2]
    places = [slice(number * chunk, (number + 1) * chunk) for number in range(chunks)]
    noise = jnp.where(own, noise_ref[:, pl.ds(pl.multiple_of(part * count, count), count)], 0.0)
    ids = (chunk, count)
    below = lax.broadcasted_iota(jnp.int32, ids, 0) - lax.broadcasted_iota(jnp.int32, ids, 1)

    crossed = product(chosen_ref[...], right)
    tiles = [product(left_ref[place, :], right) for place in places]
    store_right(kern_ref, 0, kern(crossed, chosen_half_ref[...], right_half))
    for first in range(0, panel, block):
        last = first + block
        store_right(cols_ref, first, product(factor_left_ref[first:last, : 3 * last], kern_ref[: 3 * last, :]))
    for number, place in enumerate(places):
        tile = kern(tiles[number], left_half_ref[place, :], right_half)
        block_ref[number] = tile + jnp.where(below == part * count - number * chunk, noise, 0.0)

    copies = []
    for number, place in enumerate(places):
        block_ref[number] = block_ref[number] - product(rows_ref[place, :], cols_ref[...])
        copy = pltpu.make_async_copy(block_ref.at[number], out_ref.at[pl.ds(number * chunk, chunk)], sems.at[number])
        copy.start()
        copies.append(copy)
    for copy in copies:
        copy.wait()


def shape(dims, kind=f32):
    return jax.ShapeDtypeStruct(dims, kind)


def compute_params(flops, moved):
    return dict(
        compiler_params=pltpu.CompilerParams(vmem_limit_bytes=vmem_bytes),
        cost_estimate=pl.CostEstimate(flops=flops, bytes_accessed=moved, transcendentals=0),
    )


def links_of(place, group, target_row, across):
    links = []
    step = 1 if target_row > group else -1
    links += [(0, place, z, step) for z in range(group, target_row, step)]
    (x, y), (end_x, end_y) = (place % across, place // across), (group % across, group // across)
    step = 1 if end_x > x else -1
    links += [(1, target_row, y, at, step) for at in range(x, end_x, step)]
    step = 1 if end_y > y else -1
    links += [(2, target_row, end_x, at, step) for at in range(y, end_y, step)]
    return links


def source_places(rows, halves):
    draw = random.Random(5)
    across = math.isqrt(rows)
    places = {}
    load = collections.Counter()

    def move(key, r, sign):
        change = 0
        for link in links_of(places[key][r], key[1], r, across):
            old = load[link]
            load[link] = old + sign
            change += (old + sign) ** 4 - old**4
        return change

    for h in range(halves):
        for g in range(rows):
            places[h, g] = draw.sample(range(rows), rows)
            for r in range(rows):
                move((h, g), r, 1)
    best, total, kept = 0, 0, {key: list(value) for key, value in places.items()}
    tries = 20000
    for number in range(tries):
        key = draw.randrange(halves), draw.randrange(rows)
        one, two = draw.sample(range(rows), 2)
        own = places[key]
        change = move(key, one, -1) + move(key, two, -1)
        own[one], own[two] = own[two], own[one]
        change += move(key, one, 1) + move(key, two, 1)
        heat = 30.0 * (1 - number / tries) + 0.01
        if change <= 0 or draw.random() < math.exp(-change / heat):
            total += change
            if total < best:
                best, kept = total, {key: list(value) for key, value in places.items()}
        else:
            move(key, one, -1), move(key, two, -1)
            own[one], own[two] = own[two], own[one]
            move(key, one, 1), move(key, two, 1)
    return kept


def column_pairs(rows, cols):
    halves = cols // rows
    places = source_places(rows, halves)
    return [
        (g * cols + places[h, g][r] * halves + h, r * cols + g * halves + h)
        for h in range(halves)
        for g in range(rows)
        for r in range(rows)
    ]


def swap(value, bit, cols):
    return lax.ppermute(value, "col", [(i, i ^ bit) for i in range(cols)])


def gather_panel(panel_pool, own_points, panel_block, cols):
    col_place = lax.axis_index("col")
    core = col_place % 2
    half_rows = panel_pool.shape[0] // 2
    mine = lax.dynamic_slice_in_dim(panel_pool, core * half_rows, half_rows, 0)
    others = lax.dynamic_slice_in_dim(panel_pool, (1 - core) * half_rows, half_rows, 0)
    got, mine, own_points = lax.optimization_barrier((swap(others, 1, cols), mine, own_points))
    held = jnp.where(panel_block % 2 == core, mine, got)
    apart = panel_block ^ col_place
    bits = [2**k for k in range(1, cols.bit_length() - 1)]
    turn = len(bits) // 2
    for bit, other_bit in zip(bits, bits[turn:] + bits[:turn]):
        pairs = [(i, i ^ (other_bit if i % 2 else bit)) for i in range(cols)]
        got = lax.ppermute(held, "col", pairs)
        held = jnp.where(apart & jnp.where(core == 0, bit, other_bit) == 0, held, got)
    return [held, swap(held, 1, cols)], own_points


def on_device(points, panel_pool, order, panel_index, inv_factor, ard_weights, noise):
    row_count, features = points.shape
    panel = inv_factor.shape[0]
    rows = lax.axis_size("row")
    cols = lax.axis_size("col")
    col_count = row_count * rows // cols
    halves = cols // rows
    col_place = lax.axis_index("col")
    own_points = lax.dynamic_slice_in_dim(points, col_place % halves * col_count, col_count, 0)
    pieces, own_points = gather_panel(panel_pool, own_points, panel_index[0], cols)
    sent = lax.ppermute(own_points, ("row", "col"), column_pairs(rows, cols))
    weights = ard_weights[None, :]

    packed = 4 * features
    factor_left, factor_right, pick, left, left_half = pl.pallas_call(
        parts_kernel,
        out_shape=[
            shape((panel, 3 * panel), bf16),
            shape((3 * panel, panel), bf16),
            shape((panel, panel), bf16),
            shape((row_count, packed), bf16),
            shape((row_count, 1)),
        ],
        **compute_params(10**8, 4 * 10**6),
    )(inv_factor, order[None, :], points, weights)

    rows_left, chosen, chosen_half = pl.pallas_call(
        rows_kernel,
        out_shape=[shape((row_count, 3 * panel), bf16), shape((panel, packed), bf16), shape((panel, 1))],
        scratch_shapes=[pltpu.VMEM((row_count, 3 * panel), bf16)],
        **compute_params(1, 1),
    )(*pieces, weights, factor_right, pick, left, left_half)

    chunks = 4
    return pl.pallas_call(
        functools.partial(update_kernel, rows, cols),
        out_shape=shape((row_count, col_count)),
        out_specs=pl.BlockSpec(memory_space=pl.ANY),
        scratch_shapes=[
            pltpu.VMEM((chunks, row_count // chunks, col_count), f32),
            pltpu.VMEM((3 * panel, col_count), bf16),
            pltpu.VMEM((3 * panel, col_count), bf16),
            pltpu.SemaphoreType.DMA((chunks,)),
        ],
        **compute_params(4 * 10**9, 8 * 10**6),
    )(sent, weights, noise[None, :], factor_left, left, left_half, rows_left, chosen, chosen_half)


def solution(mesh):
    in_specs = (P("row", None), P("col", None), P(), P(), P(), P(), P("row"))
    out_specs = P("row", "col")
    return jax.shard_map(
        on_device, mesh=mesh, in_specs=in_specs, out_specs=out_specs, check_vma=False
    )
```

```python
import collections
import functools
import math
import random

import jax
import jax.numpy as jnp
from jax import lax
from jax.experimental import pallas as pl
from jax.experimental.pallas import tpu as pltpu
from jax.sharding import PartitionSpec as P

log2_e = 1.4426950408889634
vmem_bytes = 32 * 1024 * 1024
f32, bf16 = jnp.float32, jnp.bfloat16
block = 256


def halves_of(value):
    high = value.astype(bf16)
    low = (value - high.astype(f32)).astype(bf16)
    return high, low


def pack_left(high, low):
    return jnp.concatenate([high, low, high, low], axis=1)


def pack_right(high, low):
    return jnp.concatenate([high, low, low, high], axis=0)


def half_square(high, low, axis):
    value = high.astype(f32) + low.astype(f32)
    return 0.5 * jnp.sum(value * value, axis=axis, keepdims=True)


def product(left, right):
    return lax.dot_general(left, right, (((1,), (0,)), ((), ())), preferred_element_type=f32)


def store_left(ref, rows, first, value):
    high, low = halves_of(value)
    for start in range(0, value.shape[1], block):
        now, at = slice(start, start + block), 3 * (first + start)
        ref[rows, at : at + block] = high[:, now]
        ref[rows, at + block : at + 2 * block] = high[:, now]
        ref[rows, at + 2 * block : at + 3 * block] = low[:, now]


def store_right(ref, first, value):
    high, low = halves_of(value)
    for start in range(0, value.shape[0], block):
        now, at = slice(start, start + block), 3 * (first + start)
        ref[at : at + block, :] = high[now]
        ref[at + block : at + 2 * block, :] = low[now]
        ref[at + 2 * block : at + 3 * block, :] = high[now]


def kern(crossed, left_half, right_half):
    return jnp.exp2((crossed - left_half) - (right_half - 1.0))


def scale_of(vectors_ref, panel, features):
    return jnp.sqrt(vectors_ref[:, panel : panel + features] * log2_e)


def parts_kernel(
    factor_ref, points_ref, vectors_ref, factor_left_ref, factor_right_ref, pick_ref, left_ref,
    left_half_ref,
):
    factor = factor_ref[...]
    store_left(factor_left_ref, slice(None), 0, factor)
    store_right(factor_right_ref, 0, jnp.transpose(factor))
    panel = factor.shape[0]
    core = lax.axis_index("col") % 2
    place = lax.broadcasted_iota(jnp.int32, (panel, panel), 0) + core * (panel // 2)
    place = jnp.where(place >= panel, place - panel, place).astype(f32)
    hit = jnp.where(place == vectors_ref[:, :panel], 1.0, 0.0).astype(f32)
    pick_ref[...] = jnp.transpose(hit).astype(bf16)
    high, low = halves_of(points_ref[...] * scale_of(vectors_ref, panel, points_ref.shape[1]))
    left_ref[...] = pack_left(high, low)
    left_half_ref[...] = half_square(high, low, 1)


def rows_kernel(
    own_ref, other_ref, vectors_ref, factor_right_ref, pick_ref, left_ref, left_half_ref,
    rows_ref, chosen_ref, chosen_half_ref, kern_ref,
):
    panel = pick_ref.shape[0]
    features = own_ref.shape[1]
    held = jnp.concatenate([own_ref[...], other_ref[...]], axis=0) * scale_of(vectors_ref, panel, features)
    chosen = product(pick_ref[...], jnp.concatenate(halves_of(held), axis=1))
    high, low = chosen[:, :features].astype(bf16), chosen[:, features:].astype(bf16)
    chosen_ref[...] = pack_left(high, low)
    chosen_half_ref[...] = half_square(high, low, 1)
    turned = jnp.transpose(chosen)
    high, low = turned[:features].astype(bf16), turned[features:].astype(bf16)
    right = pack_right(high, low)
    right_half = half_square(high, low, 0)
    chunks = 2
    count = left_ref.shape[0] // chunks
    places = [slice(number * count, (number + 1) * count) for number in range(chunks)]
    crossed = [product(left_ref[place, :], right) for place in places]
    for number, place in enumerate(places):
        store_left(kern_ref, place, 0, kern(crossed[number], left_half_ref[place, :], right_half))
        for first in range(0, panel, block):
            last = first + block
            part = product(kern_ref[place, : 3 * last], factor_right_ref[: 3 * last, first:last])
            store_left(rows_ref, place, first, part)


def update_kernel(
    rows, cols, sent_ref, vectors_ref, factor_left_ref, left_ref, left_half_ref, rows_ref, chosen_ref,
    chosen_half_ref, out_ref, block_ref, kern_ref, cols_ref, sems,
):
    row_place, col_place = lax.axis_index("row"), lax.axis_index("col")
    halves = cols // rows
    count = sent_ref.shape[0]
    part = col_place % halves
    own = row_place == col_place // halves
    panel, features = factor_left_ref.shape[0], sent_ref.shape[1]

    high, low = halves_of(jnp.transpose(sent_ref[...] * scale_of(vectors_ref, panel, features)))
    right = pack_right(high, low)
    right_half = half_square(high, low, 0)
    chunks, chunk = block_ref.shape[:2]
    places = [slice(number * chunk, (number + 1) * chunk) for number in range(chunks)]
    at = pl.multiple_of(panel + features + part * count, 128)
    noise = jnp.where(own, vectors_ref[:, pl.ds(at, count)], 0.0)
    ids = (chunk, count)
    below = lax.broadcasted_iota(jnp.int32, ids, 0) - lax.broadcasted_iota(jnp.int32, ids, 1)

    crossed = product(chosen_ref[...], right)
    tiles = [product(left_ref[place, :], right) for place in places]
    store_right(kern_ref, 0, kern(crossed, chosen_half_ref[...], right_half))
    for first in range(0, panel, block):
        last = first + block
        store_right(cols_ref, first, product(factor_left_ref[first:last, : 3 * last], kern_ref[: 3 * last, :]))
    for number, place in enumerate(places):
        tile = kern(tiles[number], left_half_ref[place, :], right_half)
        block_ref[number] = tile + jnp.where(below == part * count - number * chunk, noise, 0.0)

    copies = []
    for number, place in enumerate(places):
        block_ref[number] = block_ref[number] - product(rows_ref[place, :], cols_ref[...])
        copy = pltpu.make_async_copy(block_ref.at[number], out_ref.at[pl.ds(number * chunk, chunk)], sems.at[number])
        copy.start()
        copies.append(copy)
    for copy in copies:
        copy.wait()


def shape(dims, kind=f32):
    return jax.ShapeDtypeStruct(dims, kind)


def compute_params(flops, moved):
    return dict(
        compiler_params=pltpu.CompilerParams(vmem_limit_bytes=vmem_bytes),
        cost_estimate=pl.CostEstimate(flops=flops, bytes_accessed=moved, transcendentals=0),
    )


def links_of(place, group, target_row, across):
    links = []
    step = 1 if target_row > group else -1
    links += [(0, place, z, step) for z in range(group, target_row, step)]
    (x, y), (end_x, end_y) = (place % across, place // across), (group % across, group // across)
    step = 1 if end_x > x else -1
    links += [(1, target_row, y, at, step) for at in range(x, end_x, step)]
    step = 1 if end_y > y else -1
    links += [(2, target_row, end_x, at, step) for at in range(y, end_y, step)]
    return links


def source_places(rows, halves):
    draw = random.Random(5)
    across = math.isqrt(rows)
    places = {}
    load = collections.Counter()

    def move(key, r, sign):
        change = 0
        for link in links_of(places[key][r], key[1], r, across):
            old = load[link]
            load[link] = old + sign
            change += (old + sign) ** 4 - old**4
        return change

    for h in range(halves):
        for g in range(rows):
            places[h, g] = draw.sample(range(rows), rows)
            for r in range(rows):
                move((h, g), r, 1)
    best, total, kept = 0, 0, {key: list(value) for key, value in places.items()}
    tries = 20000
    for number in range(tries):
        key = draw.randrange(halves), draw.randrange(rows)
        one, two = draw.sample(range(rows), 2)
        own = places[key]
        change = move(key, one, -1) + move(key, two, -1)
        own[one], own[two] = own[two], own[one]
        change += move(key, one, 1) + move(key, two, 1)
        heat = 30.0 * (1 - number / tries) + 0.01
        if change <= 0 or draw.random() < math.exp(-change / heat):
            total += change
            if total < best:
                best, kept = total, {key: list(value) for key, value in places.items()}
        else:
            move(key, one, -1), move(key, two, -1)
            own[one], own[two] = own[two], own[one]
            move(key, one, 1), move(key, two, 1)
    return kept


def column_pairs(rows, cols):
    halves = cols // rows
    places = source_places(rows, halves)
    return [
        (g * cols + places[h, g][r] * halves + h, r * cols + g * halves + h)
        for h in range(halves)
        for g in range(rows)
        for r in range(rows)
    ]


def swap(value, bit, cols):
    return lax.ppermute(value, "col", [(i, i ^ bit) for i in range(cols)])


def gather_panel(panel_pool, panel_block, cols, beside):
    col_place = lax.axis_index("col")
    core = col_place % 2
    half_rows = panel_pool.shape[0] // 2
    mine = lax.dynamic_slice_in_dim(panel_pool, core * half_rows, half_rows, 0)
    got, mine, beside = lax.optimization_barrier((swap(panel_pool, 1, cols), mine, beside))
    got = lax.dynamic_slice_in_dim(got, core * half_rows, half_rows, 0)
    held = jnp.where(panel_block % 2 == core, mine, got)
    apart = panel_block ^ col_place
    low = 2
    while low < cols:
        high = min(4 * low, cols)
        away = apart & (high - low)
        received = [swap(held, bits, cols) for bits in range(low, high, low)]
        for bits, value in zip(range(low, high, low), received):
            held = jnp.where(away == bits, value, held)
        low = high
    return [held, swap(held, 1, cols)], beside


def on_device(points, panel_pool, order, panel_index, inv_factor, ard_weights, noise):
    row_count, features = points.shape
    panel = inv_factor.shape[0]
    rows = lax.axis_size("row")
    cols = lax.axis_size("col")
    col_count = row_count * rows // cols
    halves = cols // rows
    col_place = lax.axis_index("col")
    own_half = lax.dynamic_slice_in_dim(points, col_place % halves * col_count, col_count, 0)
    sent = lax.ppermute(own_half, ("row", "col"), column_pairs(rows, cols))
    vectors = jnp.concatenate([order.astype(f32), ard_weights, noise])[None, :]
    pieces, vectors = gather_panel(panel_pool, panel_index[0], cols, vectors)

    packed = 4 * features
    factor_left, factor_right, pick, left, left_half = pl.pallas_call(
        parts_kernel,
        out_shape=[
            shape((panel, 3 * panel), bf16),
            shape((3 * panel, panel), bf16),
            shape((panel, panel), bf16),
            shape((row_count, packed), bf16),
            shape((row_count, 1)),
        ],
        **compute_params(10**8, 4 * 10**6),
    )(inv_factor, points, vectors)

    rows_left, chosen, chosen_half = pl.pallas_call(
        rows_kernel,
        out_shape=[shape((row_count, 3 * panel), bf16), shape((panel, packed), bf16), shape((panel, 1))],
        scratch_shapes=[pltpu.VMEM((row_count, 3 * panel), bf16)],
        **compute_params(1, 1),
    )(*pieces, vectors, factor_right, pick, left, left_half)

    chunks = 4
    return pl.pallas_call(
        functools.partial(update_kernel, rows, cols),
        out_shape=shape((row_count, col_count)),
        out_specs=pl.BlockSpec(memory_space=pl.ANY),
        scratch_shapes=[
            pltpu.VMEM((chunks, row_count // chunks, col_count), f32),
            pltpu.VMEM((3 * panel, col_count), bf16),
            pltpu.VMEM((3 * panel, col_count), bf16),
            pltpu.SemaphoreType.DMA((chunks,)),
        ],
        **compute_params(4 * 10**9, 8 * 10**6),
    )(sent, vectors, factor_left, left, left_half, rows_left, chosen, chosen_half)


def solution(mesh):
    in_specs = (P("row", None), P("col", None), P(), P(), P(), P(), P("row"))
    out_specs = P("row", "col")
    return jax.shard_map(
        on_device, mesh=mesh, in_specs=in_specs, out_specs=out_specs, check_vma=False
    )
```

```python
import collections
import functools
import math
import random

import jax
import jax.numpy as jnp
from jax import lax
from jax.experimental import pallas as pl
from jax.experimental.pallas import tpu as pltpu
from jax.sharding import PartitionSpec as P

log2_e = 1.4426950408889634
vmem_bytes = 32 * 1024 * 1024
f32, bf16 = jnp.float32, jnp.bfloat16
block = 256


def halves_of(value):
    high = value.astype(bf16)
    low = (value - high.astype(f32)).astype(bf16)
    return high, low


def pack_left(high, low):
    return jnp.concatenate([high, low, high, low], axis=1)


def pack_right(high, low):
    return jnp.concatenate([high, low, low, high], axis=0)


def half_square(high, low, axis):
    value = high.astype(f32) + low.astype(f32)
    return 0.5 * jnp.sum(value * value, axis=axis, keepdims=True)


def product(left, right):
    return lax.dot_general(left, right, (((1,), (0,)), ((), ())), preferred_element_type=f32)


def store_left(ref, rows, first, value):
    high, low = halves_of(value)
    for start in range(0, value.shape[1], block):
        now, at = slice(start, start + block), 3 * (first + start)
        ref[rows, at : at + block] = high[:, now]
        ref[rows, at + block : at + 2 * block] = high[:, now]
        ref[rows, at + 2 * block : at + 3 * block] = low[:, now]


def store_right(ref, first, value):
    high, low = halves_of(value)
    for start in range(0, value.shape[0], block):
        now, at = slice(start, start + block), 3 * (first + start)
        ref[at : at + block, :] = high[now]
        ref[at + block : at + 2 * block, :] = low[now]
        ref[at + 2 * block : at + 3 * block, :] = high[now]


def kern(crossed, left_half, right_half):
    return jnp.exp2((crossed - left_half) - (right_half - 1.0))


def scale_of(vectors_ref, panel, features):
    return jnp.sqrt(vectors_ref[:, panel : panel + features] * log2_e)


def parts_kernel(
    factor_ref, points_ref, vectors_ref, factor_left_ref, factor_right_ref, pick_ref, left_ref,
    left_half_ref,
):
    factor = factor_ref[...]
    store_left(factor_left_ref, slice(None), 0, factor)
    store_right(factor_right_ref, 0, jnp.transpose(factor))
    panel = factor.shape[0]
    core = lax.axis_index("col") % 2
    place = lax.broadcasted_iota(jnp.int32, (panel, panel), 0) + core * (panel // 2)
    place = jnp.where(place >= panel, place - panel, place).astype(f32)
    hit = jnp.where(place == vectors_ref[:, :panel], 1.0, 0.0).astype(f32)
    pick_ref[...] = jnp.transpose(hit).astype(bf16)
    high, low = halves_of(points_ref[...] * scale_of(vectors_ref, panel, points_ref.shape[1]))
    left_ref[...] = pack_left(high, low)
    left_half_ref[...] = half_square(high, low, 1)


def rows_kernel(
    own_ref, other_ref, vectors_ref, factor_right_ref, pick_ref, left_ref, left_half_ref,
    rows_ref, chosen_ref, chosen_half_ref, kern_ref,
):
    panel = pick_ref.shape[0]
    features = own_ref.shape[1]
    held = jnp.concatenate([own_ref[...], other_ref[...]], axis=0) * scale_of(vectors_ref, panel, features)
    chosen = product(pick_ref[...], jnp.concatenate(halves_of(held), axis=1))
    high, low = chosen[:, :features].astype(bf16), chosen[:, features:].astype(bf16)
    chosen_ref[...] = pack_left(high, low)
    chosen_half_ref[...] = half_square(high, low, 1)
    turned = jnp.transpose(chosen)
    high, low = turned[:features].astype(bf16), turned[features:].astype(bf16)
    right = pack_right(high, low)
    right_half = half_square(high, low, 0)
    chunks = 2
    count = left_ref.shape[0] // chunks
    places = [slice(number * count, (number + 1) * count) for number in range(chunks)]
    crossed = [product(left_ref[place, :], right) for place in places]
    for number, place in enumerate(places):
        store_left(kern_ref, place, 0, kern(crossed[number], left_half_ref[place, :], right_half))
        for first in range(0, panel, block):
            last = first + block
            part = product(kern_ref[place, : 3 * last], factor_right_ref[: 3 * last, first:last])
            store_left(rows_ref, place, first, part)


def update_kernel(
    rows, cols, sent_ref, vectors_ref, factor_left_ref, left_ref, left_half_ref, rows_ref, chosen_ref,
    chosen_half_ref, out_ref, block_ref, kern_ref, cols_ref, sems,
):
    row_place, col_place = lax.axis_index("row"), lax.axis_index("col")
    halves = cols // rows
    count = sent_ref.shape[0]
    part = col_place % halves
    own = row_place == col_place // halves
    panel, features = factor_left_ref.shape[0], sent_ref.shape[1]

    high, low = halves_of(jnp.transpose(sent_ref[...] * scale_of(vectors_ref, panel, features)))
    right = pack_right(high, low)
    right_half = half_square(high, low, 0)
    chunks, chunk = block_ref.shape[:2]
    places = [slice(number * chunk, (number + 1) * chunk) for number in range(chunks)]
    at = pl.multiple_of(panel + features + part * count, 128)
    noise = jnp.where(own, vectors_ref[:, pl.ds(at, count)], 0.0)
    ids = (chunk, count)
    below = lax.broadcasted_iota(jnp.int32, ids, 0) - lax.broadcasted_iota(jnp.int32, ids, 1)

    crossed = product(chosen_ref[...], right)
    tiles = [product(left_ref[place, :], right) for place in places]
    store_right(kern_ref, 0, kern(crossed, chosen_half_ref[...], right_half))
    for first in range(0, panel, block):
        last = first + block
        store_right(cols_ref, first, product(factor_left_ref[first:last, : 3 * last], kern_ref[: 3 * last, :]))
    for number, place in enumerate(places):
        tile = kern(tiles[number], left_half_ref[place, :], right_half)
        block_ref[number] = tile + jnp.where(below == part * count - number * chunk, noise, 0.0)

    copies = []
    for number, place in enumerate(places):
        block_ref[number] = block_ref[number] - product(rows_ref[place, :], cols_ref[...])
        copy = pltpu.make_async_copy(block_ref.at[number], out_ref.at[pl.ds(number * chunk, chunk)], sems.at[number])
        copy.start()
        copies.append(copy)
    for copy in copies:
        copy.wait()


def shape(dims, kind=f32):
    return jax.ShapeDtypeStruct(dims, kind)


def compute_params(flops, moved):
    return dict(
        compiler_params=pltpu.CompilerParams(vmem_limit_bytes=vmem_bytes),
        cost_estimate=pl.CostEstimate(flops=flops, bytes_accessed=moved, transcendentals=0),
    )


def links_of(place, group, target_row, across):
    links = []
    step = 1 if target_row > group else -1
    links += [(0, place, z, step) for z in range(group, target_row, step)]
    (x, y), (end_x, end_y) = (place % across, place // across), (group % across, group // across)
    step = 1 if end_x > x else -1
    links += [(1, target_row, y, at, step) for at in range(x, end_x, step)]
    step = 1 if end_y > y else -1
    links += [(2, target_row, end_x, at, step) for at in range(y, end_y, step)]
    return links


def source_places(rows, halves):
    draw = random.Random(5)
    across = math.isqrt(rows)
    places = {}
    load = collections.Counter()

    def move(key, r, sign):
        change = 0
        for link in links_of(places[key][r], key[1], r, across):
            old = load[link]
            load[link] = old + sign
            change += (old + sign) ** 4 - old**4
        return change

    for h in range(halves):
        for g in range(rows):
            places[h, g] = draw.sample(range(rows), rows)
            for r in range(rows):
                move((h, g), r, 1)
    best, total, kept = 0, 0, {key: list(value) for key, value in places.items()}
    tries = 20000
    for number in range(tries):
        key = draw.randrange(halves), draw.randrange(rows)
        one, two = draw.sample(range(rows), 2)
        own = places[key]
        change = move(key, one, -1) + move(key, two, -1)
        own[one], own[two] = own[two], own[one]
        change += move(key, one, 1) + move(key, two, 1)
        heat = 30.0 * (1 - number / tries) + 0.01
        if change <= 0 or draw.random() < math.exp(-change / heat):
            total += change
            if total < best:
                best, kept = total, {key: list(value) for key, value in places.items()}
        else:
            move(key, one, -1), move(key, two, -1)
            own[one], own[two] = own[two], own[one]
            move(key, one, 1), move(key, two, 1)
    return kept


def column_pairs(rows, cols):
    halves = cols // rows
    places = source_places(rows, halves)
    return [
        (g * cols + places[h, g][r] * halves + h, r * cols + g * halves + h)
        for h in range(halves)
        for g in range(rows)
        for r in range(rows)
    ]


def swap(value, bit, cols):
    return lax.ppermute(value, "col", [(i, i ^ bit) for i in range(cols)])


def gather_panel(panel_pool, panel_block, cols, beside):
    col_place = lax.axis_index("col")
    core = col_place % 2
    half_rows = panel_pool.shape[0] // 2
    mine = lax.dynamic_slice_in_dim(panel_pool, core * half_rows, half_rows, 0)
    got, mine = lax.optimization_barrier((swap(panel_pool, 1, cols), mine))
    got = lax.dynamic_slice_in_dim(got, core * half_rows, half_rows, 0)
    held = jnp.where(panel_block % 2 == core, mine, got)
    apart = panel_block ^ col_place
    low = 2
    while low < cols:
        high = min(4 * low, cols)
        away = apart & (high - low)
        steps = range(high - low, 0, -low)
        received = [swap(held, bits, cols) for bits in steps]
        received, beside = lax.optimization_barrier((received, beside))
        for bits, value in zip(steps, received):
            held = jnp.where(away == bits, value, held)
        low = high
    return [held, swap(held, 1, cols)], beside


def on_device(points, panel_pool, order, panel_index, inv_factor, ard_weights, noise):
    row_count, features = points.shape
    panel = inv_factor.shape[0]
    rows = lax.axis_size("row")
    cols = lax.axis_size("col")
    col_count = row_count * rows // cols
    halves = cols // rows
    col_place = lax.axis_index("col")
    own_half = lax.dynamic_slice_in_dim(points, col_place % halves * col_count, col_count, 0)
    sent = lax.ppermute(own_half, ("row", "col"), column_pairs(rows, cols))
    vectors = jnp.concatenate([order.astype(f32), ard_weights, noise])[None, :]
    pieces, vectors = gather_panel(panel_pool, panel_index[0], cols, vectors)

    packed = 4 * features
    factor_left, factor_right, pick, left, left_half = pl.pallas_call(
        parts_kernel,
        out_shape=[
            shape((panel, 3 * panel), bf16),
            shape((3 * panel, panel), bf16),
            shape((panel, panel), bf16),
            shape((row_count, packed), bf16),
            shape((row_count, 1)),
        ],
        **compute_params(10**8, 4 * 10**6),
    )(inv_factor, points, vectors)

    rows_left, chosen, chosen_half = pl.pallas_call(
        rows_kernel,
        out_shape=[shape((row_count, 3 * panel), bf16), shape((panel, packed), bf16), shape((panel, 1))],
        scratch_shapes=[pltpu.VMEM((row_count, 3 * panel), bf16)],
        **compute_params(1, 1),
    )(*pieces, vectors, factor_right, pick, left, left_half)

    chunks = 4
    return pl.pallas_call(
        functools.partial(update_kernel, rows, cols),
        out_shape=shape((row_count, col_count)),
        out_specs=pl.BlockSpec(memory_space=pl.ANY),
        scratch_shapes=[
            pltpu.VMEM((chunks, row_count // chunks, col_count), f32),
            pltpu.VMEM((3 * panel, col_count), bf16),
            pltpu.VMEM((3 * panel, col_count), bf16),
            pltpu.SemaphoreType.DMA((chunks,)),
        ],
        **compute_params(4 * 10**9, 8 * 10**6),
    )(sent, vectors, factor_left, left, left_half, rows_left, chosen, chosen_half)


def solution(mesh):
    in_specs = (P("row", None), P("col", None), P(), P(), P(), P(), P("row"))
    out_specs = P("row", "col")
    return jax.shard_map(
        on_device, mesh=mesh, in_specs=in_specs, out_specs=out_specs, check_vma=False
    )
```

```python
import collections
import functools
import math
import random

import jax
import jax.numpy as jnp
from jax import lax
from jax.experimental import pallas as pl
from jax.experimental.pallas import tpu as pltpu
from jax.sharding import PartitionSpec as P

log2_e = 1.4426950408889634
vmem_bytes = 32 * 1024 * 1024
f32, bf16 = jnp.float32, jnp.bfloat16
block = 256


def halves_of(value):
    high = value.astype(bf16)
    low = (value - high.astype(f32)).astype(bf16)
    return high, low


def pack_left(high, low):
    return jnp.concatenate([high, low, high, low], axis=1)


def pack_right(high, low):
    return jnp.concatenate([high, low, low, high], axis=0)


def half_square(high, low, axis):
    value = high.astype(f32) + low.astype(f32)
    return 0.5 * jnp.sum(value * value, axis=axis, keepdims=True)


def product(left, right):
    return lax.dot_general(left, right, (((1,), (0,)), ((), ())), preferred_element_type=f32)


def store_left(ref, rows, first, value):
    high, low = halves_of(value)
    for start in range(0, value.shape[1], block):
        now, at = slice(start, start + block), 3 * (first + start)
        ref[rows, at : at + block] = high[:, now]
        ref[rows, at + block : at + 2 * block] = high[:, now]
        ref[rows, at + 2 * block : at + 3 * block] = low[:, now]


def store_right(ref, first, value):
    high, low = halves_of(value)
    for start in range(0, value.shape[0], block):
        now, at = slice(start, start + block), 3 * (first + start)
        ref[at : at + block, :] = high[now]
        ref[at + block : at + 2 * block, :] = low[now]
        ref[at + 2 * block : at + 3 * block, :] = high[now]


def kern(crossed, left_half, right_half):
    return jnp.exp2((crossed - left_half) - (right_half - 1.0))


def scale_of(vectors_ref, panel, features):
    return jnp.sqrt(vectors_ref[:, panel : panel + features] * log2_e)


def parts_kernel(
    factor_ref, points_ref, vectors_ref, factor_left_ref, factor_right_ref, pick_ref, left_ref,
    left_half_ref,
):
    factor = factor_ref[...]
    store_left(factor_left_ref, slice(None), 0, factor)
    store_right(factor_right_ref, 0, jnp.transpose(factor))
    panel = factor.shape[0]
    core = lax.axis_index("col") % 2
    place = lax.broadcasted_iota(jnp.int32, (panel, panel), 0) + core * (panel // 2)
    place = jnp.where(place >= panel, place - panel, place).astype(f32)
    hit = jnp.where(place == vectors_ref[:, :panel], 1.0, 0.0).astype(f32)
    pick_ref[...] = jnp.transpose(hit).astype(bf16)
    high, low = halves_of(points_ref[...] * scale_of(vectors_ref, panel, points_ref.shape[1]))
    left_ref[...] = pack_left(high, low)
    left_half_ref[...] = half_square(high, low, 1)


def rows_kernel(
    own_ref, other_ref, vectors_ref, factor_right_ref, pick_ref, left_ref, left_half_ref,
    rows_ref, chosen_ref, chosen_half_ref, kern_ref,
):
    panel = pick_ref.shape[0]
    features = own_ref.shape[1]
    held = jnp.concatenate([own_ref[...], other_ref[...]], axis=0) * scale_of(vectors_ref, panel, features)
    chosen = product(pick_ref[...], jnp.concatenate(halves_of(held), axis=1))
    high, low = chosen[:, :features].astype(bf16), chosen[:, features:].astype(bf16)
    chosen_ref[...] = pack_left(high, low)
    chosen_half_ref[...] = half_square(high, low, 1)
    turned = jnp.transpose(chosen)
    high, low = turned[:features].astype(bf16), turned[features:].astype(bf16)
    right = pack_right(high, low)
    right_half = half_square(high, low, 0)
    chunks = 2
    count = left_ref.shape[0] // chunks
    places = [slice(number * count, (number + 1) * count) for number in range(chunks)]
    crossed = [product(left_ref[place, :], right) for place in places]
    for number, place in enumerate(places):
        store_left(kern_ref, place, 0, kern(crossed[number], left_half_ref[place, :], right_half))
        for first in range(0, panel, block):
            last = first + block
            part = product(kern_ref[place, : 3 * last], factor_right_ref[: 3 * last, first:last])
            store_left(rows_ref, place, first, part)


def update_kernel(
    rows, cols, sent_ref, vectors_ref, factor_left_ref, left_ref, left_half_ref, rows_ref, chosen_ref,
    chosen_half_ref, out_ref, block_ref, kern_ref, cols_ref, sems,
):
    row_place, col_place = lax.axis_index("row"), lax.axis_index("col")
    halves = cols // rows
    count = sent_ref.shape[0]
    part = col_place % halves
    own = row_place == col_place // halves
    panel, features = factor_left_ref.shape[0], sent_ref.shape[1]

    high, low = halves_of(jnp.transpose(sent_ref[...] * scale_of(vectors_ref, panel, features)))
    right = pack_right(high, low)
    right_half = half_square(high, low, 0)
    chunks, chunk = block_ref.shape[:2]
    places = [slice(number * chunk, (number + 1) * chunk) for number in range(chunks)]
    at = pl.multiple_of(panel + features + part * count, 128)
    noise = jnp.where(own, vectors_ref[:, pl.ds(at, count)], 0.0)
    ids = (chunk, count)
    below = lax.broadcasted_iota(jnp.int32, ids, 0) - lax.broadcasted_iota(jnp.int32, ids, 1)

    crossed = product(chosen_ref[...], right)
    tiles = [product(left_ref[place, :], right) for place in places]
    store_right(kern_ref, 0, kern(crossed, chosen_half_ref[...], right_half))
    for first in range(0, panel, block):
        last = first + block
        store_right(cols_ref, first, product(factor_left_ref[first:last, : 3 * last], kern_ref[: 3 * last, :]))
    for number, place in enumerate(places):
        tile = kern(tiles[number], left_half_ref[place, :], right_half)
        block_ref[number] = tile + jnp.where(below == part * count - number * chunk, noise, 0.0)

    copies = []
    for number, place in enumerate(places):
        block_ref[number] = block_ref[number] - product(rows_ref[place, :], cols_ref[...])
        copy = pltpu.make_async_copy(block_ref.at[number], out_ref.at[pl.ds(number * chunk, chunk)], sems.at[number])
        copy.start()
        copies.append(copy)
    for copy in copies:
        copy.wait()


def shape(dims, kind=f32):
    return jax.ShapeDtypeStruct(dims, kind)


def compute_params(flops, moved):
    return dict(
        compiler_params=pltpu.CompilerParams(vmem_limit_bytes=vmem_bytes),
        cost_estimate=pl.CostEstimate(flops=flops, bytes_accessed=moved, transcendentals=0),
    )


def links_of(place, group, target_row, across):
    links = []
    step = 1 if target_row > group else -1
    links += [(0, place, z, step) for z in range(group, target_row, step)]
    (x, y), (end_x, end_y) = (place % across, place // across), (group % across, group // across)
    step = 1 if end_x > x else -1
    links += [(1, target_row, y, at, step) for at in range(x, end_x, step)]
    step = 1 if end_y > y else -1
    links += [(2, target_row, end_x, at, step) for at in range(y, end_y, step)]
    return links


def source_places(rows, halves):
    draw = random.Random(5)
    across = math.isqrt(rows)
    places = {}
    load = collections.Counter()

    def move(key, r, sign):
        change = 0
        for link in links_of(places[key][r], key[1], r, across):
            old = load[link]
            load[link] = old + sign
            change += (old + sign) ** 4 - old**4
        return change

    for h in range(halves):
        for g in range(rows):
            places[h, g] = draw.sample(range(rows), rows)
            for r in range(rows):
                move((h, g), r, 1)
    best, total, kept = 0, 0, {key: list(value) for key, value in places.items()}
    tries = 20000
    for number in range(tries):
        key = draw.randrange(halves), draw.randrange(rows)
        one, two = draw.sample(range(rows), 2)
        own = places[key]
        change = move(key, one, -1) + move(key, two, -1)
        own[one], own[two] = own[two], own[one]
        change += move(key, one, 1) + move(key, two, 1)
        heat = 30.0 * (1 - number / tries) + 0.01
        if change <= 0 or draw.random() < math.exp(-change / heat):
            total += change
            if total < best:
                best, kept = total, {key: list(value) for key, value in places.items()}
        else:
            move(key, one, -1), move(key, two, -1)
            own[one], own[two] = own[two], own[one]
            move(key, one, 1), move(key, two, 1)
    return kept


def column_pairs(rows, cols):
    halves = cols // rows
    places = source_places(rows, halves)
    return [
        (g * cols + places[h, g][r] * halves + h, r * cols + g * halves + halves - 1 - h)
        for h in range(halves)
        for g in range(rows)
        for r in range(rows)
    ]


def swap(value, bit, cols):
    return lax.ppermute(value, "col", [(i, i ^ bit) for i in range(cols)])


def gather_panel(panel_pool, panel_block, cols, beside):
    col_place = lax.axis_index("col")
    core = col_place % 2
    half_rows = panel_pool.shape[0] // 2
    mine = lax.dynamic_slice_in_dim(panel_pool, core * half_rows, half_rows, 0)
    got, mine = lax.optimization_barrier((swap(panel_pool, 1, cols), mine))
    got = lax.dynamic_slice_in_dim(got, core * half_rows, half_rows, 0)
    held = jnp.where(panel_block % 2 == core, mine, got)
    apart = panel_block ^ col_place
    low = 2
    while low < cols:
        high = min(4 * low, cols)
        away = apart & (high - low)
        steps = range(high - low, 0, -low)
        received = [swap(held, bits, cols) for bits in steps]
        received, beside = lax.optimization_barrier((received, beside))
        for bits, value in zip(steps, received):
            held = jnp.where(away == bits, value, held)
        low = high
    return [held, swap(held, 1, cols)], beside


def on_device(points, panel_pool, order, panel_index, inv_factor, ard_weights, noise):
    row_count, features = points.shape
    panel = inv_factor.shape[0]
    rows = lax.axis_size("row")
    cols = lax.axis_size("col")
    col_count = row_count * rows // cols
    halves = cols // rows
    col_place = lax.axis_index("col")
    part = halves - 1 - col_place % halves
    own_half = lax.dynamic_slice_in_dim(points, part * col_count, col_count, 0)
    sent = lax.ppermute(own_half, ("row", "col"), column_pairs(rows, cols))
    vectors = jnp.concatenate([order.astype(f32), ard_weights, noise])[None, :]
    pieces, vectors = gather_panel(panel_pool, panel_index[0], cols, vectors)

    packed = 4 * features
    factor_left, factor_right, pick, left, left_half = pl.pallas_call(
        parts_kernel,
        out_shape=[
            shape((panel, 3 * panel), bf16),
            shape((3 * panel, panel), bf16),
            shape((panel, panel), bf16),
            shape((row_count, packed), bf16),
            shape((row_count, 1)),
        ],
        **compute_params(10**8, 4 * 10**6),
    )(inv_factor, points, vectors)

    rows_left, chosen, chosen_half = pl.pallas_call(
        rows_kernel,
        out_shape=[shape((row_count, 3 * panel), bf16), shape((panel, packed), bf16), shape((panel, 1))],
        scratch_shapes=[pltpu.VMEM((row_count, 3 * panel), bf16)],
        **compute_params(1, 1),
    )(*pieces, vectors, factor_right, pick, left, left_half)

    chunks = 4
    return pl.pallas_call(
        functools.partial(update_kernel, rows, cols),
        out_shape=shape((row_count, col_count)),
        out_specs=pl.BlockSpec(memory_space=pl.ANY),
        scratch_shapes=[
            pltpu.VMEM((chunks, row_count // chunks, col_count), f32),
            pltpu.VMEM((3 * panel, col_count), bf16),
            pltpu.VMEM((3 * panel, col_count), bf16),
            pltpu.SemaphoreType.DMA((chunks,)),
        ],
        **compute_params(4 * 10**9, 8 * 10**6),
    )(sent, vectors, factor_left, left, left_half, rows_left, chosen, chosen_half)


def solution(mesh):
    in_specs = (P("row", None), P("col", None), P(), P(), P(), P(), P("row"))
    out_specs = P("row", "col")
    return jax.shard_map(
        on_device, mesh=mesh, in_specs=in_specs, out_specs=out_specs, check_vma=False
    )
```

```python
import collections
import functools
import math
import random

import jax
import jax.numpy as jnp
from jax import lax
from jax.experimental import pallas as pl
from jax.experimental.pallas import tpu as pltpu
from jax.sharding import PartitionSpec as P

log2_e = 1.4426950408889634
vmem_bytes = 32 * 1024 * 1024
f32, bf16 = jnp.float32, jnp.bfloat16
block = 256


def halves_of(value):
    high = value.astype(bf16)
    low = (value - high.astype(f32)).astype(bf16)
    return high, low


def pack_left(high, low):
    return jnp.concatenate([high, low, high, low], axis=1)


def pack_right(high, low):
    return jnp.concatenate([high, low, low, high], axis=0)


def half_square(high, low, axis):
    value = high.astype(f32) + low.astype(f32)
    return 0.5 * jnp.sum(value * value, axis=axis, keepdims=True)


def product(left, right):
    return lax.dot_general(left, right, (((1,), (0,)), ((), ())), preferred_element_type=f32)


def store_left(ref, rows, first, value):
    high, low = halves_of(value)
    for start in range(0, value.shape[1], block):
        now, at = slice(start, start + block), 3 * (first + start)
        ref[rows, at : at + block] = high[:, now]
        ref[rows, at + block : at + 2 * block] = high[:, now]
        ref[rows, at + 2 * block : at + 3 * block] = low[:, now]


def store_right(ref, first, value):
    high, low = halves_of(value)
    for start in range(0, value.shape[0], block):
        now, at = slice(start, start + block), 3 * (first + start)
        ref[at : at + block, :] = high[now]
        ref[at + block : at + 2 * block, :] = low[now]
        ref[at + 2 * block : at + 3 * block, :] = high[now]


def kern(crossed, left_half, right_half):
    return jnp.exp2((crossed - left_half) - (right_half - 1.0))


def scale_of(vectors_ref, panel, features):
    return jnp.sqrt(vectors_ref[:, panel : panel + features] * log2_e)


def parts_kernel(
    factor_ref, points_ref, vectors_ref, factor_left_ref, factor_right_ref, pick_ref, left_ref,
    left_half_ref,
):
    factor = factor_ref[...]
    store_left(factor_left_ref, slice(None), 0, factor)
    store_right(factor_right_ref, 0, jnp.transpose(factor))
    panel = factor.shape[0]
    core = lax.axis_index("col") % 2
    place = lax.broadcasted_iota(jnp.int32, (panel, panel), 0) + core * (panel // 2)
    place = jnp.where(place >= panel, place - panel, place).astype(f32)
    hit = jnp.where(place == vectors_ref[:, :panel], 1.0, 0.0).astype(f32)
    pick_ref[...] = jnp.transpose(hit).astype(bf16)
    high, low = halves_of(points_ref[...] * scale_of(vectors_ref, panel, points_ref.shape[1]))
    left_ref[...] = pack_left(high, low)
    left_half_ref[...] = half_square(high, low, 1)


def rows_kernel(
    own_ref, other_ref, vectors_ref, factor_right_ref, pick_ref, left_ref, left_half_ref,
    rows_ref, chosen_ref, chosen_half_ref, kern_ref,
):
    panel = pick_ref.shape[0]
    features = own_ref.shape[1]
    held = jnp.concatenate([own_ref[...], other_ref[...]], axis=0) * scale_of(vectors_ref, panel, features)
    chosen = product(pick_ref[...], jnp.concatenate(halves_of(held), axis=1))
    high, low = chosen[:, :features].astype(bf16), chosen[:, features:].astype(bf16)
    chosen_ref[...] = pack_left(high, low)
    chosen_half_ref[...] = half_square(high, low, 1)
    turned = jnp.transpose(chosen)
    high, low = turned[:features].astype(bf16), turned[features:].astype(bf16)
    right = pack_right(high, low)
    right_half = half_square(high, low, 0)
    chunks = 2
    count = left_ref.shape[0] // chunks
    places = [slice(number * count, (number + 1) * count) for number in range(chunks)]
    crossed = [product(left_ref[place, :], right) for place in places]
    for number, place in enumerate(places):
        store_left(kern_ref, place, 0, kern(crossed[number], left_half_ref[place, :], right_half))
        for first in range(0, panel, block):
            last = first + block
            part = product(kern_ref[place, : 3 * last], factor_right_ref[: 3 * last, first:last])
            store_left(rows_ref, place, first, part)


def update_kernel(
    rows, cols, sent_ref, points_ref, vectors_ref, factor_left_ref, left_ref, left_half_ref, rows_ref, chosen_ref,
    chosen_half_ref, out_ref, block_ref, kern_ref, cols_ref, sems,
):
    row_place, col_place = lax.axis_index("row"), lax.axis_index("col")
    halves = cols // rows
    count = sent_ref.shape[0]
    part = col_place % halves
    own = row_place == col_place // halves
    panel, features = factor_left_ref.shape[0], sent_ref.shape[1]

    own_points = points_ref[pl.ds(pl.multiple_of(part * count, count), count), :]
    col_points = jnp.where(own, own_points, sent_ref[...])
    high, low = halves_of(jnp.transpose(col_points * scale_of(vectors_ref, panel, features)))
    right = pack_right(high, low)
    right_half = half_square(high, low, 0)
    chunks, chunk = block_ref.shape[:2]
    places = [slice(number * chunk, (number + 1) * chunk) for number in range(chunks)]
    at = pl.multiple_of(panel + features + part * count, 128)
    noise = jnp.where(own, vectors_ref[:, pl.ds(at, count)], 0.0)
    ids = (chunk, count)
    below = lax.broadcasted_iota(jnp.int32, ids, 0) - lax.broadcasted_iota(jnp.int32, ids, 1)

    crossed = product(chosen_ref[...], right)
    tiles = [product(left_ref[place, :], right) for place in places]
    store_right(kern_ref, 0, kern(crossed, chosen_half_ref[...], right_half))
    for first in range(0, panel, block):
        last = first + block
        store_right(cols_ref, first, product(factor_left_ref[first:last, : 3 * last], kern_ref[: 3 * last, :]))
    for number, place in enumerate(places):
        tile = kern(tiles[number], left_half_ref[place, :], right_half)
        block_ref[number] = tile + jnp.where(below == part * count - number * chunk, noise, 0.0)

    copies = []
    for number, place in enumerate(places):
        block_ref[number] = block_ref[number] - product(rows_ref[place, :], cols_ref[...])
        copy = pltpu.make_async_copy(block_ref.at[number], out_ref.at[pl.ds(number * chunk, chunk)], sems.at[number])
        copy.start()
        copies.append(copy)
    for copy in copies:
        copy.wait()


def shape(dims, kind=f32):
    return jax.ShapeDtypeStruct(dims, kind)


def compute_params(flops, moved):
    return dict(
        compiler_params=pltpu.CompilerParams(vmem_limit_bytes=vmem_bytes),
        cost_estimate=pl.CostEstimate(flops=flops, bytes_accessed=moved, transcendentals=0),
    )


def links_of(place, group, target_row, across):
    links = []
    step = 1 if target_row > group else -1
    links += [(0, place, z, step) for z in range(group, target_row, step)]
    (x, y), (end_x, end_y) = (place % across, place // across), (group % across, group // across)
    step = 1 if end_x > x else -1
    links += [(1, target_row, y, at, step) for at in range(x, end_x, step)]
    step = 1 if end_y > y else -1
    links += [(2, target_row, end_x, at, step) for at in range(y, end_y, step)]
    return links


def source_places(rows, halves):
    draw = random.Random(0)
    across = math.isqrt(rows)
    places = {}
    load = collections.Counter()

    def move(key, r, sign):
        change = 0
        if r == key[1]:
            return change
        for link in links_of(places[key][r], key[1], r, across):
            old = load[link]
            load[link] = old + sign
            change += (old + sign) ** 4 - old**4
        return change

    for h in range(halves):
        for g in range(rows):
            places[h, g] = draw.sample(range(rows), rows)
            for r in range(rows):
                move((h, g), r, 1)
    best, total, kept = 0, 0, {key: list(value) for key, value in places.items()}
    tries = 20000
    for number in range(tries):
        key = draw.randrange(halves), draw.randrange(rows)
        one, two = draw.sample(range(rows), 2)
        own = places[key]
        change = move(key, one, -1) + move(key, two, -1)
        own[one], own[two] = own[two], own[one]
        change += move(key, one, 1) + move(key, two, 1)
        heat = 30.0 * (1 - number / tries) + 0.01
        if change <= 0 or draw.random() < math.exp(-change / heat):
            total += change
            if total < best:
                best, kept = total, {key: list(value) for key, value in places.items()}
        else:
            move(key, one, -1), move(key, two, -1)
            own[one], own[two] = own[two], own[one]
            move(key, one, 1), move(key, two, 1)
    return kept


def column_pairs(rows, cols):
    halves = cols // rows
    places = source_places(rows, halves)
    return [
        (g * cols + places[h, g][r] * halves + h, r * cols + g * halves + halves - 1 - h)
        for h in range(halves)
        for g in range(rows)
        for r in range(rows)
        if r != g
    ]


def swap(value, bit, cols):
    return lax.ppermute(value, "col", [(i, i ^ bit) for i in range(cols)])


def gather_panel(panel_pool, panel_block, cols, beside):
    col_place = lax.axis_index("col")
    core = col_place % 2
    half_rows = panel_pool.shape[0] // 2
    mine = lax.dynamic_slice_in_dim(panel_pool, core * half_rows, half_rows, 0)
    got, mine = lax.optimization_barrier((swap(panel_pool, 1, cols), mine))
    got = lax.dynamic_slice_in_dim(got, core * half_rows, half_rows, 0)
    held = jnp.where(panel_block % 2 == core, mine, got)
    apart = panel_block ^ col_place
    low = 2
    while low < cols:
        high = min(4 * low, cols)
        away = apart & (high - low)
        steps = range(high - low, 0, -low)
        received = [swap(held, bits, cols) for bits in steps]
        received, beside = lax.optimization_barrier((received, beside))
        for bits, value in zip(steps, received):
            held = jnp.where(away == bits, value, held)
        low = high
    return [held, swap(held, 1, cols)], beside


def on_device(points, panel_pool, order, panel_index, inv_factor, ard_weights, noise):
    row_count, features = points.shape
    panel = inv_factor.shape[0]
    rows = lax.axis_size("row")
    cols = lax.axis_size("col")
    col_count = row_count * rows // cols
    halves = cols // rows
    col_place = lax.axis_index("col")
    part = halves - 1 - col_place % halves
    own_half = lax.dynamic_slice_in_dim(points, part * col_count, col_count, 0)
    sent = lax.ppermute(own_half, ("row", "col"), column_pairs(rows, cols))
    vectors = jnp.concatenate([order.astype(f32), ard_weights, noise])[None, :]
    pieces, vectors = gather_panel(panel_pool, panel_index[0], cols, vectors)

    packed = 4 * features
    factor_left, factor_right, pick, left, left_half = pl.pallas_call(
        parts_kernel,
        out_shape=[
            shape((panel, 3 * panel), bf16),
            shape((3 * panel, panel), bf16),
            shape((panel, panel), bf16),
            shape((row_count, packed), bf16),
            shape((row_count, 1)),
        ],
        **compute_params(10**8, 4 * 10**6),
    )(inv_factor, points, vectors)

    rows_left, chosen, chosen_half = pl.pallas_call(
        rows_kernel,
        out_shape=[shape((row_count, 3 * panel), bf16), shape((panel, packed), bf16), shape((panel, 1))],
        scratch_shapes=[pltpu.VMEM((row_count, 3 * panel), bf16)],
        **compute_params(1, 1),
    )(*pieces, vectors, factor_right, pick, left, left_half)

    chunks = 4
    return pl.pallas_call(
        functools.partial(update_kernel, rows, cols),
        out_shape=shape((row_count, col_count)),
        out_specs=pl.BlockSpec(memory_space=pl.ANY),
        scratch_shapes=[
            pltpu.VMEM((chunks, row_count // chunks, col_count), f32),
            pltpu.VMEM((3 * panel, col_count), bf16),
            pltpu.VMEM((3 * panel, col_count), bf16),
            pltpu.SemaphoreType.DMA((chunks,)),
        ],
        **compute_params(4 * 10**9, 8 * 10**6),
    )(sent, points, vectors, factor_left, left, left_half, rows_left, chosen, chosen_half)


def solution(mesh):
    in_specs = (P("row", None), P("col", None), P(), P(), P(), P(), P("row"))
    out_specs = P("row", "col")
    return jax.shard_map(
        on_device, mesh=mesh, in_specs=in_specs, out_specs=out_specs, check_vma=False
    )
```

```python
import collections
import functools
import math
import random

import jax
import jax.numpy as jnp
from jax import lax
from jax.experimental import pallas as pl
from jax.experimental.pallas import tpu as pltpu
from jax.sharding import PartitionSpec as P

log2_e = 1.4426950408889634
vmem_bytes = 32 * 1024 * 1024
f32, bf16 = jnp.float32, jnp.bfloat16
block = 256


def halves_of(value):
    high = value.astype(bf16)
    low = (value - high.astype(f32)).astype(bf16)
    return high, low


def pack_left(high, low):
    return jnp.concatenate([high, low, high, low], axis=1)


def pack_right(high, low):
    return jnp.concatenate([high, low, low, high], axis=0)


def half_square(high, low, axis):
    value = high.astype(f32) + low.astype(f32)
    return 0.5 * jnp.sum(value * value, axis=axis, keepdims=True)


def product(left, right):
    return lax.dot_general(left, right, (((1,), (0,)), ((), ())), preferred_element_type=f32)


def store_left(ref, rows, first, value):
    high, low = halves_of(value)
    for start in range(0, value.shape[1], block):
        now, at = slice(start, start + block), 3 * (first + start)
        ref[rows, at : at + block] = high[:, now]
        ref[rows, at + block : at + 2 * block] = high[:, now]
        ref[rows, at + 2 * block : at + 3 * block] = low[:, now]


def store_right(ref, first, value):
    high, low = halves_of(value)
    for start in range(0, value.shape[0], block):
        now, at = slice(start, start + block), 3 * (first + start)
        ref[at : at + block, :] = high[now]
        ref[at + block : at + 2 * block, :] = low[now]
        ref[at + 2 * block : at + 3 * block, :] = high[now]


def kern(crossed, left_half, right_half):
    return jnp.exp2((crossed - left_half) - (right_half - 1.0))


def scale_of(vectors_ref, features):
    return jnp.sqrt(vectors_ref[:, :features] * log2_e)


def parts_kernel(
    factor_ref, order_ref, points_ref, vectors_ref, factor_left_ref, factor_right_ref, pick_ref, left_ref,
    left_half_ref,
):
    factor = factor_ref[...]
    store_left(factor_left_ref, slice(None), 0, factor)
    store_right(factor_right_ref, 0, jnp.transpose(factor))
    panel = factor.shape[0]
    core = lax.axis_index("col") % 2
    place = lax.broadcasted_iota(jnp.int32, (panel, panel), 0) + core * (panel // 2)
    place = jnp.where(place >= panel, place - panel, place)
    hit = jnp.where(place == order_ref[...], 1.0, 0.0).astype(f32)
    pick_ref[...] = jnp.transpose(hit).astype(bf16)
    high, low = halves_of(points_ref[...] * scale_of(vectors_ref, points_ref.shape[1]))
    left_ref[...] = pack_left(high, low)
    left_half_ref[...] = half_square(high, low, 1)


def rows_kernel(
    own_ref, other_ref, vectors_ref, factor_right_ref, pick_ref, left_ref, left_half_ref,
    rows_ref, chosen_ref, chosen_half_ref, kern_ref,
):
    panel = pick_ref.shape[0]
    features = own_ref.shape[1]
    held = jnp.concatenate([own_ref[...], other_ref[...]], axis=0) * scale_of(vectors_ref, features)
    chosen = product(pick_ref[...], jnp.concatenate(halves_of(held), axis=1))
    high, low = chosen[:, :features].astype(bf16), chosen[:, features:].astype(bf16)
    chosen_ref[...] = pack_left(high, low)
    chosen_half_ref[...] = half_square(high, low, 1)
    turned = jnp.transpose(chosen)
    high, low = turned[:features].astype(bf16), turned[features:].astype(bf16)
    right = pack_right(high, low)
    right_half = half_square(high, low, 0)
    chunks = 2
    count = left_ref.shape[0] // chunks
    places = [slice(number * count, (number + 1) * count) for number in range(chunks)]
    crossed = [product(left_ref[place, :], right) for place in places]
    for number, place in enumerate(places):
        store_left(kern_ref, place, 0, kern(crossed[number], left_half_ref[place, :], right_half))
        for first in range(0, panel, block):
            last = first + block
            part = product(kern_ref[place, : 3 * last], factor_right_ref[: 3 * last, first:last])
            store_left(rows_ref, place, first, part)


def update_kernel(
    rows, cols, sent_ref, vectors_ref, factor_left_ref, left_ref, left_half_ref, rows_ref, chosen_ref,
    chosen_half_ref, out_ref, block_ref, kern_ref, cols_ref, sems,
):
    row_place, col_place = lax.axis_index("row"), lax.axis_index("col")
    halves = cols // rows
    count = sent_ref.shape[0]
    part = col_place % halves
    own = row_place == col_place // halves
    panel, features = factor_left_ref.shape[0], sent_ref.shape[1]

    high, low = halves_of(jnp.transpose(sent_ref[...] * scale_of(vectors_ref, features)))
    right = pack_right(high, low)
    right_half = half_square(high, low, 0)
    chunks, chunk = block_ref.shape[:2]
    places = [slice(number * chunk, (number + 1) * chunk) for number in range(chunks)]
    at = pl.multiple_of(features + part * count, 128)
    noise = jnp.where(own, vectors_ref[:, pl.ds(at, count)], 0.0)
    ids = (chunk, count)
    below = lax.broadcasted_iota(jnp.int32, ids, 0) - lax.broadcasted_iota(jnp.int32, ids, 1)

    crossed = product(chosen_ref[...], right)
    tiles = [product(left_ref[place, :], right) for place in places]
    store_right(kern_ref, 0, kern(crossed, chosen_half_ref[...], right_half))
    for first in range(0, panel, block):
        last = first + block
        store_right(cols_ref, first, product(factor_left_ref[first:last, : 3 * last], kern_ref[: 3 * last, :]))
    for number, place in enumerate(places):
        tile = kern(tiles[number], left_half_ref[place, :], right_half)
        block_ref[number] = tile + jnp.where(below == part * count - number * chunk, noise, 0.0)

    copies = []
    for number, place in enumerate(places):
        block_ref[number] = block_ref[number] - product(rows_ref[place, :], cols_ref[...])
        copy = pltpu.make_async_copy(block_ref.at[number], out_ref.at[pl.ds(number * chunk, chunk)], sems.at[number])
        copy.start()
        copies.append(copy)
    for copy in copies:
        copy.wait()


def shape(dims, kind=f32):
    return jax.ShapeDtypeStruct(dims, kind)


def compute_params(flops, moved):
    return dict(
        compiler_params=pltpu.CompilerParams(vmem_limit_bytes=vmem_bytes),
        cost_estimate=pl.CostEstimate(flops=flops, bytes_accessed=moved, transcendentals=0),
    )


def links_of(place, group, target_row, across):
    links = []
    step = 1 if target_row > group else -1
    links += [(0, place, z, step) for z in range(group, target_row, step)]
    (x, y), (end_x, end_y) = (place % across, place // across), (group % across, group // across)
    step = 1 if end_x > x else -1
    links += [(1, target_row, y, at, step) for at in range(x, end_x, step)]
    step = 1 if end_y > y else -1
    links += [(2, target_row, end_x, at, step) for at in range(y, end_y, step)]
    return links


def source_places(rows, halves):
    draw = random.Random(5)
    across = math.isqrt(rows)
    places = {}
    load = collections.Counter()

    def move(key, r, sign):
        change = 0
        for link in links_of(places[key][r], key[1], r, across):
            old = load[link]
            load[link] = old + sign
            change += (old + sign) ** 4 - old**4
        return change

    for h in range(halves):
        for g in range(rows):
            places[h, g] = draw.sample(range(rows), rows)
            for r in range(rows):
                move((h, g), r, 1)
    best, total, kept = 0, 0, {key: list(value) for key, value in places.items()}
    tries = 20000
    for number in range(tries):
        key = draw.randrange(halves), draw.randrange(rows)
        one, two = draw.sample(range(rows), 2)
        own = places[key]
        change = move(key, one, -1) + move(key, two, -1)
        own[one], own[two] = own[two], own[one]
        change += move(key, one, 1) + move(key, two, 1)
        heat = 30.0 * (1 - number / tries) + 0.01
        if change <= 0 or draw.random() < math.exp(-change / heat):
            total += change
            if total < best:
                best, kept = total, {key: list(value) for key, value in places.items()}
        else:
            move(key, one, -1), move(key, two, -1)
            own[one], own[two] = own[two], own[one]
            move(key, one, 1), move(key, two, 1)
    return kept


def column_pairs(rows, cols):
    halves = cols // rows
    places = source_places(rows, halves)
    return [
        (g * cols + places[h, g][r] * halves + h, r * cols + g * halves + halves - 1 - h)
        for h in range(halves)
        for g in range(rows)
        for r in range(rows)
    ]


def swap(value, bit, cols):
    return lax.ppermute(value, "col", [(i, i ^ bit) for i in range(cols)])


def gather_panel(panel_pool, panel_block, cols, beside):
    col_place = lax.axis_index("col")
    core = col_place % 2
    half_rows = panel_pool.shape[0] // 2
    mine = lax.dynamic_slice_in_dim(panel_pool, core * half_rows, half_rows, 0)
    got, mine = lax.optimization_barrier((swap(panel_pool, 1, cols), mine))
    got = lax.dynamic_slice_in_dim(got, core * half_rows, half_rows, 0)
    held = jnp.where(panel_block % 2 == core, mine, got)
    apart = panel_block ^ col_place
    low = 2
    while low < cols:
        high = min(4 * low, cols)
        away = apart & (high - low)
        steps = range(low, high, low)
        received = [swap(held, bits, cols) for bits in steps]
        received, beside = lax.optimization_barrier((received, beside))
        for bits, value in zip(steps, received):
            held = jnp.where(away == bits, value, held)
        low = high
    return [held, swap(held, 1, cols)], beside


def on_device(points, panel_pool, order, panel_index, inv_factor, ard_weights, noise):
    row_count, features = points.shape
    panel = inv_factor.shape[0]
    rows = lax.axis_size("row")
    cols = lax.axis_size("col")
    col_count = row_count * rows // cols
    halves = cols // rows
    col_place = lax.axis_index("col")
    part = halves - 1 - col_place % halves
    own_half = lax.dynamic_slice_in_dim(points, part * col_count, col_count, 0)
    vectors = jnp.concatenate([ard_weights, noise])[None, :]
    own_half, vectors = lax.optimization_barrier((own_half, vectors))
    sent = lax.ppermute(own_half, ("row", "col"), column_pairs(rows, cols))
    pieces, vectors = gather_panel(panel_pool, panel_index[0], cols, vectors)

    packed = 4 * features
    factor_left, factor_right, pick, left, left_half = pl.pallas_call(
        parts_kernel,
        out_shape=[
            shape((panel, 3 * panel), bf16),
            shape((3 * panel, panel), bf16),
            shape((panel, panel), bf16),
            shape((row_count, packed), bf16),
            shape((row_count, 1)),
        ],
        **compute_params(10**8, 4 * 10**6),
    )(inv_factor, order[None, :], points, vectors)

    rows_left, chosen, chosen_half = pl.pallas_call(
        rows_kernel,
        out_shape=[shape((row_count, 3 * panel), bf16), shape((panel, packed), bf16), shape((panel, 1))],
        scratch_shapes=[pltpu.VMEM((row_count, 3 * panel), bf16)],
        **compute_params(1, 1),
    )(*pieces, vectors, factor_right, pick, left, left_half)

    chunks = 4
    return pl.pallas_call(
        functools.partial(update_kernel, rows, cols),
        out_shape=shape((row_count, col_count)),
        out_specs=pl.BlockSpec(memory_space=pl.ANY),
        scratch_shapes=[
            pltpu.VMEM((chunks, row_count // chunks, col_count), f32),
            pltpu.VMEM((3 * panel, col_count), bf16),
            pltpu.VMEM((3 * panel, col_count), bf16),
            pltpu.SemaphoreType.DMA((chunks,)),
        ],
        **compute_params(4 * 10**9, 8 * 10**6),
    )(sent, vectors, factor_left, left, left_half, rows_left, chosen, chosen_half)


def solution(mesh):
    in_specs = (P("row", None), P("col", None), P(), P(), P(), P(), P("row"))
    out_specs = P("row", "col")
    return jax.shard_map(
        on_device, mesh=mesh, in_specs=in_specs, out_specs=out_specs, check_vma=False
    )
```

```python
import collections
import functools
import math
import random

import jax
import jax.numpy as jnp
from jax import lax
from jax.experimental import pallas as pl
from jax.experimental.pallas import tpu as pltpu
from jax.sharding import PartitionSpec as P

log2_e = 1.4426950408889634
vmem_bytes = 32 * 1024 * 1024
f32, bf16 = jnp.float32, jnp.bfloat16
block, square = 256, 128


def halves_of(value):
    high = value.astype(bf16)
    low = (value - high.astype(f32)).astype(bf16)
    return high, low


def pack_left(high, low):
    return jnp.concatenate([high, low, high, low], axis=1)


def pack_right(high, low):
    return jnp.concatenate([high, low, low, high], axis=0)


def half_square(high, low, axis):
    value = high.astype(f32) + low.astype(f32)
    return 0.5 * jnp.sum(value * value, axis=axis, keepdims=True)


def product(left, right):
    return lax.dot_general(left, right, (((1,), (0,)), ((), ())), preferred_element_type=f32)


def store_left(ref, rows, first, value):
    high, low = halves_of(value)
    for start in range(0, value.shape[1], block):
        now, at = slice(start, start + block), 3 * (first + start)
        ref[rows, at : at + block] = high[:, now]
        ref[rows, at + block : at + 2 * block] = high[:, now]
        ref[rows, at + 2 * block : at + 3 * block] = low[:, now]


def store_right(ref, first, value):
    high, low = halves_of(value)
    for start in range(0, value.shape[0], block):
        now, at = slice(start, start + block), 3 * (first + start)
        ref[at : at + block, :] = high[now]
        ref[at + block : at + 2 * block, :] = low[now]
        ref[at + 2 * block : at + 3 * block, :] = high[now]


def kern(crossed, left_half, right_half):
    return jnp.exp2((crossed - left_half) - (right_half - 1.0))


def scale_of(vectors_ref, panel, features):
    return jnp.sqrt(vectors_ref[:, panel : panel + features] * log2_e)


def parts_kernel(
    factor_ref, points_ref, vectors_ref, factor_left_ref, factor_right_ref, pick_ref, left_ref,
    left_half_ref,
):
    factor = factor_ref[...]
    store_left(factor_left_ref, slice(None), 0, factor)
    store_right(factor_right_ref, 0, jnp.transpose(factor))
    panel = factor.shape[0]
    core = lax.axis_index("col") % 2
    place = lax.broadcasted_iota(jnp.int32, (panel, panel), 0) + core * (panel // 2)
    place = jnp.where(place >= panel, place - panel, place).astype(f32)
    hit = jnp.where(place == vectors_ref[:, :panel], 1.0, 0.0).astype(f32)
    pick_ref[...] = jnp.transpose(hit).astype(bf16)
    high, low = halves_of(points_ref[...] * scale_of(vectors_ref, panel, points_ref.shape[1]))
    left_ref[...] = pack_left(high, low)
    left_half_ref[...] = half_square(high, low, 1)


def rows_kernel(
    own_ref, other_ref, vectors_ref, factor_right_ref, pick_ref, left_ref, left_half_ref,
    rows_ref, chosen_ref, chosen_half_ref, kern_ref,
):
    panel = pick_ref.shape[0]
    features = own_ref.shape[1]
    held = jnp.concatenate([own_ref[...], other_ref[...]], axis=0) * scale_of(vectors_ref, panel, features)
    chosen = product(pick_ref[...], jnp.concatenate(halves_of(held), axis=1))
    high, low = chosen[:, :features].astype(bf16), chosen[:, features:].astype(bf16)
    chosen_ref[...] = pack_left(high, low)
    chosen_half_ref[...] = half_square(high, low, 1)
    turned = jnp.transpose(chosen)
    high, low = turned[:features].astype(bf16), turned[features:].astype(bf16)
    right = pack_right(high, low)
    right_half = half_square(high, low, 0)
    chunks = 2
    count = left_ref.shape[0] // chunks
    places = [slice(number * count, (number + 1) * count) for number in range(chunks)]
    crossed = [product(left_ref[place, :], right) for place in places]
    for number, place in enumerate(places):
        store_left(kern_ref, place, 0, kern(crossed[number], left_half_ref[place, :], right_half))
        for first in range(0, panel, block):
            last = first + block
            part = product(kern_ref[place, : 3 * last], factor_right_ref[: 3 * last, first:last])
            store_left(rows_ref, place, first, part)


def update_kernel(
    rows, cols, sent_ref, vectors_ref, factor_left_ref, left_ref, left_half_ref, rows_ref, chosen_ref,
    chosen_half_ref, out_ref, block_ref, kern_ref, cols_ref, sems,
):
    row_place, col_place = lax.axis_index("row"), lax.axis_index("col")
    halves = cols // rows
    count = sent_ref.shape[0]
    part = col_place % halves
    own = row_place == col_place // halves
    panel, features = factor_left_ref.shape[0], sent_ref.shape[1]

    high, low = halves_of(jnp.transpose(sent_ref[...] * scale_of(vectors_ref, panel, features)))
    right = pack_right(high, low)
    right_half = half_square(high, low, 0)
    chunks, chunk = block_ref.shape[:2]
    places = [slice(number * chunk, (number + 1) * chunk) for number in range(chunks)]
    at = pl.multiple_of(panel + features + part * count, 128)
    noise = jnp.where(own, vectors_ref[:, pl.ds(at, count)], 0.0)
    ids = (square, square)
    on_diagonal = lax.broadcasted_iota(jnp.int32, ids, 0) == lax.broadcasted_iota(jnp.int32, ids, 1)

    crossed = product(chosen_ref[...], right)
    tiles = [product(left_ref[place, :], right) for place in places]
    store_right(kern_ref, 0, kern(crossed, chosen_half_ref[...], right_half))
    for first in range(0, panel, block):
        last = first + block
        store_right(cols_ref, first, product(factor_left_ref[first:last, : 3 * last], kern_ref[: 3 * last, :]))
    copies = []
    for number, place in enumerate(places):
        update = product(rows_ref[place, :], cols_ref[...])
        block_ref[number] = kern(tiles[number], left_half_ref[place, :], right_half) - update
        here = jnp.where(part == place.start // count, noise, 0.0)
        for start in range(0, chunk, square):
            first = place.start % count + start
            now, across = slice(start, start + square), slice(first, first + square)
            block_ref[number, now, across] += jnp.where(on_diagonal, here[:, across], 0.0)
        copy = pltpu.make_async_copy(block_ref.at[number], out_ref.at[pl.ds(number * chunk, chunk)], sems.at[number])
        copy.start()
        copies.append(copy)
    for copy in copies:
        copy.wait()


def shape(dims, kind=f32):
    return jax.ShapeDtypeStruct(dims, kind)


def compute_params(flops, moved):
    return dict(
        compiler_params=pltpu.CompilerParams(vmem_limit_bytes=vmem_bytes),
        cost_estimate=pl.CostEstimate(flops=flops, bytes_accessed=moved, transcendentals=0),
    )


def links_of(place, group, target_row, across):
    links = []
    step = 1 if target_row > group else -1
    links += [(0, place, z, step) for z in range(group, target_row, step)]
    (x, y), (end_x, end_y) = (place % across, place // across), (group % across, group // across)
    step = 1 if end_x > x else -1
    links += [(1, target_row, y, at, step) for at in range(x, end_x, step)]
    step = 1 if end_y > y else -1
    links += [(2, target_row, end_x, at, step) for at in range(y, end_y, step)]
    return links


def source_places(rows, halves):
    draw = random.Random(1)
    across = math.isqrt(rows)
    places = {}
    load = collections.Counter()

    def move(key, r, sign):
        change = 0
        for link in links_of(places[key][r], key[1], r, across):
            old = load[link]
            load[link] = old + sign
            change += (old + sign) ** 4 - old**4
        return change

    for h in range(halves):
        for g in range(rows):
            places[h, g] = draw.sample(range(rows), rows)
            for r in range(rows):
                move((h, g), r, 1)
    best, total, kept = 0, 0, {key: list(value) for key, value in places.items()}
    tries = 20000
    for number in range(tries):
        key = draw.randrange(halves), draw.randrange(rows)
        one, two = draw.sample(range(rows), 2)
        own = places[key]
        change = move(key, one, -1) + move(key, two, -1)
        own[one], own[two] = own[two], own[one]
        change += move(key, one, 1) + move(key, two, 1)
        heat = 30.0 * (1 - number / tries) + 0.01
        if change <= 0 or draw.random() < math.exp(-change / heat):
            total += change
            if total < best:
                best, kept = total, {key: list(value) for key, value in places.items()}
        else:
            move(key, one, -1), move(key, two, -1)
            own[one], own[two] = own[two], own[one]
            move(key, one, 1), move(key, two, 1)
    return kept


def column_pairs(rows, cols):
    halves = cols // rows
    places = source_places(rows, halves)
    return [
        (g * cols + places[h, g][r] * halves + h, r * cols + g * halves + halves - 1 - h)
        for h in range(halves)
        for g in range(rows)
        for r in range(rows)
    ]


def swap(value, bit, cols):
    return lax.ppermute(value, "col", [(i, i ^ bit) for i in range(cols)])


def gather_panel(panel_pool, panel_block, cols, beside):
    col_place = lax.axis_index("col")
    core = col_place % 2
    half_rows = panel_pool.shape[0] // 2
    mine = lax.dynamic_slice_in_dim(panel_pool, core * half_rows, half_rows, 0)
    got, mine = lax.optimization_barrier((swap(panel_pool, 1, cols), mine))
    got = lax.dynamic_slice_in_dim(got, core * half_rows, half_rows, 0)
    held = jnp.where(panel_block % 2 == core, mine, got)
    apart = panel_block ^ col_place
    low = 2
    while low < cols:
        high = min(4 * low, cols)
        away = apart & (high - low)
        steps = range(high - low, 0, -low)
        received = [swap(held, bits, cols) for bits in steps]
        received, beside = lax.optimization_barrier((received, beside))
        for bits, value in zip(steps, received):
            held = jnp.where(away == bits, value, held)
        low = high
    return [held, swap(held, 1, cols)], beside


def on_device(points, panel_pool, order, panel_index, inv_factor, ard_weights, noise):
    row_count, features = points.shape
    panel = inv_factor.shape[0]
    rows = lax.axis_size("row")
    cols = lax.axis_size("col")
    col_count = row_count * rows // cols
    halves = cols // rows
    col_place = lax.axis_index("col")
    part = halves - 1 - col_place % halves
    own_half = lax.dynamic_slice_in_dim(points, part * col_count, col_count, 0)
    sent = lax.ppermute(own_half, ("row", "col"), column_pairs(rows, cols))
    vectors = jnp.concatenate([order.astype(f32), ard_weights, noise])[None, :]
    pieces, vectors = gather_panel(panel_pool, panel_index[0], cols, vectors)

    packed = 4 * features
    factor_left, factor_right, pick, left, left_half = pl.pallas_call(
        parts_kernel,
        out_shape=[
            shape((panel, 3 * panel), bf16),
            shape((3 * panel, panel), bf16),
            shape((panel, panel), bf16),
            shape((row_count, packed), bf16),
            shape((row_count, 1)),
        ],
        **compute_params(10**8, 4 * 10**6),
    )(inv_factor, points, vectors)

    rows_left, chosen, chosen_half = pl.pallas_call(
        rows_kernel,
        out_shape=[shape((row_count, 3 * panel), bf16), shape((panel, packed), bf16), shape((panel, 1))],
        scratch_shapes=[pltpu.VMEM((row_count, 3 * panel), bf16)],
        **compute_params(1, 1),
    )(*pieces, vectors, factor_right, pick, left, left_half)

    chunks = 4
    return pl.pallas_call(
        functools.partial(update_kernel, rows, cols),
        out_shape=shape((row_count, col_count)),
        out_specs=pl.BlockSpec(memory_space=pl.ANY),
        scratch_shapes=[
            pltpu.VMEM((chunks, row_count // chunks, col_count), f32),
            pltpu.VMEM((3 * panel, col_count), bf16),
            pltpu.VMEM((3 * panel, col_count), bf16),
            pltpu.SemaphoreType.DMA((chunks,)),
        ],
        **compute_params(4 * 10**9, 8 * 10**6),
    )(sent, vectors, factor_left, left, left_half, rows_left, chosen, chosen_half)


def solution(mesh):
    in_specs = (P("row", None), P("col", None), P(), P(), P(), P(), P("row"))
    out_specs = P("row", "col")
    return jax.shard_map(
        on_device, mesh=mesh, in_specs=in_specs, out_specs=out_specs, check_vma=False
    )
```

```python
import collections
import functools
import math
import random

import jax
import jax.numpy as jnp
from jax import lax
from jax.experimental import pallas as pl
from jax.experimental.pallas import tpu as pltpu
from jax.sharding import PartitionSpec as P

log2_e = 1.4426950408889634
vmem_bytes = 32 * 1024 * 1024
f32, bf16 = jnp.float32, jnp.bfloat16
block, square = 256, 128


def halves_of(value):
    high = value.astype(bf16)
    low = (value - high.astype(f32)).astype(bf16)
    return high, low


def pack_left(high, low):
    return jnp.concatenate([high, low, high, low], axis=1)


def pack_right(high, low):
    return jnp.concatenate([high, low, low, high], axis=0)


def half_square(high, low, axis):
    value = high.astype(f32) + low.astype(f32)
    return 0.5 * jnp.sum(value * value, axis=axis, keepdims=True)


def product(left, right):
    return lax.dot_general(left, right, (((1,), (0,)), ((), ())), preferred_element_type=f32)


def store_left(ref, rows, first, value):
    high, low = halves_of(value)
    for start in range(0, value.shape[1], block):
        now, at = slice(start, start + block), 3 * (first + start)
        ref[rows, at : at + block] = high[:, now]
        ref[rows, at + block : at + 2 * block] = high[:, now]
        ref[rows, at + 2 * block : at + 3 * block] = low[:, now]


def store_right(ref, first, value):
    high, low = halves_of(value)
    for start in range(0, value.shape[0], block):
        now, at = slice(start, start + block), 3 * (first + start)
        ref[at : at + block, :] = high[now]
        ref[at + block : at + 2 * block, :] = low[now]
        ref[at + 2 * block : at + 3 * block, :] = high[now]


def kern(crossed, left_half, right_half):
    return jnp.exp2((crossed - left_half) - (right_half - 1.0))


def scale_of(vectors_ref, panel, features):
    return jnp.sqrt(vectors_ref[:, panel : panel + features] * log2_e)


def parts_kernel(
    factor_ref, points_ref, vectors_ref, factor_left_ref, factor_right_ref, pick_ref, left_ref,
    left_half_ref,
):
    factor = factor_ref[...]
    store_left(factor_left_ref, slice(None), 0, factor)
    store_right(factor_right_ref, 0, jnp.transpose(factor))
    panel = factor.shape[0]
    core = lax.axis_index("col") % 2
    place = lax.broadcasted_iota(jnp.int32, (panel, panel), 0) + core * (panel // 2)
    place = jnp.where(place >= panel, place - panel, place).astype(f32)
    hit = jnp.where(place == vectors_ref[:, :panel], 1.0, 0.0).astype(f32)
    pick_ref[...] = jnp.transpose(hit).astype(bf16)
    high, low = halves_of(points_ref[...] * scale_of(vectors_ref, panel, points_ref.shape[1]))
    left_ref[...] = pack_left(high, low)
    left_half_ref[...] = half_square(high, low, 1)


def rows_kernel(
    own_ref, other_ref, vectors_ref, factor_right_ref, pick_ref, left_ref, left_half_ref,
    rows_ref, chosen_ref, chosen_half_ref, kern_ref,
):
    panel = pick_ref.shape[0]
    features = own_ref.shape[1]
    held = jnp.concatenate([own_ref[...], other_ref[...]], axis=0) * scale_of(vectors_ref, panel, features)
    chosen = product(pick_ref[...], jnp.concatenate(halves_of(held), axis=1))
    high, low = chosen[:, :features].astype(bf16), chosen[:, features:].astype(bf16)
    chosen_ref[...] = pack_left(high, low)
    chosen_half_ref[...] = half_square(high, low, 1)
    turned = jnp.transpose(chosen)
    high, low = turned[:features].astype(bf16), turned[features:].astype(bf16)
    right = pack_right(high, low)
    right_half = half_square(high, low, 0)
    chunks = 2
    count = left_ref.shape[0] // chunks
    places = [slice(number * count, (number + 1) * count) for number in range(chunks)]
    crossed = [product(left_ref[place, :], right) for place in places]
    for number, place in enumerate(places):
        store_left(kern_ref, place, 0, kern(crossed[number], left_half_ref[place, :], right_half))
        for first in range(0, panel, block):
            last = first + block
            part = product(kern_ref[place, : 3 * last], factor_right_ref[: 3 * last, first:last])
            store_left(rows_ref, place, first, part)


def update_kernel(
    rows, cols, sent_ref, vectors_ref, factor_left_ref, left_ref, left_half_ref, rows_ref, chosen_ref,
    chosen_half_ref, out_ref, block_ref, kern_ref, cols_ref, sems,
):
    row_place, col_place = lax.axis_index("row"), lax.axis_index("col")
    halves = cols // rows
    count = sent_ref.shape[0]
    part = col_place % halves
    own = row_place == col_place // halves
    panel, features = factor_left_ref.shape[0], sent_ref.shape[1]

    high, low = halves_of(jnp.transpose(sent_ref[...] * scale_of(vectors_ref, panel, features)))
    right = pack_right(high, low)
    right_half = half_square(high, low, 0)
    chunks, chunk = block_ref.shape[:2]
    places = [slice(number * chunk, (number + 1) * chunk) for number in range(chunks)]
    at = pl.multiple_of(panel + features + part * count, 128)
    noise = jnp.where(own, vectors_ref[:, pl.ds(at, count)], 0.0)
    ids = (square, square)
    on_diagonal = lax.broadcasted_iota(jnp.int32, ids, 0) == lax.broadcasted_iota(jnp.int32, ids, 1)

    crossed = product(chosen_ref[...], right)
    tiles = [product(left_ref[place, :], right) for place in places]
    store_right(kern_ref, 0, kern(crossed, chosen_half_ref[...], right_half))
    for first in range(0, panel, block):
        last = first + block
        store_right(cols_ref, first, product(factor_left_ref[first:last, : 3 * last], kern_ref[: 3 * last, :]))
    copies = []
    for number, place in enumerate(places):
        update = product(rows_ref[place, :], cols_ref[...])
        block_ref[number] = kern(tiles[number], left_half_ref[place, :], right_half) - update
        here = jnp.where(part == place.start // count, noise, 0.0)
        for start in range(0, chunk, square):
            first = place.start % count + start
            now, across = slice(start, start + square), slice(first, first + square)
            block_ref[number, now, across] += jnp.where(on_diagonal, here[:, across], 0.0)
        copy = pltpu.make_async_copy(block_ref.at[number], out_ref.at[pl.ds(number * chunk, chunk)], sems.at[number])
        copy.start()
        copies.append(copy)
    for copy in copies:
        copy.wait()


def shape(dims, kind=f32):
    return jax.ShapeDtypeStruct(dims, kind)


def compute_params(flops, moved):
    return dict(
        compiler_params=pltpu.CompilerParams(vmem_limit_bytes=vmem_bytes),
        cost_estimate=pl.CostEstimate(flops=flops, bytes_accessed=moved, transcendentals=0),
    )


def links_of(place, group, target_row, across):
    links = []
    step = 1 if target_row > group else -1
    links += [(0, place, z, step) for z in range(group, target_row, step)]
    (x, y), (end_x, end_y) = (place % across, place // across), (group % across, group // across)
    step = 1 if end_x > x else -1
    links += [(1, target_row, y, at, step) for at in range(x, end_x, step)]
    step = 1 if end_y > y else -1
    links += [(2, target_row, end_x, at, step) for at in range(y, end_y, step)]
    return links


def source_places(rows, halves):
    draw = random.Random(2)
    across = math.isqrt(rows)
    places = {}
    load = collections.Counter()

    def move(key, r, sign):
        change = 0
        early = rows - 1 == r <= key[1] + 1
        for link in links_of(places[key][r], key[1], r, across):
            old = load[link]
            load[link] = old + sign
            change += (old + sign) ** 4 - old**4 + sign * 40 * (early and link[0] == 2)
        return change

    for h in range(halves):
        for g in range(rows):
            places[h, g] = draw.sample(range(rows), rows)
            for r in range(rows):
                move((h, g), r, 1)
    best, total, kept = 0, 0, {key: list(value) for key, value in places.items()}
    tries = 20000
    for number in range(tries):
        key = draw.randrange(halves), draw.randrange(rows)
        one, two = draw.sample(range(rows), 2)
        own = places[key]
        change = move(key, one, -1) + move(key, two, -1)
        own[one], own[two] = own[two], own[one]
        change += move(key, one, 1) + move(key, two, 1)
        heat = 30.0 * (1 - number / tries) + 0.01
        if change <= 0 or draw.random() < math.exp(-change / heat):
            total += change
            if total < best:
                best, kept = total, {key: list(value) for key, value in places.items()}
        else:
            move(key, one, -1), move(key, two, -1)
            own[one], own[two] = own[two], own[one]
            move(key, one, 1), move(key, two, 1)
    return kept


def column_pairs(rows, cols):
    halves = cols // rows
    places = source_places(rows, halves)
    return [
        (g * cols + places[h, g][r] * halves + h, r * cols + g * halves + halves - 1 - h)
        for h in range(halves)
        for g in range(rows)
        for r in range(rows)
    ]


def swap(value, bit, cols):
    return lax.ppermute(value, "col", [(i, i ^ bit) for i in range(cols)])


def gather_panel(panel_pool, panel_block, cols, beside):
    col_place = lax.axis_index("col")
    core = col_place % 2
    half_rows = panel_pool.shape[0] // 2
    mine = lax.dynamic_slice_in_dim(panel_pool, core * half_rows, half_rows, 0)
    got, mine = lax.optimization_barrier((swap(panel_pool, 1, cols), mine))
    got = lax.dynamic_slice_in_dim(got, core * half_rows, half_rows, 0)
    held = jnp.where(panel_block % 2 == core, mine, got)
    apart = panel_block ^ col_place
    low = 2
    while low < cols:
        high = min(4 * low, cols)
        away = apart & (high - low)
        steps = range(high - low, 0, -low)
        received = [swap(held, bits, cols) for bits in steps]
        received, beside = lax.optimization_barrier((received, beside))
        for bits, value in zip(steps, received):
            held = jnp.where(away == bits, value, held)
        low = high
    return [held, swap(held, 1, cols)], beside


def on_device(points, panel_pool, order, panel_index, inv_factor, ard_weights, noise):
    row_count, features = points.shape
    panel = inv_factor.shape[0]
    rows = lax.axis_size("row")
    cols = lax.axis_size("col")
    col_count = row_count * rows // cols
    halves = cols // rows
    col_place = lax.axis_index("col")
    part = halves - 1 - col_place % halves
    own_half = lax.dynamic_slice_in_dim(points, part * col_count, col_count, 0)
    sent = lax.ppermute(own_half, ("row", "col"), column_pairs(rows, cols))
    vectors = jnp.concatenate([order.astype(f32), ard_weights, noise])[None, :]
    pieces, vectors = gather_panel(panel_pool, panel_index[0], cols, vectors)

    packed = 4 * features
    factor_left, factor_right, pick, left, left_half = pl.pallas_call(
        parts_kernel,
        out_shape=[
            shape((panel, 3 * panel), bf16),
            shape((3 * panel, panel), bf16),
            shape((panel, panel), bf16),
            shape((row_count, packed), bf16),
            shape((row_count, 1)),
        ],
        **compute_params(10**8, 4 * 10**6),
    )(inv_factor, points, vectors)

    rows_left, chosen, chosen_half = pl.pallas_call(
        rows_kernel,
        out_shape=[shape((row_count, 3 * panel), bf16), shape((panel, packed), bf16), shape((panel, 1))],
        scratch_shapes=[pltpu.VMEM((row_count, 3 * panel), bf16)],
        **compute_params(1, 1),
    )(*pieces, vectors, factor_right, pick, left, left_half)

    chunks = 4
    return pl.pallas_call(
        functools.partial(update_kernel, rows, cols),
        out_shape=shape((row_count, col_count)),
        out_specs=pl.BlockSpec(memory_space=pl.ANY),
        scratch_shapes=[
            pltpu.VMEM((chunks, row_count // chunks, col_count), f32),
            pltpu.VMEM((3 * panel, col_count), bf16),
            pltpu.VMEM((3 * panel, col_count), bf16),
            pltpu.SemaphoreType.DMA((chunks,)),
        ],
        **compute_params(4 * 10**9, 8 * 10**6),
    )(sent, vectors, factor_left, left, left_half, rows_left, chosen, chosen_half)


def solution(mesh):
    in_specs = (P("row", None), P("col", None), P(), P(), P(), P(), P("row"))
    out_specs = P("row", "col")
    return jax.shard_map(
        on_device, mesh=mesh, in_specs=in_specs, out_specs=out_specs, check_vma=False
    )
```

```python
import collections
import functools
import math
import random

import jax
import jax.numpy as jnp
from jax import lax
from jax.experimental import pallas as pl
from jax.experimental.pallas import tpu as pltpu
from jax.sharding import PartitionSpec as P

log2_e = 1.4426950408889634
vmem_bytes = 32 * 1024 * 1024
f32, bf16 = jnp.float32, jnp.bfloat16
block, square = 256, 128


def halves_of(value):
    high = value.astype(bf16)
    low = (value - high.astype(f32)).astype(bf16)
    return high, low


def pack_left(high, low):
    return jnp.concatenate([high, low, high, low], axis=1)


def pack_right(high, low):
    return jnp.concatenate([high, low, low, high], axis=0)


def half_square(high, low, axis):
    value = high.astype(f32) + low.astype(f32)
    return 0.5 * jnp.sum(value * value, axis=axis, keepdims=True)


def product(left, right):
    return lax.dot_general(left, right, (((1,), (0,)), ((), ())), preferred_element_type=f32)


def store_left(ref, rows, first, value):
    high, low = halves_of(value)
    for start in range(0, value.shape[1], block):
        now, at = slice(start, start + block), 3 * (first + start)
        ref[rows, at : at + block] = high[:, now]
        ref[rows, at + block : at + 2 * block] = high[:, now]
        ref[rows, at + 2 * block : at + 3 * block] = low[:, now]


def store_right(ref, first, value):
    high, low = halves_of(value)
    for start in range(0, value.shape[0], block):
        now, at = slice(start, start + block), 3 * (first + start)
        ref[at : at + block, :] = high[now]
        ref[at + block : at + 2 * block, :] = low[now]
        ref[at + 2 * block : at + 3 * block, :] = high[now]


def kern(crossed, left_half, right_half):
    return jnp.exp2((crossed - left_half) - (right_half - 1.0))


def scale_of(vectors_ref, panel, features):
    return jnp.sqrt(vectors_ref[:, panel : panel + features] * log2_e)


def parts_kernel(
    factor_ref, points_ref, vectors_ref, factor_left_ref, factor_right_ref, pick_ref, left_ref,
    left_half_ref,
):
    factor = factor_ref[...]
    store_left(factor_left_ref, slice(None), 0, factor)
    store_right(factor_right_ref, 0, jnp.transpose(factor))
    panel = factor.shape[0]
    core = lax.axis_index("col") % 2
    place = lax.broadcasted_iota(jnp.int32, (panel, panel), 0) + core * (panel // 2)
    place = jnp.where(place >= panel, place - panel, place).astype(f32)
    hit = jnp.where(place == vectors_ref[:, :panel], 1.0, 0.0).astype(f32)
    pick_ref[...] = jnp.transpose(hit).astype(bf16)
    high, low = halves_of(points_ref[...] * scale_of(vectors_ref, panel, points_ref.shape[1]))
    left_ref[...] = pack_left(high, low)
    left_half_ref[...] = half_square(high, low, 1)


def rows_kernel(
    own_ref, other_ref, vectors_ref, factor_right_ref, pick_ref, left_ref, left_half_ref,
    rows_ref, chosen_ref, chosen_half_ref, kern_ref,
):
    panel = pick_ref.shape[0]
    features = own_ref.shape[1]
    held = jnp.concatenate([own_ref[...], other_ref[...]], axis=0) * scale_of(vectors_ref, panel, features)
    chosen = product(pick_ref[...], jnp.concatenate(halves_of(held), axis=1))
    high, low = chosen[:, :features].astype(bf16), chosen[:, features:].astype(bf16)
    chosen_ref[...] = pack_left(high, low)
    chosen_half_ref[...] = half_square(high, low, 1)
    turned = jnp.transpose(chosen)
    high, low = turned[:features].astype(bf16), turned[features:].astype(bf16)
    right = pack_right(high, low)
    right_half = half_square(high, low, 0)
    chunks = 2
    count = left_ref.shape[0] // chunks
    places = [slice(number * count, (number + 1) * count) for number in range(chunks)]
    crossed = [product(left_ref[place, :], right) for place in places]
    for number, place in enumerate(places):
        store_left(kern_ref, place, 0, kern(crossed[number], left_half_ref[place, :], right_half))
        for first in range(0, panel, block):
            last = first + block
            part = product(kern_ref[place, : 3 * last], factor_right_ref[: 3 * last, first:last])
            store_left(rows_ref, place, first, part)


def update_kernel(
    rows, cols, sent_ref, vectors_ref, factor_left_ref, left_ref, left_half_ref, rows_ref, chosen_ref,
    chosen_half_ref, out_ref, block_ref, kern_ref, cols_ref, sems,
):
    row_place, col_place = lax.axis_index("row"), lax.axis_index("col")
    halves = cols // rows
    count = sent_ref.shape[0]
    part = col_place % halves
    own = row_place == col_place // halves
    panel, features = factor_left_ref.shape[0], sent_ref.shape[1]

    high, low = halves_of(jnp.transpose(sent_ref[...] * scale_of(vectors_ref, panel, features)))
    right = pack_right(high, low)
    right_half = half_square(high, low, 0)
    chunks, chunk = block_ref.shape[:2]
    places = [slice(number * chunk, (number + 1) * chunk) for number in range(chunks)]
    at = pl.multiple_of(panel + features + part * count, 128)
    noise = jnp.where(own, vectors_ref[:, pl.ds(at, count)], 0.0)
    ids = (square, square)
    on_diagonal = lax.broadcasted_iota(jnp.int32, ids, 0) == lax.broadcasted_iota(jnp.int32, ids, 1)

    crossed = product(chosen_ref[...], right)
    tiles = [product(left_ref[place, :], right) for place in places]
    store_right(kern_ref, 0, kern(crossed, chosen_half_ref[...], right_half))
    for first in range(0, panel, block):
        last = first + block
        store_right(cols_ref, first, product(factor_left_ref[first:last, : 3 * last], kern_ref[: 3 * last, :]))
    copies = []
    for number, place in enumerate(places):
        update = product(rows_ref[place, :], cols_ref[...])
        block_ref[number] = kern(tiles[number], left_half_ref[place, :], right_half) - update
        here = jnp.where(part == place.start // count, noise, 0.0)
        for start in range(0, chunk, square):
            first = place.start % count + start
            now, across = slice(start, start + square), slice(first, first + square)
            block_ref[number, now, across] += jnp.where(on_diagonal, here[:, across], 0.0)
        copy = pltpu.make_async_copy(block_ref.at[number], out_ref.at[pl.ds(number * chunk, chunk)], sems.at[number])
        copy.start()
        copies.append(copy)
    for copy in copies:
        copy.wait()


def shape(dims, kind=f32):
    return jax.ShapeDtypeStruct(dims, kind)


def compute_params(flops, moved):
    return dict(
        compiler_params=pltpu.CompilerParams(vmem_limit_bytes=vmem_bytes),
        cost_estimate=pl.CostEstimate(flops=flops, bytes_accessed=moved, transcendentals=0),
    )


def links_of(place, group, target_row, across):
    links = []
    step = 1 if target_row > group else -1
    links += [(0, place, z, step) for z in range(group, target_row, step)]
    (x, y), (end_x, end_y) = (place % across, place // across), (group % across, group // across)
    step = 1 if end_x > x else -1
    links += [(1, target_row, y, at, step) for at in range(x, end_x, step)]
    step = 1 if end_y > y else -1
    links += [(2, target_row, end_x, at, step) for at in range(y, end_y, step)]
    return links


def source_places(rows, halves):
    draw = random.Random(5)
    across = math.isqrt(rows)
    places = {}
    load = collections.Counter()

    def move(key, r, sign):
        change = 0
        for link in links_of(places[key][r], key[1], r, across):
            old = load[link]
            load[link] = old + sign
            change += (old + sign) ** 4 - old**4
        return change

    for h in range(halves):
        for g in range(rows):
            places[h, g] = draw.sample(range(rows), rows)
            for r in range(rows):
                move((h, g), r, 1)
    best, total, kept = 0, 0, {key: list(value) for key, value in places.items()}
    tries = 20000
    for number in range(tries):
        key = draw.randrange(halves), draw.randrange(rows)
        one, two = draw.sample(range(rows), 2)
        own = places[key]
        change = move(key, one, -1) + move(key, two, -1)
        own[one], own[two] = own[two], own[one]
        change += move(key, one, 1) + move(key, two, 1)
        heat = 30.0 * (1 - number / tries) + 0.01
        if change <= 0 or draw.random() < math.exp(-change / heat):
            total += change
            if total < best:
                best, kept = total, {key: list(value) for key, value in places.items()}
        else:
            move(key, one, -1), move(key, two, -1)
            own[one], own[two] = own[two], own[one]
            move(key, one, 1), move(key, two, 1)
    return kept


def column_pairs(rows, cols):
    halves = cols // rows
    places = source_places(rows, halves)
    return [
        (g * cols + places[h, g][r] * halves + h, r * cols + g * halves + halves - 1 - h)
        for h in range(halves)
        for g in range(rows)
        for r in range(rows)
    ]


def swap(value, bit, cols):
    return lax.ppermute(value, "col", [(i, i ^ bit) for i in range(cols)])


def gather_panel(panel_pool, panel_block, cols, beside):
    col_place = lax.axis_index("col")
    core = col_place % 2
    half_rows = panel_pool.shape[0] // 2
    mine = lax.dynamic_slice_in_dim(panel_pool, core * half_rows, half_rows, 0)
    got, mine = lax.optimization_barrier((swap(panel_pool, 1, cols), mine))
    got = lax.dynamic_slice_in_dim(got, core * half_rows, half_rows, 0)
    held = jnp.where(panel_block % 2 == core, mine, got)
    apart = panel_block ^ col_place
    low = 2
    while low < cols:
        high = min(4 * low, cols)
        away = apart & (high - low)
        steps = [2 * low, 3 * low, low] if high == 4 * low else [low]
        received = [swap(held, bits, cols) for bits in steps]
        received, beside = lax.optimization_barrier((received, beside))
        for bits, value in zip(steps, received):
            held = jnp.where(away == bits, value, held)
        low = high
    return [held, swap(held, 1, cols)], beside


def on_device(points, panel_pool, order, panel_index, inv_factor, ard_weights, noise):
    row_count, features = points.shape
    panel = inv_factor.shape[0]
    rows = lax.axis_size("row")
    cols = lax.axis_size("col")
    col_count = row_count * rows // cols
    halves = cols // rows
    col_place = lax.axis_index("col")
    part = halves - 1 - col_place % halves
    own_half = lax.dynamic_slice_in_dim(points, part * col_count, col_count, 0)
    sent = lax.ppermute(own_half, ("row", "col"), column_pairs(rows, cols))
    vectors = jnp.concatenate([order.astype(f32), ard_weights, noise])[None, :]
    pieces, vectors = gather_panel(panel_pool, panel_index[0], cols, vectors)

    packed = 4 * features
    factor_left, factor_right, pick, left, left_half = pl.pallas_call(
        parts_kernel,
        out_shape=[
            shape((panel, 3 * panel), bf16),
            shape((3 * panel, panel), bf16),
            shape((panel, panel), bf16),
            shape((row_count, packed), bf16),
            shape((row_count, 1)),
        ],
        **compute_params(10**8, 4 * 10**6),
    )(inv_factor, points, vectors)

    rows_left, chosen, chosen_half = pl.pallas_call(
        rows_kernel,
        out_shape=[shape((row_count, 3 * panel), bf16), shape((panel, packed), bf16), shape((panel, 1))],
        scratch_shapes=[pltpu.VMEM((row_count, 3 * panel), bf16)],
        **compute_params(1, 1),
    )(*pieces, vectors, factor_right, pick, left, left_half)

    chunks = 4
    return pl.pallas_call(
        functools.partial(update_kernel, rows, cols),
        out_shape=shape((row_count, col_count)),
        out_specs=pl.BlockSpec(memory_space=pl.ANY),
        scratch_shapes=[
            pltpu.VMEM((chunks, row_count // chunks, col_count), f32),
            pltpu.VMEM((3 * panel, col_count), bf16),
            pltpu.VMEM((3 * panel, col_count), bf16),
            pltpu.SemaphoreType.DMA((chunks,)),
        ],
        **compute_params(4 * 10**9, 8 * 10**6),
    )(sent, vectors, factor_left, left, left_half, rows_left, chosen, chosen_half)


def solution(mesh):
    in_specs = (P("row", None), P("col", None), P(), P(), P(), P(), P("row"))
    out_specs = P("row", "col")
    return jax.shard_map(
        on_device, mesh=mesh, in_specs=in_specs, out_specs=out_specs, check_vma=False
    )
```

```python
import collections
import functools
import math
import random

import jax
import jax.numpy as jnp
from jax import lax
from jax.experimental import pallas as pl
from jax.experimental.pallas import tpu as pltpu
from jax.sharding import PartitionSpec as P

log2_e = 1.4426950408889634
vmem_bytes = 32 * 1024 * 1024
f32, bf16 = jnp.float32, jnp.bfloat16
block, square = 256, 128


def halves_of(value):
    high = value.astype(bf16)
    low = (value - high.astype(f32)).astype(bf16)
    return high, low


def pack_left(high, low):
    return jnp.concatenate([high, low, high, low], axis=1)


def pack_right(high, low):
    return jnp.concatenate([high, low, low, high], axis=0)


def half_square(high, low, axis):
    value = high.astype(f32) + low.astype(f32)
    return 0.5 * jnp.sum(value * value, axis=axis, keepdims=True)


def product(left, right):
    return lax.dot_general(left, right, (((1,), (0,)), ((), ())), preferred_element_type=f32)


def store_left(ref, rows, first, value):
    high, low = halves_of(value)
    for start in range(0, value.shape[1], block):
        now, at = slice(start, start + block), 3 * (first + start)
        ref[rows, at : at + block] = high[:, now]
        ref[rows, at + block : at + 2 * block] = high[:, now]
        ref[rows, at + 2 * block : at + 3 * block] = low[:, now]


def store_right(ref, first, value):
    high, low = halves_of(value)
    for start in range(0, value.shape[0], block):
        now, at = slice(start, start + block), 3 * (first + start)
        ref[at : at + block, :] = high[now]
        ref[at + block : at + 2 * block, :] = low[now]
        ref[at + 2 * block : at + 3 * block, :] = high[now]


def kern(crossed, left_half, right_half):
    return jnp.exp2((crossed - left_half) - (right_half - 1.0))


def scale_of(vectors_ref, panel, features):
    return jnp.sqrt(vectors_ref[:, panel : panel + features] * log2_e)


def parts_kernel(
    factor_ref, points_ref, vectors_ref, factor_left_ref, factor_right_ref, pick_ref, left_ref,
    left_half_ref,
):
    factor = factor_ref[...]
    store_left(factor_left_ref, slice(None), 0, factor)
    store_right(factor_right_ref, 0, jnp.transpose(factor))
    panel = factor.shape[0]
    core = lax.axis_index("col") % 2
    place = lax.broadcasted_iota(jnp.int32, (panel, panel), 0) + core * (panel // 2)
    place = jnp.where(place >= panel, place - panel, place).astype(f32)
    hit = jnp.where(place == vectors_ref[:, :panel], 1.0, 0.0).astype(f32)
    pick_ref[...] = jnp.transpose(hit).astype(bf16)
    high, low = halves_of(points_ref[...] * scale_of(vectors_ref, panel, points_ref.shape[1]))
    left_ref[...] = pack_left(high, low)
    left_half_ref[...] = half_square(high, low, 1)


def rows_kernel(
    own_ref, other_ref, vectors_ref, factor_right_ref, pick_ref, left_ref, left_half_ref,
    rows_ref, chosen_ref, chosen_half_ref, kern_ref,
):
    panel = pick_ref.shape[0]
    features = own_ref.shape[1]
    held = jnp.concatenate([own_ref[...], other_ref[...]], axis=0) * scale_of(vectors_ref, panel, features)
    chosen = product(pick_ref[...], jnp.concatenate(halves_of(held), axis=1))
    high, low = chosen[:, :features].astype(bf16), chosen[:, features:].astype(bf16)
    chosen_ref[...] = pack_left(high, low)
    chosen_half_ref[...] = half_square(high, low, 1)
    turned = jnp.transpose(chosen)
    high, low = turned[:features].astype(bf16), turned[features:].astype(bf16)
    right = pack_right(high, low)
    right_half = half_square(high, low, 0)
    chunks = 2
    count = left_ref.shape[0] // chunks
    places = [slice(number * count, (number + 1) * count) for number in range(chunks)]
    crossed = [product(left_ref[place, :], right) for place in places]
    for number, place in enumerate(places):
        store_left(kern_ref, place, 0, kern(crossed[number], left_half_ref[place, :], right_half))
        for first in range(0, panel, block):
            last = first + block
            part = product(kern_ref[place, : 3 * last], factor_right_ref[: 3 * last, first:last])
            store_left(rows_ref, place, first, part)


def update_kernel(
    rows, cols, sent_ref, vectors_ref, factor_left_ref, left_ref, left_half_ref, rows_ref, chosen_ref,
    chosen_half_ref, out_ref, block_ref, kern_ref, cols_ref, sems,
):
    row_place, col_place = lax.axis_index("row"), lax.axis_index("col")
    halves = cols // rows
    count = sent_ref.shape[0]
    part = col_place % halves
    own = row_place == col_place // halves
    panel, features = factor_left_ref.shape[0], sent_ref.shape[1]

    high, low = halves_of(jnp.transpose(sent_ref[...] * scale_of(vectors_ref, panel, features)))
    right = pack_right(high, low)
    right_half = half_square(high, low, 0)
    chunks, chunk = block_ref.shape[:2]
    places = [slice(number * chunk, (number + 1) * chunk) for number in range(chunks)]
    at = pl.multiple_of(panel + features + part * count, 128)
    noise = jnp.where(own, vectors_ref[:, pl.ds(at, count)], 0.0)
    ids = (square, square)
    on_diagonal = lax.broadcasted_iota(jnp.int32, ids, 0) == lax.broadcasted_iota(jnp.int32, ids, 1)

    crossed = product(chosen_ref[...], right)
    tiles = [product(left_ref[place, :], right) for place in places]
    store_right(kern_ref, 0, kern(crossed, chosen_half_ref[...], right_half))
    for first in range(0, panel, block):
        last = first + block
        store_right(cols_ref, first, product(factor_left_ref[first:last, : 3 * last], kern_ref[: 3 * last, :]))
    copies = []
    for number, place in enumerate(places):
        update = product(rows_ref[place, :], cols_ref[...])
        block_ref[number] = kern(tiles[number], left_half_ref[place, :], right_half) - update
        here = jnp.where(part == place.start // count, noise, 0.0)
        for start in range(0, chunk, square):
            first = place.start % count + start
            now, across = slice(start, start + square), slice(first, first + square)
            block_ref[number, now, across] += jnp.where(on_diagonal, here[:, across], 0.0)
        copy = pltpu.make_async_copy(block_ref.at[number], out_ref.at[pl.ds(number * chunk, chunk)], sems.at[number])
        copy.start()
        copies.append(copy)
    for copy in copies:
        copy.wait()


def shape(dims, kind=f32):
    return jax.ShapeDtypeStruct(dims, kind)


def compute_params(flops, moved):
    return dict(
        compiler_params=pltpu.CompilerParams(vmem_limit_bytes=vmem_bytes),
        cost_estimate=pl.CostEstimate(flops=flops, bytes_accessed=moved, transcendentals=0),
    )


def links_of(place, group, target_row, across):
    links = []
    step = 1 if target_row > group else -1
    links += [(0, place, z, step) for z in range(group, target_row, step)]
    (x, y), (end_x, end_y) = (place % across, place // across), (group % across, group // across)
    step = 1 if end_x > x else -1
    links += [(1, target_row, y, at, step) for at in range(x, end_x, step)]
    step = 1 if end_y > y else -1
    links += [(2, target_row, end_x, at, step) for at in range(y, end_y, step)]
    return links


def source_places(rows, halves):
    draw = random.Random(4)
    across = math.isqrt(rows)
    places = {}
    load = collections.Counter()

    def move(key, r, sign):
        change = 0
        early = (1 + 2 * r / rows) * (0 <= r - key[1] <= 1)
        for link in links_of(places[key][r], key[1], r, across):
            old = load[link]
            load[link] = old + sign
            change += (old + sign) ** 4 - old**4 + sign * early * (link[0] == 2)
        return change

    for h in range(halves):
        for g in range(rows):
            places[h, g] = draw.sample(range(rows), rows)
            for r in range(rows):
                move((h, g), r, 1)
    best, total, kept = 0, 0, {key: list(value) for key, value in places.items()}
    tries = 20000
    for number in range(tries):
        key = draw.randrange(halves), draw.randrange(rows)
        one, two = draw.sample(range(rows), 2)
        own = places[key]
        change = move(key, one, -1) + move(key, two, -1)
        own[one], own[two] = own[two], own[one]
        change += move(key, one, 1) + move(key, two, 1)
        heat = 30.0 * (1 - number / tries) + 0.01
        if change <= 0 or draw.random() < math.exp(-change / heat):
            total += change
            if total < best:
                best, kept = total, {key: list(value) for key, value in places.items()}
        else:
            move(key, one, -1), move(key, two, -1)
            own[one], own[two] = own[two], own[one]
            move(key, one, 1), move(key, two, 1)
    return kept


def column_pairs(rows, cols):
    halves = cols // rows
    places = source_places(rows, halves)
    return [
        (g * cols + places[h, g][r] * halves + h, r * cols + g * halves + halves - 1 - h)
        for h in range(halves)
        for g in range(rows)
        for r in range(rows)
    ]


def swap(value, bit, cols):
    return lax.ppermute(value, "col", [(i, i ^ bit) for i in range(cols)])


def gather_panel(panel_pool, panel_block, cols, beside):
    col_place = lax.axis_index("col")
    core = col_place % 2
    half_rows = panel_pool.shape[0] // 2
    mine = lax.dynamic_slice_in_dim(panel_pool, core * half_rows, half_rows, 0)
    got, mine = lax.optimization_barrier((swap(panel_pool, 1, cols), mine))
    got = lax.dynamic_slice_in_dim(got, core * half_rows, half_rows, 0)
    held = jnp.where(panel_block % 2 == core, mine, got)
    apart = panel_block ^ col_place
    low = 2
    while low < cols:
        high = min(4 * low, cols)
        away = apart & (high - low)
        steps = range(high - low, 0, -low)
        received = [swap(held, bits, cols) for bits in steps]
        received, beside = lax.optimization_barrier((received, beside))
        for bits, value in zip(steps, received):
            held = jnp.where(away == bits, value, held)
        low = high
    return [held, swap(held, 1, cols)], beside


def on_device(points, panel_pool, order, panel_index, inv_factor, ard_weights, noise):
    row_count, features = points.shape
    panel = inv_factor.shape[0]
    rows = lax.axis_size("row")
    cols = lax.axis_size("col")
    col_count = row_count * rows // cols
    halves = cols // rows
    col_place = lax.axis_index("col")
    part = halves - 1 - col_place % halves
    own_half = lax.dynamic_slice_in_dim(points, part * col_count, col_count, 0)
    sent = lax.ppermute(own_half, ("row", "col"), column_pairs(rows, cols))
    vectors = jnp.concatenate([order.astype(f32), ard_weights, noise])[None, :]
    pieces, vectors = gather_panel(panel_pool, panel_index[0], cols, vectors)

    packed = 4 * features
    factor_left, factor_right, pick, left, left_half = pl.pallas_call(
        parts_kernel,
        out_shape=[
            shape((panel, 3 * panel), bf16),
            shape((3 * panel, panel), bf16),
            shape((panel, panel), bf16),
            shape((row_count, packed), bf16),
            shape((row_count, 1)),
        ],
        **compute_params(10**8, 4 * 10**6),
    )(inv_factor, points, vectors)

    rows_left, chosen, chosen_half = pl.pallas_call(
        rows_kernel,
        out_shape=[shape((row_count, 3 * panel), bf16), shape((panel, packed), bf16), shape((panel, 1))],
        scratch_shapes=[pltpu.VMEM((row_count, 3 * panel), bf16)],
        **compute_params(1, 1),
    )(*pieces, vectors, factor_right, pick, left, left_half)

    chunks = 4
    return pl.pallas_call(
        functools.partial(update_kernel, rows, cols),
        out_shape=shape((row_count, col_count)),
        out_specs=pl.BlockSpec(memory_space=pl.ANY),
        scratch_shapes=[
            pltpu.VMEM((chunks, row_count // chunks, col_count), f32),
            pltpu.VMEM((3 * panel, col_count), bf16),
            pltpu.VMEM((3 * panel, col_count), bf16),
            pltpu.SemaphoreType.DMA((chunks,)),
        ],
        **compute_params(4 * 10**9, 8 * 10**6),
    )(sent, vectors, factor_left, left, left_half, rows_left, chosen, chosen_half)


def solution(mesh):
    in_specs = (P("row", None), P("col", None), P(), P(), P(), P(), P("row"))
    out_specs = P("row", "col")
    return jax.shard_map(
        on_device, mesh=mesh, in_specs=in_specs, out_specs=out_specs, check_vma=False
    )
```

```python
import collections
import functools
import math
import random

import jax
import jax.numpy as jnp
from jax import lax
from jax.experimental import pallas as pl
from jax.experimental.pallas import tpu as pltpu
from jax.sharding import PartitionSpec as P

log2_e = 1.4426950408889634
vmem_bytes = 32 * 1024 * 1024
f32, bf16 = jnp.float32, jnp.bfloat16
block, square = 256, 128


def halves_of(value):
    high = value.astype(bf16)
    low = (value - high.astype(f32)).astype(bf16)
    return high, low


def pack_left(high, low):
    return jnp.concatenate([high, low, high, low], axis=1)


def pack_right(high, low):
    return jnp.concatenate([high, low, low, high], axis=0)


def half_square(high, low, axis):
    value = high.astype(f32) + low.astype(f32)
    return 0.5 * jnp.sum(value * value, axis=axis, keepdims=True)


def product(left, right):
    return lax.dot_general(left, right, (((1,), (0,)), ((), ())), preferred_element_type=f32)


def store_left(ref, rows, first, value):
    high, low = halves_of(value)
    for start in range(0, value.shape[1], block):
        now, at = slice(start, start + block), 3 * (first + start)
        ref[rows, at : at + block] = high[:, now]
        ref[rows, at + block : at + 2 * block] = high[:, now]
        ref[rows, at + 2 * block : at + 3 * block] = low[:, now]


def store_right(ref, first, value):
    high, low = halves_of(value)
    for start in range(0, value.shape[0], block):
        now, at = slice(start, start + block), 3 * (first + start)
        ref[at : at + block, :] = high[now]
        ref[at + block : at + 2 * block, :] = low[now]
        ref[at + 2 * block : at + 3 * block, :] = high[now]


def kern(crossed, left_half, right_half):
    return jnp.exp2((crossed - left_half) - (right_half - 1.0))


def scale_of(vectors_ref, panel, features):
    return jnp.sqrt(vectors_ref[:, panel : panel + features] * log2_e)


def parts_kernel(
    factor_ref, points_ref, vectors_ref, factor_left_ref, factor_right_ref, pick_ref, left_ref,
    left_half_ref,
):
    factor = factor_ref[...]
    store_left(factor_left_ref, slice(None), 0, factor)
    store_right(factor_right_ref, 0, jnp.transpose(factor))
    panel = factor.shape[0]
    core = lax.axis_index("col") % 2
    place = lax.broadcasted_iota(jnp.int32, (panel, panel), 0) + core * (panel // 2)
    place = jnp.where(place >= panel, place - panel, place).astype(f32)
    hit = jnp.where(place == vectors_ref[:, :panel], 1.0, 0.0).astype(f32)
    pick_ref[...] = jnp.transpose(hit).astype(bf16)
    high, low = halves_of(points_ref[...] * scale_of(vectors_ref, panel, points_ref.shape[1]))
    left_ref[...] = pack_left(high, low)
    left_half_ref[...] = half_square(high, low, 1)


def rows_kernel(
    own_ref, other_ref, vectors_ref, factor_right_ref, pick_ref, left_ref, left_half_ref,
    rows_ref, chosen_ref, chosen_half_ref, kern_ref,
):
    panel = pick_ref.shape[0]
    features = own_ref.shape[1]
    held = jnp.concatenate([own_ref[...], other_ref[...]], axis=0) * scale_of(vectors_ref, panel, features)
    chosen = product(pick_ref[...], jnp.concatenate(halves_of(held), axis=1))
    high, low = chosen[:, :features].astype(bf16), chosen[:, features:].astype(bf16)
    chosen_ref[...] = pack_left(high, low)
    chosen_half_ref[...] = half_square(high, low, 1)
    turned = jnp.transpose(chosen)
    high, low = turned[:features].astype(bf16), turned[features:].astype(bf16)
    right = pack_right(high, low)
    right_half = half_square(high, low, 0)
    chunks = 2
    count = left_ref.shape[0] // chunks
    places = [slice(number * count, (number + 1) * count) for number in range(chunks)]
    crossed = [product(left_ref[place, :], right) for place in places]
    for number, place in enumerate(places):
        store_left(kern_ref, place, 0, kern(crossed[number], left_half_ref[place, :], right_half))
        for first in range(0, panel, block):
            last = first + block
            part = product(kern_ref[place, : 3 * last], factor_right_ref[: 3 * last, first:last])
            store_left(rows_ref, place, first, part)


def update_kernel(
    rows, cols, sent_ref, vectors_ref, factor_left_ref, left_ref, left_half_ref, rows_ref, chosen_ref,
    chosen_half_ref, out_ref, block_ref, kern_ref, cols_ref, sems,
):
    row_place, col_place = lax.axis_index("row"), lax.axis_index("col")
    halves = cols // rows
    count = sent_ref.shape[0]
    part = col_place % halves
    own = row_place == col_place // halves
    panel, features = factor_left_ref.shape[0], sent_ref.shape[1]

    high, low = halves_of(jnp.transpose(sent_ref[...] * scale_of(vectors_ref, panel, features)))
    right = pack_right(high, low)
    right_half = half_square(high, low, 0)
    chunks, chunk = block_ref.shape[:2]
    places = [slice(number * chunk, (number + 1) * chunk) for number in range(chunks)]
    at = pl.multiple_of(panel + features + part * count, 128)
    noise = jnp.where(own, vectors_ref[:, pl.ds(at, count)], 0.0)
    ids = (square, square)
    on_diagonal = lax.broadcasted_iota(jnp.int32, ids, 0) == lax.broadcasted_iota(jnp.int32, ids, 1)

    crossed = product(chosen_ref[...], right)
    tiles = [product(left_ref[place, :], right) for place in places]
    store_right(kern_ref, 0, kern(crossed, chosen_half_ref[...], right_half))
    for first in range(0, panel, block):
        last = first + block
        store_right(cols_ref, first, product(factor_left_ref[first:last, : 3 * last], kern_ref[: 3 * last, :]))
    copies = []
    for number, place in enumerate(places):
        update = product(rows_ref[place, :], cols_ref[...])
        block_ref[number] = kern(tiles[number], left_half_ref[place, :], right_half) - update
        here = jnp.where(part == place.start // count, noise, 0.0)
        for start in range(0, chunk, square):
            first = place.start % count + start
            now, across = slice(start, start + square), slice(first, first + square)
            block_ref[number, now, across] += jnp.where(on_diagonal, here[:, across], 0.0)
        copy = pltpu.make_async_copy(block_ref.at[number], out_ref.at[pl.ds(number * chunk, chunk)], sems.at[number])
        copy.start()
        copies.append(copy)
    for copy in copies:
        copy.wait()


def shape(dims, kind=f32):
    return jax.ShapeDtypeStruct(dims, kind)


def compute_params(flops, moved):
    return dict(
        compiler_params=pltpu.CompilerParams(vmem_limit_bytes=vmem_bytes),
        cost_estimate=pl.CostEstimate(flops=flops, bytes_accessed=moved, transcendentals=0),
    )


def links_of(place, group, target_row, across):
    links = []
    step = 1 if target_row > group else -1
    links += [(0, place, z, step) for z in range(group, target_row, step)]
    (x, y), (end_x, end_y) = (place % across, place // across), (group % across, group // across)
    step = 1 if end_x > x else -1
    links += [(1, target_row, y, at, step) for at in range(x, end_x, step)]
    step = 1 if end_y > y else -1
    links += [(2, target_row, end_x, at, step) for at in range(y, end_y, step)]
    return links


def source_places(rows, halves):
    draw = random.Random(5)
    across = math.isqrt(rows)
    places = {}
    load = collections.Counter()

    def move(key, r, sign):
        change = 0
        for link in links_of(places[key][r], key[1], r, across):
            old = load[link]
            load[link] = old + sign
            change += (old + sign) ** 4 - old**4
        return change

    for h in range(halves):
        for g in range(rows):
            places[h, g] = draw.sample(range(rows), rows)
            for r in range(rows):
                move((h, g), r, 1)
    best, total, kept = 0, 0, {key: list(value) for key, value in places.items()}
    tries = 20000
    for number in range(tries):
        key = draw.randrange(halves), draw.randrange(rows)
        one, two = draw.sample(range(rows), 2)
        own = places[key]
        change = move(key, one, -1) + move(key, two, -1)
        own[one], own[two] = own[two], own[one]
        change += move(key, one, 1) + move(key, two, 1)
        heat = 30.0 * (1 - number / tries) + 0.01
        if change <= 0 or draw.random() < math.exp(-change / heat):
            total += change
            if total < best:
                best, kept = total, {key: list(value) for key, value in places.items()}
        else:
            move(key, one, -1), move(key, two, -1)
            own[one], own[two] = own[two], own[one]
            move(key, one, 1), move(key, two, 1)
    return kept


def column_pairs(rows, cols):
    halves = cols // rows
    places = source_places(rows, halves)
    return [
        (g * cols + places[h, g][r] * halves + h, r * cols + g * halves + halves - 1 - h)
        for h in range(halves)
        for g in range(rows)
        for r in range(rows)
    ]


def swap(value, bit, cols):
    return lax.ppermute(value, "col", [(i, i ^ bit) for i in range(cols)])


def gather_panel(panel_pool, panel_block, cols, beside):
    col_place = lax.axis_index("col")
    core = col_place % 2
    half_rows = panel_pool.shape[0] // 2
    mine = lax.dynamic_slice_in_dim(panel_pool, core * half_rows, half_rows, 0)
    got, mine = lax.optimization_barrier((swap(panel_pool, 1, cols), mine))
    got = lax.dynamic_slice_in_dim(got, core * half_rows, half_rows, 0)
    held = jnp.where(panel_block % 2 == core, mine, got)
    apart = panel_block ^ col_place
    bits = [2**k for k in range(1, cols.bit_length() - 1)]
    turn = len(bits) // 2
    for bit, other_bit in zip(bits, bits[turn:] + bits[:turn]):
        pairs = [(i, i ^ (other_bit if i % 2 else bit)) for i in range(cols)]
        got = lax.ppermute(held, "col", pairs)
        got, beside = lax.optimization_barrier((got, beside))
        held = jnp.where(apart & jnp.where(core == 0, bit, other_bit) == 0, held, got)
    return [held, swap(held, 1, cols)], beside


def on_device(points, panel_pool, order, panel_index, inv_factor, ard_weights, noise):
    row_count, features = points.shape
    panel = inv_factor.shape[0]
    rows = lax.axis_size("row")
    cols = lax.axis_size("col")
    col_count = row_count * rows // cols
    halves = cols // rows
    col_place = lax.axis_index("col")
    part = halves - 1 - col_place % halves
    own_half = lax.dynamic_slice_in_dim(points, part * col_count, col_count, 0)
    vectors = jnp.concatenate([order.astype(f32), ard_weights, noise])[None, :]
    pieces, vectors = gather_panel(panel_pool, panel_index[0], cols, vectors)
    sent = lax.ppermute(own_half, ("row", "col"), column_pairs(rows, cols))

    packed = 4 * features
    factor_left, factor_right, pick, left, left_half = pl.pallas_call(
        parts_kernel,
        out_shape=[
            shape((panel, 3 * panel), bf16),
            shape((3 * panel, panel), bf16),
            shape((panel, panel), bf16),
            shape((row_count, packed), bf16),
            shape((row_count, 1)),
        ],
        **compute_params(10**8, 4 * 10**6),
    )(inv_factor, points, vectors)

    rows_left, chosen, chosen_half = pl.pallas_call(
        rows_kernel,
        out_shape=[shape((row_count, 3 * panel), bf16), shape((panel, packed), bf16), shape((panel, 1))],
        scratch_shapes=[pltpu.VMEM((row_count, 3 * panel), bf16)],
        **compute_params(1, 1),
    )(*pieces, vectors, factor_right, pick, left, left_half)

    chunks = 4
    return pl.pallas_call(
        functools.partial(update_kernel, rows, cols),
        out_shape=shape((row_count, col_count)),
        out_specs=pl.BlockSpec(memory_space=pl.ANY),
        scratch_shapes=[
            pltpu.VMEM((chunks, row_count // chunks, col_count), f32),
            pltpu.VMEM((3 * panel, col_count), bf16),
            pltpu.VMEM((3 * panel, col_count), bf16),
            pltpu.SemaphoreType.DMA((chunks,)),
        ],
        **compute_params(4 * 10**9, 8 * 10**6),
    )(sent, vectors, factor_left, left, left_half, rows_left, chosen, chosen_half)


def solution(mesh):
    in_specs = (P("row", None), P("col", None), P(), P(), P(), P(), P("row"))
    out_specs = P("row", "col")
    return jax.shard_map(
        on_device, mesh=mesh, in_specs=in_specs, out_specs=out_specs, check_vma=False
    )
```

```python
import collections
import functools
import math
import random

import jax
import jax.numpy as jnp
from jax import lax
from jax.experimental import pallas as pl
from jax.experimental.pallas import tpu as pltpu
from jax.sharding import PartitionSpec as P

log2_e = 1.4426950408889634
vmem_bytes = 32 * 1024 * 1024
f32, bf16 = jnp.float32, jnp.bfloat16
block, square = 256, 128


def halves_of(value):
    high = value.astype(bf16)
    low = (value - high.astype(f32)).astype(bf16)
    return high, low


def pack_left(high, low):
    return jnp.concatenate([high, low, high, low], axis=1)


def pack_right(high, low):
    return jnp.concatenate([high, low, low, high], axis=0)


def half_square(high, low, axis):
    value = high.astype(f32) + low.astype(f32)
    return 0.5 * jnp.sum(value * value, axis=axis, keepdims=True)


def product(left, right):
    return lax.dot_general(left, right, (((1,), (0,)), ((), ())), preferred_element_type=f32)


def store_left(ref, rows, first, value):
    high, low = halves_of(value)
    for start in range(0, value.shape[1], block):
        now, at = slice(start, start + block), 3 * (first + start)
        ref[rows, at : at + block] = high[:, now]
        ref[rows, at + block : at + 2 * block] = high[:, now]
        ref[rows, at + 2 * block : at + 3 * block] = low[:, now]


def store_right(ref, first, value):
    high, low = halves_of(value)
    for start in range(0, value.shape[0], block):
        now, at = slice(start, start + block), 3 * (first + start)
        ref[at : at + block, :] = high[now]
        ref[at + block : at + 2 * block, :] = low[now]
        ref[at + 2 * block : at + 3 * block, :] = high[now]


def kern(crossed, left_half, right_half):
    return jnp.exp2((crossed - left_half) - (right_half - 1.0))


def scale_of(vectors_ref, panel, features):
    return jnp.sqrt(vectors_ref[:, panel : panel + features] * log2_e)


def parts_kernel(
    factor_ref, points_ref, vectors_ref, factor_left_ref, factor_right_ref, pick_ref, left_ref,
    left_half_ref,
):
    factor = factor_ref[...]
    store_left(factor_left_ref, slice(None), 0, factor)
    store_right(factor_right_ref, 0, jnp.transpose(factor))
    panel = factor.shape[0]
    core = lax.axis_index("col") % 2
    place = lax.broadcasted_iota(jnp.int32, (panel, panel), 0) + core * (panel // 2)
    place = jnp.where(place >= panel, place - panel, place).astype(f32)
    hit = jnp.where(place == vectors_ref[:, :panel], 1.0, 0.0).astype(f32)
    pick_ref[...] = jnp.transpose(hit).astype(bf16)
    high, low = halves_of(points_ref[...] * scale_of(vectors_ref, panel, points_ref.shape[1]))
    left_ref[...] = pack_left(high, low)
    left_half_ref[...] = half_square(high, low, 1)


def rows_kernel(
    own_ref, other_ref, vectors_ref, factor_right_ref, pick_ref, left_ref, left_half_ref,
    rows_ref, chosen_ref, chosen_half_ref, kern_ref,
):
    panel = pick_ref.shape[0]
    features = own_ref.shape[1]
    held = jnp.concatenate([own_ref[...], other_ref[...]], axis=0) * scale_of(vectors_ref, panel, features)
    chosen = product(pick_ref[...], jnp.concatenate(halves_of(held), axis=1))
    high, low = chosen[:, :features].astype(bf16), chosen[:, features:].astype(bf16)
    chosen_ref[...] = pack_left(high, low)
    chosen_half_ref[...] = half_square(high, low, 1)
    turned = jnp.transpose(chosen)
    high, low = turned[:features].astype(bf16), turned[features:].astype(bf16)
    right = pack_right(high, low)
    right_half = half_square(high, low, 0)
    chunks = 2
    count = left_ref.shape[0] // chunks
    places = [slice(number * count, (number + 1) * count) for number in range(chunks)]
    crossed = [product(left_ref[place, :], right) for place in places]
    for number, place in enumerate(places):
        store_left(kern_ref, place, 0, kern(crossed[number], left_half_ref[place, :], right_half))
        for first in range(0, panel, block):
            last = first + block
            part = product(kern_ref[place, : 3 * last], factor_right_ref[: 3 * last, first:last])
            store_left(rows_ref, place, first, part)


def update_kernel(
    rows, cols, sent_ref, vectors_ref, factor_left_ref, left_ref, left_half_ref, rows_ref, chosen_ref,
    chosen_half_ref, out_ref, block_ref, kern_ref, cols_ref, sems,
):
    row_place, col_place = lax.axis_index("row"), lax.axis_index("col")
    halves = cols // rows
    count = sent_ref.shape[0]
    part = col_place % halves
    own = row_place == col_place // halves
    panel, features = factor_left_ref.shape[0], sent_ref.shape[1]

    high, low = halves_of(jnp.transpose(sent_ref[...] * scale_of(vectors_ref, panel, features)))
    right = pack_right(high, low)
    right_half = half_square(high, low, 0)
    chunks, chunk = block_ref.shape[:2]
    places = [slice(number * chunk, (number + 1) * chunk) for number in range(chunks)]
    at = pl.multiple_of(panel + features + part * count, 128)
    noise = jnp.where(own, vectors_ref[:, pl.ds(at, count)], 0.0)
    ids = (square, square)
    on_diagonal = lax.broadcasted_iota(jnp.int32, ids, 0) == lax.broadcasted_iota(jnp.int32, ids, 1)

    crossed = product(chosen_ref[...], right)
    tiles = [product(left_ref[place, :], right) for place in places]
    store_right(kern_ref, 0, kern(crossed, chosen_half_ref[...], right_half))
    for first in range(0, panel, block):
        last = first + block
        store_right(cols_ref, first, product(factor_left_ref[first:last, : 3 * last], kern_ref[: 3 * last, :]))
    copies = []
    for number, place in enumerate(places):
        update = product(rows_ref[place, :], cols_ref[...])
        block_ref[number] = kern(tiles[number], left_half_ref[place, :], right_half) - update
        here = jnp.where(part == place.start // count, noise, 0.0)
        for start in range(0, chunk, square):
            first = place.start % count + start
            now, across = slice(start, start + square), slice(first, first + square)
            block_ref[number, now, across] += jnp.where(on_diagonal, here[:, across], 0.0)
        copy = pltpu.make_async_copy(block_ref.at[number], out_ref.at[pl.ds(number * chunk, chunk)], sems.at[number])
        copy.start()
        copies.append(copy)
    for copy in copies:
        copy.wait()


def shape(dims, kind=f32):
    return jax.ShapeDtypeStruct(dims, kind)


def compute_params(flops, moved):
    return dict(
        compiler_params=pltpu.CompilerParams(vmem_limit_bytes=vmem_bytes),
        cost_estimate=pl.CostEstimate(flops=flops, bytes_accessed=moved, transcendentals=0),
    )


def links_of(place, group, target_row, across):
    links = []
    step = 1 if target_row > group else -1
    links += [(0, place, z, step) for z in range(group, target_row, step)]
    (x, y), (end_x, end_y) = (place % across, place // across), (group % across, group // across)
    step = 1 if end_x > x else -1
    links += [(1, target_row, y, at, step) for at in range(x, end_x, step)]
    step = 1 if end_y > y else -1
    links += [(2, target_row, end_x, at, step) for at in range(y, end_y, step)]
    return links


def source_places(rows, halves):
    draw = random.Random(5)
    across = math.isqrt(rows)
    places = {}
    load = collections.Counter()

    def move(key, r, sign):
        change = 0
        for link in links_of(places[key][r], key[1], r, across):
            old = load[link]
            load[link] = old + sign
            change += (old + sign) ** 4 - old**4
        return change

    for h in range(halves):
        for g in range(rows):
            places[h, g] = draw.sample(range(rows), rows)
            for r in range(rows):
                move((h, g), r, 1)
    best, total, kept = 0, 0, {key: list(value) for key, value in places.items()}
    tries = 20000
    for number in range(tries):
        key = draw.randrange(halves), draw.randrange(rows)
        one, two = draw.sample(range(rows), 2)
        own = places[key]
        change = move(key, one, -1) + move(key, two, -1)
        own[one], own[two] = own[two], own[one]
        change += move(key, one, 1) + move(key, two, 1)
        heat = 30.0 * (1 - number / tries) + 0.01
        if change <= 0 or draw.random() < math.exp(-change / heat):
            total += change
            if total < best:
                best, kept = total, {key: list(value) for key, value in places.items()}
        else:
            move(key, one, -1), move(key, two, -1)
            own[one], own[two] = own[two], own[one]
            move(key, one, 1), move(key, two, 1)
    return kept


def column_pairs(rows, cols):
    halves = cols // rows
    places = source_places(rows, halves)
    return [
        (g * cols + places[h, g][r] * halves + h, r * cols + g * halves + halves - 1 - h)
        for h in range(halves)
        for g in range(rows)
        for r in range(rows)
    ]


def swap(value, bit, cols):
    return lax.ppermute(value, "col", [(i, i ^ bit) for i in range(cols)])


def gather_panel(panel_pool, panel_block, cols, beside):
    col_place = lax.axis_index("col")
    core = col_place % 2
    half_rows = panel_pool.shape[0] // 2
    mine = lax.dynamic_slice_in_dim(panel_pool, core * half_rows, half_rows, 0)
    got, mine = lax.optimization_barrier((swap(panel_pool, 1, cols), mine))
    got = lax.dynamic_slice_in_dim(got, core * half_rows, half_rows, 0)
    held = jnp.where(panel_block % 2 == core, mine, got)
    apart = panel_block ^ col_place
    low = 2
    while low < cols:
        high = min(4 * low, cols)
        away = apart & (high - low)
        steps = range(high - low, 0, -low)
        received = [swap(held, bits, cols) for bits in steps]
        received, beside = lax.optimization_barrier((received, beside))
        for bits, value in zip(steps, received):
            held = jnp.where(away == bits, value, held)
        low = high
    return [held, swap(held, 1, cols)], beside


def on_device(points, panel_pool, order, panel_index, inv_factor, ard_weights, noise):
    row_count, features = points.shape
    panel = inv_factor.shape[0]
    rows = lax.axis_size("row")
    cols = lax.axis_size("col")
    col_count = row_count * rows // cols
    halves = cols // rows
    col_place = lax.axis_index("col")
    part = halves - 1 - col_place % halves
    own_half = lax.dynamic_slice_in_dim(points, part * col_count, col_count, 0)
    sent = lax.ppermute(own_half, ("row", "col"), column_pairs(rows, cols))
    vectors = jnp.concatenate([order.astype(f32), ard_weights, noise])[None, :]
    pieces, vectors = gather_panel(panel_pool, panel_index[0], cols, vectors)

    packed = 4 * features
    factor_left, factor_right, pick, left, left_half = pl.pallas_call(
        parts_kernel,
        out_shape=[
            shape((panel, 3 * panel), bf16),
            shape((3 * panel, panel), bf16),
            shape((panel, panel), bf16),
            shape((row_count, packed), bf16),
            shape((row_count, 1)),
        ],
        **compute_params(10**8, 4 * 10**6),
    )(inv_factor, points, vectors)

    rows_left, chosen, chosen_half = pl.pallas_call(
        rows_kernel,
        out_shape=[shape((row_count, 3 * panel), bf16), shape((panel, packed), bf16), shape((panel, 1))],
        scratch_shapes=[pltpu.VMEM((row_count, 3 * panel), bf16)],
        **compute_params(1, 1),
    )(*pieces, vectors, factor_right, pick, left, left_half)

    chunks = 4
    return pl.pallas_call(
        functools.partial(update_kernel, rows, cols),
        out_shape=shape((row_count, col_count)),
        out_specs=pl.BlockSpec(memory_space=pl.ANY),
        scratch_shapes=[
            pltpu.VMEM((chunks, row_count // chunks, col_count), f32),
            pltpu.VMEM((3 * panel, col_count), bf16),
            pltpu.VMEM((3 * panel, col_count), bf16),
            pltpu.SemaphoreType.DMA((chunks,)),
        ],
        **compute_params(4 * 10**9, 8 * 10**6),
    )(sent, vectors, factor_left, left, left_half, rows_left, chosen, chosen_half)


def solution(mesh):
    in_specs = (P("row", None), P("col", None), P(), P(), P(), P(), P("row"))
    out_specs = P("row", "col")
    return jax.shard_map(
        on_device, mesh=mesh, in_specs=in_specs, out_specs=out_specs, check_vma=False
    )
```

```python
import collections
import functools
import math
import random

import jax
import jax.numpy as jnp
from jax import lax
from jax.experimental import pallas as pl
from jax.experimental.pallas import tpu as pltpu
from jax.sharding import PartitionSpec as P

log2_e = 1.4426950408889634
vmem_bytes = 32 * 1024 * 1024
f32, bf16 = jnp.float32, jnp.bfloat16
block, square = 256, 128


def halves_of(value):
    high = value.astype(bf16)
    low = (value - high.astype(f32)).astype(bf16)
    return high, low


def pack_left(high, low):
    return jnp.concatenate([high, low, high, low], axis=1)


def pack_right(high, low):
    return jnp.concatenate([high, low, low, high], axis=0)


def half_square(high, low, axis):
    value = high.astype(f32) + low.astype(f32)
    return 0.5 * jnp.sum(value * value, axis=axis, keepdims=True)


def product(left, right):
    return lax.dot_general(left, right, (((1,), (0,)), ((), ())), preferred_element_type=f32)


def store_left(ref, rows, first, value):
    high, low = halves_of(value)
    for start in range(0, value.shape[1], block):
        now, at = slice(start, start + block), 3 * (first + start)
        ref[rows, at : at + block] = high[:, now]
        ref[rows, at + block : at + 2 * block] = high[:, now]
        ref[rows, at + 2 * block : at + 3 * block] = low[:, now]


def store_right(ref, first, value):
    high, low = halves_of(value)
    for start in range(0, value.shape[0], block):
        now, at = slice(start, start + block), 3 * (first + start)
        ref[at : at + block, :] = high[now]
        ref[at + block : at + 2 * block, :] = low[now]
        ref[at + 2 * block : at + 3 * block, :] = high[now]


def kern(crossed, left_half, right_half):
    return jnp.exp2((crossed - left_half) - (right_half - 1.0))


def scale_of(vectors_ref, panel, features):
    return jnp.sqrt(vectors_ref[:, panel : panel + features] * log2_e)


def parts_kernel(
    factor_ref, points_ref, vectors_ref, factor_left_ref, factor_right_ref, pick_ref, left_ref,
    left_half_ref,
):
    factor = factor_ref[...]
    store_left(factor_left_ref, slice(None), 0, factor)
    store_right(factor_right_ref, 0, jnp.transpose(factor))
    panel = factor.shape[0]
    core = lax.axis_index("col") % 2
    place = lax.broadcasted_iota(jnp.int32, (panel, panel), 0) + core * (panel // 2)
    place = jnp.where(place >= panel, place - panel, place).astype(f32)
    hit = jnp.where(place == vectors_ref[:, :panel], 1.0, 0.0).astype(f32)
    pick_ref[...] = jnp.transpose(hit).astype(bf16)
    high, low = halves_of(points_ref[...] * scale_of(vectors_ref, panel, points_ref.shape[1]))
    left_ref[...] = pack_left(high, low)
    left_half_ref[...] = half_square(high, low, 1)


def rows_kernel(
    own_ref, other_ref, vectors_ref, factor_right_ref, pick_ref, left_ref, left_half_ref,
    rows_ref, chosen_ref, chosen_half_ref, kern_ref,
):
    panel = pick_ref.shape[0]
    features = own_ref.shape[1]
    held = jnp.concatenate([own_ref[...], other_ref[...]], axis=0) * scale_of(vectors_ref, panel, features)
    chosen = product(pick_ref[...], jnp.concatenate(halves_of(held), axis=1))
    high, low = chosen[:, :features].astype(bf16), chosen[:, features:].astype(bf16)
    chosen_ref[...] = pack_left(high, low)
    chosen_half_ref[...] = half_square(high, low, 1)
    turned = jnp.transpose(chosen)
    high, low = turned[:features].astype(bf16), turned[features:].astype(bf16)
    right = pack_right(high, low)
    right_half = half_square(high, low, 0)
    chunks = 2
    count = left_ref.shape[0] // chunks
    places = [slice(number * count, (number + 1) * count) for number in range(chunks)]
    crossed = [product(left_ref[place, :], right) for place in places]
    for number, place in enumerate(places):
        store_left(kern_ref, place, 0, kern(crossed[number], left_half_ref[place, :], right_half))
        for first in range(0, panel, block):
            last = first + block
            part = product(kern_ref[place, : 3 * last], factor_right_ref[: 3 * last, first:last])
            store_left(rows_ref, place, first, part)


def update_kernel(
    rows, cols, sent_ref, vectors_ref, factor_left_ref, left_ref, left_half_ref, rows_ref, chosen_ref,
    chosen_half_ref, out_ref, block_ref, kern_ref, cols_ref, sems,
):
    row_place, col_place = lax.axis_index("row"), lax.axis_index("col")
    halves = cols // rows
    count = sent_ref.shape[0]
    part = col_place % halves
    own = row_place == col_place // halves
    panel, features = factor_left_ref.shape[0], sent_ref.shape[1]

    high, low = halves_of(jnp.transpose(sent_ref[...] * scale_of(vectors_ref, panel, features)))
    right = pack_right(high, low)
    right_half = half_square(high, low, 0)
    chunks, chunk = block_ref.shape[:2]
    places = [slice(number * chunk, (number + 1) * chunk) for number in range(chunks)]
    at = pl.multiple_of(panel + features + part * count, 128)
    noise = jnp.where(own, vectors_ref[:, pl.ds(at, count)], 0.0)
    ids = (square, square)
    on_diagonal = lax.broadcasted_iota(jnp.int32, ids, 0) == lax.broadcasted_iota(jnp.int32, ids, 1)

    crossed = product(chosen_ref[...], right)
    tiles = [product(left_ref[place, :], right) for place in places]
    store_right(kern_ref, 0, kern(crossed, chosen_half_ref[...], right_half))
    for first in range(0, panel, block):
        last = first + block
        store_right(cols_ref, first, product(factor_left_ref[first:last, : 3 * last], kern_ref[: 3 * last, :]))
    copies = []
    for number, place in enumerate(places):
        update = product(rows_ref[place, :], cols_ref[...])
        block_ref[number] = kern(tiles[number], left_half_ref[place, :], right_half) - update
        here = jnp.where(part == place.start // count, noise, 0.0)
        for start in range(0, chunk, square):
            first = place.start % count + start
            now, across = slice(start, start + square), slice(first, first + square)
            block_ref[number, now, across] += jnp.where(on_diagonal, here[:, across], 0.0)
        copy = pltpu.make_async_copy(block_ref.at[number], out_ref.at[pl.ds(number * chunk, chunk)], sems.at[number])
        copy.start()
        copies.append(copy)
    for copy in copies:
        copy.wait()


def shape(dims, kind=f32):
    return jax.ShapeDtypeStruct(dims, kind)


def compute_params(flops, moved):
    return dict(
        compiler_params=pltpu.CompilerParams(vmem_limit_bytes=vmem_bytes),
        cost_estimate=pl.CostEstimate(flops=flops, bytes_accessed=moved, transcendentals=0),
    )


def links_of(place, group, target_row, across):
    links = []
    step = 1 if target_row > group else -1
    links += [(0, place, z, step) for z in range(group, target_row, step)]
    (x, y), (end_x, end_y) = (place % across, place // across), (group % across, group // across)
    step = 1 if end_x > x else -1
    links += [(1, target_row, y, at, step) for at in range(x, end_x, step)]
    step = 1 if end_y > y else -1
    links += [(2, target_row, end_x, at, step) for at in range(y, end_y, step)]
    return links


def source_places(rows, halves):
    draw = random.Random(1)
    across = math.isqrt(rows)
    fewest = rows * halves // 4
    places = {}
    load = collections.Counter()

    def price(link, count):
        if link[0] == 0:
            return 15 * max(0, count - fewest)
        plane = link[1]
        return (0.3, 10, 40)[min(plane, 2)] * max(0, count - 1) ** 2

    def move(key, r, sign):
        change = 0
        ahead = r - key[1]
        early = {-1: 0.7, 0: 0.5, 1: 40 if r == rows - 1 else 2}.get(ahead, 0)
        for link in links_of(places[key][r], key[1], r, across):
            old = load[link]
            load[link] = old + sign
            change += price(link, old + sign) - price(link, old) + sign * early * (link[0] == 2)
        return change

    for h in range(halves):
        for g in range(rows):
            places[h, g] = draw.sample(range(rows), rows)
            for r in range(rows):
                move((h, g), r, 1)
    best, total, kept = 0, 0, {key: list(value) for key, value in places.items()}
    tries = 20000
    for number in range(tries):
        key = draw.randrange(halves), draw.randrange(rows)
        one, two = draw.sample(range(rows), 2)
        own = places[key]
        change = move(key, one, -1) + move(key, two, -1)
        own[one], own[two] = own[two], own[one]
        change += move(key, one, 1) + move(key, two, 1)
        heat = 6.0 * (1 - number / tries) + 0.02
        if change <= 0 or draw.random() < math.exp(-change / heat):
            total += change
            if total < best:
                best, kept = total, {key: list(value) for key, value in places.items()}
        else:
            move(key, one, -1), move(key, two, -1)
            own[one], own[two] = own[two], own[one]
            move(key, one, 1), move(key, two, 1)
    return kept


def column_pairs(rows, cols):
    halves = cols // rows
    places = source_places(rows, halves)
    return [
        (g * cols + places[h, g][r] * halves + h, r * cols + g * halves + halves - 1 - h)
        for h in range(halves)
        for g in range(rows)
        for r in range(rows)
    ]


def swap(value, bit, cols):
    return lax.ppermute(value, "col", [(i, i ^ bit) for i in range(cols)])


def gather_panel(panel_pool, panel_block, cols, beside):
    col_place = lax.axis_index("col")
    core = col_place % 2
    half_rows = panel_pool.shape[0] // 2
    mine = lax.dynamic_slice_in_dim(panel_pool, core * half_rows, half_rows, 0)
    got, mine = lax.optimization_barrier((swap(panel_pool, 1, cols), mine))
    got = lax.dynamic_slice_in_dim(got, core * half_rows, half_rows, 0)
    held = jnp.where(panel_block % 2 == core, mine, got)
    apart = panel_block ^ col_place
    low = 2
    while low < cols:
        high = min(4 * low, cols)
        away = apart & (high - low)
        steps = range(high - low, 0, -low)
        received = [swap(held, bits, cols) for bits in steps]
        received, beside = lax.optimization_barrier((received, beside))
        for bits, value in zip(steps, received):
            held = jnp.where(away == bits, value, held)
        low = high
    return [held, swap(held, 1, cols)], beside


def on_device(points, panel_pool, order, panel_index, inv_factor, ard_weights, noise):
    row_count, features = points.shape
    panel = inv_factor.shape[0]
    rows = lax.axis_size("row")
    cols = lax.axis_size("col")
    col_count = row_count * rows // cols
    halves = cols // rows
    col_place = lax.axis_index("col")
    part = halves - 1 - col_place % halves
    own_half = lax.dynamic_slice_in_dim(points, part * col_count, col_count, 0)
    sent = lax.ppermute(own_half, ("row", "col"), column_pairs(rows, cols))
    vectors = jnp.concatenate([order.astype(f32), ard_weights, noise])[None, :]
    pieces, vectors = gather_panel(panel_pool, panel_index[0], cols, vectors)

    packed = 4 * features
    factor_left, factor_right, pick, left, left_half = pl.pallas_call(
        parts_kernel,
        out_shape=[
            shape((panel, 3 * panel), bf16),
            shape((3 * panel, panel), bf16),
            shape((panel, panel), bf16),
            shape((row_count, packed), bf16),
            shape((row_count, 1)),
        ],
        **compute_params(10**8, 4 * 10**6),
    )(inv_factor, points, vectors)

    rows_left, chosen, chosen_half = pl.pallas_call(
        rows_kernel,
        out_shape=[shape((row_count, 3 * panel), bf16), shape((panel, packed), bf16), shape((panel, 1))],
        scratch_shapes=[pltpu.VMEM((row_count, 3 * panel), bf16)],
        **compute_params(1, 1),
    )(*pieces, vectors, factor_right, pick, left, left_half)

    chunks = 4
    return pl.pallas_call(
        functools.partial(update_kernel, rows, cols),
        out_shape=shape((row_count, col_count)),
        out_specs=pl.BlockSpec(memory_space=pl.ANY),
        scratch_shapes=[
            pltpu.VMEM((chunks, row_count // chunks, col_count), f32),
            pltpu.VMEM((3 * panel, col_count), bf16),
            pltpu.VMEM((3 * panel, col_count), bf16),
            pltpu.SemaphoreType.DMA((chunks,)),
        ],
        **compute_params(4 * 10**9, 8 * 10**6),
    )(sent, vectors, factor_left, left, left_half, rows_left, chosen, chosen_half)


def solution(mesh):
    in_specs = (P("row", None), P("col", None), P(), P(), P(), P(), P("row"))
    out_specs = P("row", "col")
    return jax.shard_map(
        on_device, mesh=mesh, in_specs=in_specs, out_specs=out_specs, check_vma=False
    )
```

```python
import collections
import functools
import math
import random

import jax
import jax.numpy as jnp
from jax import lax
from jax.experimental import pallas as pl
from jax.experimental.pallas import tpu as pltpu
from jax.sharding import PartitionSpec as P

log2_e = 1.4426950408889634
vmem_bytes = 32 * 1024 * 1024
f32, bf16 = jnp.float32, jnp.bfloat16
block, square = 256, 128


def halves_of(value):
    high = value.astype(bf16)
    low = (value - high.astype(f32)).astype(bf16)
    return high, low


def pack_left(high, low):
    return jnp.concatenate([high, low, high, low], axis=1)


def pack_right(high, low):
    return jnp.concatenate([high, low, low, high], axis=0)


def half_square(high, low, axis):
    value = high.astype(f32) + low.astype(f32)
    return 0.5 * jnp.sum(value * value, axis=axis, keepdims=True)


def product(left, right):
    return lax.dot_general(left, right, (((1,), (0,)), ((), ())), preferred_element_type=f32)


def store_left(ref, rows, first, value):
    high, low = halves_of(value)
    for start in range(0, value.shape[1], block):
        now, at = slice(start, start + block), 3 * (first + start)
        ref[rows, at : at + block] = high[:, now]
        ref[rows, at + block : at + 2 * block] = high[:, now]
        ref[rows, at + 2 * block : at + 3 * block] = low[:, now]


def store_right(ref, first, value):
    high, low = halves_of(value)
    for start in range(0, value.shape[0], block):
        now, at = slice(start, start + block), 3 * (first + start)
        ref[at : at + block, :] = high[now]
        ref[at + block : at + 2 * block, :] = low[now]
        ref[at + 2 * block : at + 3 * block, :] = high[now]


def kern(crossed, left_half, right_half):
    return jnp.exp2((crossed - left_half) - (right_half - 1.0))


def scale_of(vectors_ref, panel, features):
    return jnp.sqrt(vectors_ref[:, panel : panel + features] * log2_e)


def parts_kernel(
    factor_ref, points_ref, vectors_ref, factor_left_ref, factor_right_ref, pick_ref, left_ref,
    left_half_ref,
):
    factor = factor_ref[...]
    store_left(factor_left_ref, slice(None), 0, factor)
    store_right(factor_right_ref, 0, jnp.transpose(factor))
    panel = factor.shape[0]
    core = lax.axis_index("col") % 2
    place = lax.broadcasted_iota(jnp.int32, (panel, panel), 0) + core * (panel // 2)
    place = jnp.where(place >= panel, place - panel, place).astype(f32)
    hit = jnp.where(place == vectors_ref[:, :panel], 1.0, 0.0).astype(f32)
    pick_ref[...] = jnp.transpose(hit).astype(bf16)
    high, low = halves_of(points_ref[...] * scale_of(vectors_ref, panel, points_ref.shape[1]))
    left_ref[...] = pack_left(high, low)
    left_half_ref[...] = half_square(high, low, 1)


def rows_kernel(
    own_ref, other_ref, vectors_ref, factor_right_ref, pick_ref, left_ref, left_half_ref,
    rows_ref, chosen_ref, chosen_half_ref, kern_ref,
):
    panel = pick_ref.shape[0]
    features = own_ref.shape[1]
    held = jnp.concatenate([own_ref[...], other_ref[...]], axis=0) * scale_of(vectors_ref, panel, features)
    chosen = product(pick_ref[...], jnp.concatenate(halves_of(held), axis=1))
    high, low = chosen[:, :features].astype(bf16), chosen[:, features:].astype(bf16)
    chosen_ref[...] = pack_left(high, low)
    chosen_half_ref[...] = half_square(high, low, 1)
    turned = jnp.transpose(chosen)
    high, low = turned[:features].astype(bf16), turned[features:].astype(bf16)
    right = pack_right(high, low)
    right_half = half_square(high, low, 0)
    chunks = 4
    count = left_ref.shape[0] // chunks
    places = [slice(number * count, (number + 1) * count) for number in range(chunks)]
    crossed = [product(left_ref[place, :], right) for place in places]
    for number, place in enumerate(places):
        store_left(kern_ref, place, 0, kern(crossed[number], left_half_ref[place, :], right_half))
        for first in range(0, panel, block):
            last = first + block
            part = product(kern_ref[place, : 3 * last], factor_right_ref[: 3 * last, first:last])
            store_left(rows_ref, place, first, part)


def update_kernel(
    rows, cols, sent_ref, vectors_ref, factor_left_ref, left_ref, left_half_ref, rows_ref, chosen_ref,
    chosen_half_ref, out_ref, block_ref, kern_ref, cols_ref, sems,
):
    row_place, col_place = lax.axis_index("row"), lax.axis_index("col")
    halves = cols // rows
    count = sent_ref.shape[0]
    part = col_place % halves
    own = row_place == col_place // halves
    panel, features = factor_left_ref.shape[0], sent_ref.shape[1]

    high, low = halves_of(jnp.transpose(sent_ref[...] * scale_of(vectors_ref, panel, features)))
    right = pack_right(high, low)
    right_half = half_square(high, low, 0)
    chunks, chunk = block_ref.shape[:2]
    places = [slice(number * chunk, (number + 1) * chunk) for number in range(chunks)]
    at = pl.multiple_of(panel + features + part * count, 128)
    noise = jnp.where(own, vectors_ref[:, pl.ds(at, count)], 0.0)
    ids = (square, square)
    on_diagonal = lax.broadcasted_iota(jnp.int32, ids, 0) == lax.broadcasted_iota(jnp.int32, ids, 1)

    crossed = product(chosen_ref[...], right)
    tiles = [product(left_ref[place, :], right) for place in places]
    store_right(kern_ref, 0, kern(crossed, chosen_half_ref[...], right_half))
    for first in range(0, panel, block):
        last = first + block
        store_right(cols_ref, first, product(factor_left_ref[first:last, : 3 * last], kern_ref[: 3 * last, :]))
    copies = []
    for number, place in enumerate(places):
        update = product(rows_ref[place, :], cols_ref[...])
        block_ref[number] = kern(tiles[number], left_half_ref[place, :], right_half) - update
        here = jnp.where(part == place.start // count, noise, 0.0)
        for start in range(0, chunk, square):
            first = place.start % count + start
            now, across = slice(start, start + square), slice(first, first + square)
            block_ref[number, now, across] += jnp.where(on_diagonal, here[:, across], 0.0)
        copy = pltpu.make_async_copy(block_ref.at[number], out_ref.at[pl.ds(number * chunk, chunk)], sems.at[number])
        copy.start()
        copies.append(copy)
    for copy in copies:
        copy.wait()


def shape(dims, kind=f32):
    return jax.ShapeDtypeStruct(dims, kind)


def compute_params(flops, moved):
    return dict(
        compiler_params=pltpu.CompilerParams(vmem_limit_bytes=vmem_bytes),
        cost_estimate=pl.CostEstimate(flops=flops, bytes_accessed=moved, transcendentals=0),
    )


def links_of(place, group, target_row, across):
    links = []
    step = 1 if target_row > group else -1
    links += [(0, place, z, step) for z in range(group, target_row, step)]
    (x, y), (end_x, end_y) = (place % across, place // across), (group % across, group // across)
    step = 1 if end_x > x else -1
    links += [(1, target_row, y, at, step) for at in range(x, end_x, step)]
    step = 1 if end_y > y else -1
    links += [(2, target_row, end_x, at, step) for at in range(y, end_y, step)]
    return links


def source_places(rows, halves):
    draw = random.Random(5)
    across = math.isqrt(rows)
    places = {}
    load = collections.Counter()

    def move(key, r, sign):
        change = 0
        for link in links_of(places[key][r], key[1], r, across):
            old = load[link]
            load[link] = old + sign
            change += (old + sign) ** 4 - old**4
        return change

    for h in range(halves):
        for g in range(rows):
            places[h, g] = draw.sample(range(rows), rows)
            for r in range(rows):
                move((h, g), r, 1)
    best, total, kept = 0, 0, {key: list(value) for key, value in places.items()}
    tries = 20000
    for number in range(tries):
        key = draw.randrange(halves), draw.randrange(rows)
        one, two = draw.sample(range(rows), 2)
        own = places[key]
        change = move(key, one, -1) + move(key, two, -1)
        own[one], own[two] = own[two], own[one]
        change += move(key, one, 1) + move(key, two, 1)
        heat = 30.0 * (1 - number / tries) + 0.01
        if change <= 0 or draw.random() < math.exp(-change / heat):
            total += change
            if total < best:
                best, kept = total, {key: list(value) for key, value in places.items()}
        else:
            move(key, one, -1), move(key, two, -1)
            own[one], own[two] = own[two], own[one]
            move(key, one, 1), move(key, two, 1)
    return kept


def column_pairs(rows, cols):
    halves = cols // rows
    places = source_places(rows, halves)
    return [
        (g * cols + places[h, g][r] * halves + h, r * cols + g * halves + halves - 1 - h)
        for h in range(halves)
        for g in range(rows)
        for r in range(rows)
    ]


def swap(value, bit, cols):
    return lax.ppermute(value, "col", [(i, i ^ bit) for i in range(cols)])


def gather_panel(panel_pool, panel_block, cols, beside):
    col_place = lax.axis_index("col")
    core = col_place % 2
    half_rows = panel_pool.shape[0] // 2
    mine = lax.dynamic_slice_in_dim(panel_pool, core * half_rows, half_rows, 0)
    got, mine = lax.optimization_barrier((swap(panel_pool, 1, cols), mine))
    got = lax.dynamic_slice_in_dim(got, core * half_rows, half_rows, 0)
    held = jnp.where(panel_block % 2 == core, mine, got)
    apart = panel_block ^ col_place
    low = 2
    while low < cols:
        high = min(4 * low, cols)
        away = apart & (high - low)
        steps = range(high - low, 0, -low)
        received = [swap(held, bits, cols) for bits in steps]
        received, beside = lax.optimization_barrier((received, beside))
        for bits, value in zip(steps, received):
            held = jnp.where(away == bits, value, held)
        low = high
    return [held, swap(held, 1, cols)], beside


def on_device(points, panel_pool, order, panel_index, inv_factor, ard_weights, noise):
    row_count, features = points.shape
    panel = inv_factor.shape[0]
    rows = lax.axis_size("row")
    cols = lax.axis_size("col")
    col_count = row_count * rows // cols
    halves = cols // rows
    col_place = lax.axis_index("col")
    part = halves - 1 - col_place % halves
    own_half = lax.dynamic_slice_in_dim(points, part * col_count, col_count, 0)
    sent = lax.ppermute(own_half, ("row", "col"), column_pairs(rows, cols))
    vectors = jnp.concatenate([order.astype(f32), ard_weights, noise])[None, :]
    pieces, vectors = gather_panel(panel_pool, panel_index[0], cols, vectors)

    packed = 4 * features
    factor_left, factor_right, pick, left, left_half = pl.pallas_call(
        parts_kernel,
        out_shape=[
            shape((panel, 3 * panel), bf16),
            shape((3 * panel, panel), bf16),
            shape((panel, panel), bf16),
            shape((row_count, packed), bf16),
            shape((row_count, 1)),
        ],
        **compute_params(10**8, 4 * 10**6),
    )(inv_factor, points, vectors)

    rows_left, chosen, chosen_half = pl.pallas_call(
        rows_kernel,
        out_shape=[shape((row_count, 3 * panel), bf16), shape((panel, packed), bf16), shape((panel, 1))],
        scratch_shapes=[pltpu.VMEM((row_count, 3 * panel), bf16)],
        **compute_params(1, 1),
    )(*pieces, vectors, factor_right, pick, left, left_half)

    chunks = 8
    return pl.pallas_call(
        functools.partial(update_kernel, rows, cols),
        out_shape=shape((row_count, col_count)),
        out_specs=pl.BlockSpec(memory_space=pl.ANY),
        scratch_shapes=[
            pltpu.VMEM((chunks, row_count // chunks, col_count), f32),
            pltpu.VMEM((3 * panel, col_count), bf16),
            pltpu.VMEM((3 * panel, col_count), bf16),
            pltpu.SemaphoreType.DMA((chunks,)),
        ],
        **compute_params(4 * 10**9, 8 * 10**6),
    )(sent, vectors, factor_left, left, left_half, rows_left, chosen, chosen_half)


def solution(mesh):
    in_specs = (P("row", None), P("col", None), P(), P(), P(), P(), P("row"))
    out_specs = P("row", "col")
    return jax.shard_map(
        on_device, mesh=mesh, in_specs=in_specs, out_specs=out_specs, check_vma=False
    )
```

```python
import collections
import functools
import math
import random

import jax
import jax.numpy as jnp
from jax import lax
from jax.experimental import pallas as pl
from jax.experimental.pallas import tpu as pltpu
from jax.sharding import PartitionSpec as P

log2_e = 1.4426950408889634
vmem_bytes = 32 * 1024 * 1024
f32, bf16 = jnp.float32, jnp.bfloat16
block, square = 256, 128


def halves_of(value):
    high = value.astype(bf16)
    low = (value - high.astype(f32)).astype(bf16)
    return high, low


def pack_left(high, low):
    return jnp.concatenate([high, low, high, low], axis=1)


def pack_right(high, low):
    return jnp.concatenate([high, low, low, high], axis=0)


def half_square(high, low, axis):
    value = high.astype(f32) + low.astype(f32)
    return 0.5 * jnp.sum(value * value, axis=axis, keepdims=True)


def product(left, right):
    return lax.dot_general(left, right, (((1,), (0,)), ((), ())), preferred_element_type=f32)


def store_left(ref, rows, first, value):
    high, low = halves_of(value)
    for start in range(0, value.shape[1], block):
        now, at = slice(start, start + block), 3 * (first + start)
        ref[rows, at : at + block] = high[:, now]
        ref[rows, at + block : at + 2 * block] = high[:, now]
        ref[rows, at + 2 * block : at + 3 * block] = low[:, now]


def store_right(ref, first, value):
    high, low = halves_of(value)
    for start in range(0, value.shape[0], block):
        now, at = slice(start, start + block), 3 * (first + start)
        ref[at : at + block, :] = high[now]
        ref[at + block : at + 2 * block, :] = low[now]
        ref[at + 2 * block : at + 3 * block, :] = high[now]


def kern(crossed, left_half, right_half):
    return jnp.exp2((crossed - left_half) - (right_half - 1.0))


def scale_of(vectors_ref, panel, features):
    return jnp.sqrt(vectors_ref[:, panel : panel + features] * log2_e)


def parts_kernel(
    factor_ref, points_ref, vectors_ref, factor_left_ref, factor_right_ref, pick_ref, left_ref,
    left_half_ref,
):
    factor = factor_ref[...]
    store_left(factor_left_ref, slice(None), 0, factor)
    store_right(factor_right_ref, 0, jnp.transpose(factor))
    panel = factor.shape[0]
    core = lax.axis_index("col") % 2
    place = lax.broadcasted_iota(jnp.int32, (panel, panel), 0) + core * (panel // 2)
    place = jnp.where(place >= panel, place - panel, place).astype(f32)
    hit = jnp.where(place == vectors_ref[:, :panel], 1.0, 0.0).astype(f32)
    pick_ref[...] = jnp.transpose(hit).astype(bf16)
    high, low = halves_of(points_ref[...] * scale_of(vectors_ref, panel, points_ref.shape[1]))
    left_ref[...] = pack_left(high, low)
    left_half_ref[...] = half_square(high, low, 1)


def rows_kernel(
    own_ref, other_ref, vectors_ref, factor_right_ref, pick_ref, left_ref, left_half_ref,
    rows_ref, chosen_ref, chosen_half_ref, kern_ref,
):
    panel = pick_ref.shape[0]
    features = own_ref.shape[1]
    held = jnp.concatenate([own_ref[...], other_ref[...]], axis=0) * scale_of(vectors_ref, panel, features)
    chosen = product(pick_ref[...], jnp.concatenate(halves_of(held), axis=1))
    high, low = chosen[:, :features].astype(bf16), chosen[:, features:].astype(bf16)
    chosen_ref[...] = pack_left(high, low)
    chosen_half_ref[...] = half_square(high, low, 1)
    turned = jnp.transpose(chosen)
    high, low = turned[:features].astype(bf16), turned[features:].astype(bf16)
    right = pack_right(high, low)
    right_half = half_square(high, low, 0)
    chunks = 8
    count = left_ref.shape[0] // chunks
    places = [slice(number * count, (number + 1) * count) for number in range(chunks)]
    crossed = [product(left_ref[place, :], right) for place in places]
    for number, place in enumerate(places):
        store_left(kern_ref, place, 0, kern(crossed[number], left_half_ref[place, :], right_half))
        for first in range(0, panel, block):
            last = first + block
            part = product(kern_ref[place, : 3 * last], factor_right_ref[: 3 * last, first:last])
            store_left(rows_ref, place, first, part)


def update_kernel(
    rows, cols, sent_ref, vectors_ref, factor_left_ref, left_ref, left_half_ref, rows_ref, chosen_ref,
    chosen_half_ref, out_ref, block_ref, kern_ref, cols_ref, sems,
):
    row_place, col_place = lax.axis_index("row"), lax.axis_index("col")
    halves = cols // rows
    count = sent_ref.shape[0]
    part = col_place % halves
    own = row_place == col_place // halves
    panel, features = factor_left_ref.shape[0], sent_ref.shape[1]

    high, low = halves_of(jnp.transpose(sent_ref[...] * scale_of(vectors_ref, panel, features)))
    right = pack_right(high, low)
    right_half = half_square(high, low, 0)
    chunks, chunk = block_ref.shape[:2]
    places = [slice(number * chunk, (number + 1) * chunk) for number in range(chunks)]
    at = pl.multiple_of(panel + features + part * count, 128)
    noise = jnp.where(own, vectors_ref[:, pl.ds(at, count)], 0.0)
    ids = (square, square)
    on_diagonal = lax.broadcasted_iota(jnp.int32, ids, 0) == lax.broadcasted_iota(jnp.int32, ids, 1)

    blocks = [slice(first, first + block) for first in range(0, panel, block)]
    crossed = [product(chosen_ref[place, :], right) for place in blocks]
    tiles = [product(left_ref[place, :], right) for place in places]
    for number, place in enumerate(blocks):
        first, last = place.start, place.stop
        store_right(kern_ref, first, kern(crossed[number], chosen_half_ref[place, :], right_half))
        store_right(cols_ref, first, product(factor_left_ref[first:last, : 3 * last], kern_ref[: 3 * last, :]))
    copies = []
    for number, place in enumerate(places):
        update = product(rows_ref[place, :], cols_ref[...])
        block_ref[number] = kern(tiles[number], left_half_ref[place, :], right_half) - update
        here = jnp.where(part == place.start // count, noise, 0.0)
        for start in range(0, chunk, square):
            first = place.start % count + start
            now, across = slice(start, start + square), slice(first, first + square)
            block_ref[number, now, across] += jnp.where(on_diagonal, here[:, across], 0.0)
        copy = pltpu.make_async_copy(block_ref.at[number], out_ref.at[pl.ds(number * chunk, chunk)], sems.at[number])
        copy.start()
        copies.append(copy)
    for copy in copies:
        copy.wait()


def shape(dims, kind=f32):
    return jax.ShapeDtypeStruct(dims, kind)


def compute_params(flops, moved):
    return dict(
        compiler_params=pltpu.CompilerParams(vmem_limit_bytes=vmem_bytes),
        cost_estimate=pl.CostEstimate(flops=flops, bytes_accessed=moved, transcendentals=0),
    )


def links_of(place, group, target_row, across):
    links = []
    step = 1 if target_row > group else -1
    links += [(0, place, z, step) for z in range(group, target_row, step)]
    (x, y), (end_x, end_y) = (place % across, place // across), (group % across, group // across)
    step = 1 if end_x > x else -1
    links += [(1, target_row, y, at, step) for at in range(x, end_x, step)]
    step = 1 if end_y > y else -1
    links += [(2, target_row, end_x, at, step) for at in range(y, end_y, step)]
    return links


def source_places(rows, halves):
    draw = random.Random(5)
    across = math.isqrt(rows)
    places = {}
    load = collections.Counter()

    def move(key, r, sign):
        change = 0
        for link in links_of(places[key][r], key[1], r, across):
            old = load[link]
            load[link] = old + sign
            change += (old + sign) ** 4 - old**4
        return change

    for h in range(halves):
        for g in range(rows):
            places[h, g] = draw.sample(range(rows), rows)
            for r in range(rows):
                move((h, g), r, 1)
    best, total, kept = 0, 0, {key: list(value) for key, value in places.items()}
    tries = 20000
    for number in range(tries):
        key = draw.randrange(halves), draw.randrange(rows)
        one, two = draw.sample(range(rows), 2)
        own = places[key]
        change = move(key, one, -1) + move(key, two, -1)
        own[one], own[two] = own[two], own[one]
        change += move(key, one, 1) + move(key, two, 1)
        heat = 30.0 * (1 - number / tries) + 0.01
        if change <= 0 or draw.random() < math.exp(-change / heat):
            total += change
            if total < best:
                best, kept = total, {key: list(value) for key, value in places.items()}
        else:
            move(key, one, -1), move(key, two, -1)
            own[one], own[two] = own[two], own[one]
            move(key, one, 1), move(key, two, 1)
    return kept


def column_pairs(rows, cols):
    halves = cols // rows
    places = source_places(rows, halves)
    return [
        (g * cols + places[h, g][r] * halves + h, r * cols + g * halves + halves - 1 - h)
        for h in range(halves)
        for g in range(rows)
        for r in range(rows)
    ]


def swap(value, bit, cols):
    return lax.ppermute(value, "col", [(i, i ^ bit) for i in range(cols)])


def gather_panel(panel_pool, panel_block, cols, beside):
    col_place = lax.axis_index("col")
    core = col_place % 2
    half_rows = panel_pool.shape[0] // 2
    mine = lax.dynamic_slice_in_dim(panel_pool, core * half_rows, half_rows, 0)
    got, mine = lax.optimization_barrier((swap(panel_pool, 1, cols), mine))
    got = lax.dynamic_slice_in_dim(got, core * half_rows, half_rows, 0)
    held = jnp.where(panel_block % 2 == core, mine, got)
    apart = panel_block ^ col_place
    low = 2
    while low < cols:
        high = min(4 * low, cols)
        away = apart & (high - low)
        steps = range(high - low, 0, -low)
        received = [swap(held, bits, cols) for bits in steps]
        received, beside = lax.optimization_barrier((received, beside))
        for bits, value in zip(steps, received):
            held = jnp.where(away == bits, value, held)
        low = high
    return [held, swap(held, 1, cols)], beside


def on_device(points, panel_pool, order, panel_index, inv_factor, ard_weights, noise):
    row_count, features = points.shape
    panel = inv_factor.shape[0]
    rows = lax.axis_size("row")
    cols = lax.axis_size("col")
    col_count = row_count * rows // cols
    halves = cols // rows
    col_place = lax.axis_index("col")
    part = halves - 1 - col_place % halves
    own_half = lax.dynamic_slice_in_dim(points, part * col_count, col_count, 0)
    sent = lax.ppermute(own_half, ("row", "col"), column_pairs(rows, cols))
    vectors = jnp.concatenate([order.astype(f32), ard_weights, noise])[None, :]
    pieces, vectors = gather_panel(panel_pool, panel_index[0], cols, vectors)

    packed = 4 * features
    factor_left, factor_right, pick, left, left_half = pl.pallas_call(
        parts_kernel,
        out_shape=[
            shape((panel, 3 * panel), bf16),
            shape((3 * panel, panel), bf16),
            shape((panel, panel), bf16),
            shape((row_count, packed), bf16),
            shape((row_count, 1)),
        ],
        **compute_params(10**8, 4 * 10**6),
    )(inv_factor, points, vectors)

    rows_left, chosen, chosen_half = pl.pallas_call(
        rows_kernel,
        out_shape=[shape((row_count, 3 * panel), bf16), shape((panel, packed), bf16), shape((panel, 1))],
        scratch_shapes=[pltpu.VMEM((row_count, 3 * panel), bf16)],
        **compute_params(1, 1),
    )(*pieces, vectors, factor_right, pick, left, left_half)

    chunks = 8
    return pl.pallas_call(
        functools.partial(update_kernel, rows, cols),
        out_shape=shape((row_count, col_count)),
        out_specs=pl.BlockSpec(memory_space=pl.ANY),
        scratch_shapes=[
            pltpu.VMEM((chunks, row_count // chunks, col_count), f32),
            pltpu.VMEM((3 * panel, col_count), bf16),
            pltpu.VMEM((3 * panel, col_count), bf16),
            pltpu.SemaphoreType.DMA((chunks,)),
        ],
        **compute_params(4 * 10**9, 8 * 10**6),
    )(sent, vectors, factor_left, left, left_half, rows_left, chosen, chosen_half)


def solution(mesh):
    in_specs = (P("row", None), P("col", None), P(), P(), P(), P(), P("row"))
    out_specs = P("row", "col")
    return jax.shard_map(
        on_device, mesh=mesh, in_specs=in_specs, out_specs=out_specs, check_vma=False
    )
```

```python
import collections
import functools
import math
import random

import jax
import jax.numpy as jnp
from jax import lax
from jax.experimental import pallas as pl
from jax.experimental.pallas import tpu as pltpu
from jax.sharding import PartitionSpec as P

log2_e = 1.4426950408889634
vmem_bytes = 32 * 1024 * 1024
f32, bf16 = jnp.float32, jnp.bfloat16
block, square = 256, 128


def halves_of(value):
    high = value.astype(bf16)
    low = (value - high.astype(f32)).astype(bf16)
    return high, low


def pack_left(high, low):
    return jnp.concatenate([high, low, high, low], axis=1)


def pack_right(high, low):
    return jnp.concatenate([high, low, low, high], axis=0)


def half_square(high, low, axis):
    value = high.astype(f32) + low.astype(f32)
    return 0.5 * jnp.sum(value * value, axis=axis, keepdims=True)


def product(left, right):
    return lax.dot_general(left, right, (((1,), (0,)), ((), ())), preferred_element_type=f32)


def store_left(ref, rows, first, value):
    high, low = halves_of(value)
    for start in range(0, value.shape[1], block):
        now, at = slice(start, start + block), 3 * (first + start)
        ref[rows, at : at + block] = high[:, now]
        ref[rows, at + block : at + 2 * block] = high[:, now]
        ref[rows, at + 2 * block : at + 3 * block] = low[:, now]


def store_right(ref, first, value):
    high, low = halves_of(value)
    for start in range(0, value.shape[0], block):
        now, at = slice(start, start + block), 3 * (first + start)
        ref[at : at + block, :] = high[now]
        ref[at + block : at + 2 * block, :] = low[now]
        ref[at + 2 * block : at + 3 * block, :] = high[now]


def kern(crossed, left_half, right_half):
    return jnp.exp2((crossed - left_half) - (right_half - 1.0))


def scale_of(vectors_ref, panel, features):
    return jnp.sqrt(vectors_ref[:, panel : panel + features] * log2_e)


def parts_kernel(
    factor_ref, points_ref, vectors_ref, factor_left_ref, factor_right_ref, pick_ref, left_ref,
    left_half_ref,
):
    factor = factor_ref[...]
    store_left(factor_left_ref, slice(None), 0, factor)
    store_right(factor_right_ref, 0, jnp.transpose(factor))
    panel = factor.shape[0]
    core = lax.axis_index("col") % 2
    place = lax.broadcasted_iota(jnp.int32, (panel, panel), 0) + core * (panel // 2)
    place = jnp.where(place >= panel, place - panel, place).astype(f32)
    hit = jnp.where(place == vectors_ref[:, :panel], 1.0, 0.0).astype(f32)
    pick_ref[...] = jnp.transpose(hit).astype(bf16)
    high, low = halves_of(points_ref[...] * scale_of(vectors_ref, panel, points_ref.shape[1]))
    left_ref[...] = pack_left(high, low)
    left_half_ref[...] = half_square(high, low, 1)


def rows_kernel(
    own_ref, other_ref, vectors_ref, factor_right_ref, pick_ref, left_ref, left_half_ref,
    rows_ref, chosen_ref, chosen_half_ref, kern_ref,
):
    panel = pick_ref.shape[0]
    features = own_ref.shape[1]
    held = jnp.concatenate([own_ref[...], other_ref[...]], axis=0) * scale_of(vectors_ref, panel, features)
    chosen = product(pick_ref[...], jnp.concatenate(halves_of(held), axis=1))
    high, low = chosen[:, :features].astype(bf16), chosen[:, features:].astype(bf16)
    chosen_ref[...] = pack_left(high, low)
    chosen_half_ref[...] = half_square(high, low, 1)
    turned = jnp.transpose(chosen)
    high, low = turned[:features].astype(bf16), turned[features:].astype(bf16)
    right = pack_right(high, low)
    right_half = half_square(high, low, 0)
    chunks = 4
    count = left_ref.shape[0] // chunks
    places = [slice(number * count, (number + 1) * count) for number in range(chunks)]
    crossed = [product(left_ref[place, :], right) for place in places]
    for number, place in enumerate(places):
        store_left(kern_ref, place, 0, kern(crossed[number], left_half_ref[place, :], right_half))
        for first in range(0, panel, block):
            last = first + block
            part = product(kern_ref[place, : 3 * last], factor_right_ref[: 3 * last, first:last])
            store_left(rows_ref, place, first, part)


def update_kernel(
    rows, cols, sent_ref, vectors_ref, factor_left_ref, left_ref, left_half_ref, rows_ref, chosen_ref,
    chosen_half_ref, out_ref, block_ref, kern_ref, cols_ref, sems,
):
    row_place, col_place = lax.axis_index("row"), lax.axis_index("col")
    halves = cols // rows
    count = sent_ref.shape[0]
    part = col_place % halves
    own = row_place == col_place // halves
    panel, features = factor_left_ref.shape[0], sent_ref.shape[1]

    high, low = halves_of(jnp.transpose(sent_ref[...] * scale_of(vectors_ref, panel, features)))
    right = pack_right(high, low)
    right_half = half_square(high, low, 0)
    chunks, chunk = block_ref.shape[:2]
    places = [slice(number * chunk, (number + 1) * chunk) for number in range(chunks)]
    at = pl.multiple_of(panel + features + part * count, 128)
    noise = jnp.where(own, vectors_ref[:, pl.ds(at, count)], 0.0)
    ids = (square, square)
    on_diagonal = lax.broadcasted_iota(jnp.int32, ids, 0) == lax.broadcasted_iota(jnp.int32, ids, 1)

    crossed = product(chosen_ref[...], right)
    tiles = [product(left_ref[place, :], right) for place in places]
    store_right(kern_ref, 0, kern(crossed, chosen_half_ref[...], right_half))
    for first in range(0, panel, block):
        last = first + block
        store_right(cols_ref, first, product(factor_left_ref[first:last, : 3 * last], kern_ref[: 3 * last, :]))
    copies = []
    for number, place in enumerate(places):
        update = product(rows_ref[place, :], cols_ref[...])
        block_ref[number] = kern(tiles[number], left_half_ref[place, :], right_half) - update
        here = jnp.where(part == place.start // count, noise, 0.0)
        for start in range(0, chunk, square):
            first = place.start % count + start
            now, across = slice(start, start + square), slice(first, first + square)
            block_ref[number, now, across] += jnp.where(on_diagonal, here[:, across], 0.0)
        copy = pltpu.make_async_copy(block_ref.at[number], out_ref.at[pl.ds(number * chunk, chunk)], sems.at[number])
        copy.start()
        copies.append(copy)
    for copy in copies:
        copy.wait()


def shape(dims, kind=f32):
    return jax.ShapeDtypeStruct(dims, kind)


def compute_params(flops, moved):
    return dict(
        compiler_params=pltpu.CompilerParams(vmem_limit_bytes=vmem_bytes),
        cost_estimate=pl.CostEstimate(flops=flops, bytes_accessed=moved, transcendentals=0),
    )


def links_of(place, group, target_row, across):
    links = []
    step = 1 if target_row > group else -1
    links += [(0, place, z, step) for z in range(group, target_row, step)]
    (x, y), (end_x, end_y) = (place % across, place // across), (group % across, group // across)
    step = 1 if end_x > x else -1
    links += [(1, target_row, y, at, step) for at in range(x, end_x, step)]
    step = 1 if end_y > y else -1
    links += [(2, target_row, end_x, at, step) for at in range(y, end_y, step)]
    return links


def source_places(rows, halves):
    draw = random.Random(5)
    across = math.isqrt(rows)
    places = {}
    load = collections.Counter()

    def move(key, r, sign):
        change = 0
        for link in links_of(places[key][r], key[1], r, across):
            old = load[link]
            load[link] = old + sign
            change += (old + sign) ** 4 - old**4
        return change

    for h in range(halves):
        for g in range(rows):
            places[h, g] = draw.sample(range(rows), rows)
            for r in range(rows):
                move((h, g), r, 1)
    best, total, kept = 0, 0, {key: list(value) for key, value in places.items()}
    tries = 20000
    for number in range(tries):
        key = draw.randrange(halves), draw.randrange(rows)
        one, two = draw.sample(range(rows), 2)
        own = places[key]
        change = move(key, one, -1) + move(key, two, -1)
        own[one], own[two] = own[two], own[one]
        change += move(key, one, 1) + move(key, two, 1)
        heat = 30.0 * (1 - number / tries) + 0.01
        if change <= 0 or draw.random() < math.exp(-change / heat):
            total += change
            if total < best:
                best, kept = total, {key: list(value) for key, value in places.items()}
        else:
            move(key, one, -1), move(key, two, -1)
            own[one], own[two] = own[two], own[one]
            move(key, one, 1), move(key, two, 1)
    return kept


def column_pairs(rows, cols):
    halves = cols // rows
    places = source_places(rows, halves)
    return [
        (g * cols + places[h, g][r] * halves + h, r * cols + g * halves + halves - 1 - h)
        for h in range(halves)
        for g in range(rows)
        for r in range(rows)
    ]


def swap(value, bit, cols):
    return lax.ppermute(value, "col", [(i, i ^ bit) for i in range(cols)])


def gather_panel(panel_pool, panel_block, cols, beside):
    col_place = lax.axis_index("col")
    core = col_place % 2
    half_rows = panel_pool.shape[0] // 2
    mine = lax.dynamic_slice_in_dim(panel_pool, core * half_rows, half_rows, 0)
    got, mine = lax.optimization_barrier((swap(panel_pool, 1, cols), mine))
    got = lax.dynamic_slice_in_dim(got, core * half_rows, half_rows, 0)
    held = jnp.where(panel_block % 2 == core, mine, got)
    apart = panel_block ^ col_place
    low = 2
    while low < cols:
        high = min(4 * low, cols)
        away = apart & (high - low)
        steps = [(2 * low, 3 * low), (3 * low, 2 * low), (low, low)] if high == 4 * low else [(low, low)]
        received = [
            lax.ppermute(held, "col", [(i, i ^ step[i % 2]) for i in range(cols)]) for step in steps
        ]
        received, beside = lax.optimization_barrier((received, beside))
        for step, value in zip(steps, received):
            held = jnp.where(away == jnp.where(core == 0, step[0], step[1]), value, held)
        low = high
    return [held, swap(held, 1, cols)], beside


def on_device(points, panel_pool, order, panel_index, inv_factor, ard_weights, noise):
    row_count, features = points.shape
    panel = inv_factor.shape[0]
    rows = lax.axis_size("row")
    cols = lax.axis_size("col")
    col_count = row_count * rows // cols
    halves = cols // rows
    col_place = lax.axis_index("col")
    part = halves - 1 - col_place % halves
    own_half = lax.dynamic_slice_in_dim(points, part * col_count, col_count, 0)
    sent = lax.ppermute(own_half, ("row", "col"), column_pairs(rows, cols))
    vectors = jnp.concatenate([order.astype(f32), ard_weights, noise])[None, :]
    pieces, vectors = gather_panel(panel_pool, panel_index[0], cols, vectors)

    packed = 4 * features
    factor_left, factor_right, pick, left, left_half = pl.pallas_call(
        parts_kernel,
        out_shape=[
            shape((panel, 3 * panel), bf16),
            shape((3 * panel, panel), bf16),
            shape((panel, panel), bf16),
            shape((row_count, packed), bf16),
            shape((row_count, 1)),
        ],
        **compute_params(10**8, 4 * 10**6),
    )(inv_factor, points, vectors)

    rows_left, chosen, chosen_half = pl.pallas_call(
        rows_kernel,
        out_shape=[shape((row_count, 3 * panel), bf16), shape((panel, packed), bf16), shape((panel, 1))],
        scratch_shapes=[pltpu.VMEM((row_count, 3 * panel), bf16)],
        **compute_params(1, 1),
    )(*pieces, vectors, factor_right, pick, left, left_half)

    chunks = 8
    return pl.pallas_call(
        functools.partial(update_kernel, rows, cols),
        out_shape=shape((row_count, col_count)),
        out_specs=pl.BlockSpec(memory_space=pl.ANY),
        scratch_shapes=[
            pltpu.VMEM((chunks, row_count // chunks, col_count), f32),
            pltpu.VMEM((3 * panel, col_count), bf16),
            pltpu.VMEM((3 * panel, col_count), bf16),
            pltpu.SemaphoreType.DMA((chunks,)),
        ],
        **compute_params(4 * 10**9, 8 * 10**6),
    )(sent, vectors, factor_left, left, left_half, rows_left, chosen, chosen_half)


def solution(mesh):
    in_specs = (P("row", None), P("col", None), P(), P(), P(), P(), P("row"))
    out_specs = P("row", "col")
    return jax.shard_map(
        on_device, mesh=mesh, in_specs=in_specs, out_specs=out_specs, check_vma=False
    )
```

```python
import collections
import functools
import math
import random

import jax
import jax.numpy as jnp
from jax import lax
from jax.experimental import pallas as pl
from jax.experimental.pallas import tpu as pltpu
from jax.sharding import PartitionSpec as P

log2_e = 1.4426950408889634
vmem_bytes = 32 * 1024 * 1024
f32, bf16 = jnp.float32, jnp.bfloat16
block, square = 256, 128


def halves_of(value):
    high = value.astype(bf16)
    low = (value - high.astype(f32)).astype(bf16)
    return high, low


def pack_left(high, low):
    return jnp.concatenate([high, low, high, low], axis=1)


def pack_right(high, low):
    return jnp.concatenate([high, low, low, high], axis=0)


def half_square(high, low, axis):
    value = high.astype(f32) + low.astype(f32)
    return 0.5 * jnp.sum(value * value, axis=axis, keepdims=True)


def product(left, right):
    return lax.dot_general(left, right, (((1,), (0,)), ((), ())), preferred_element_type=f32)


def store_left(ref, rows, first, value):
    high, low = halves_of(value)
    for start in range(0, value.shape[1], block):
        now, at = slice(start, start + block), 3 * (first + start)
        ref[rows, at : at + block] = high[:, now]
        ref[rows, at + block : at + 2 * block] = high[:, now]
        ref[rows, at + 2 * block : at + 3 * block] = low[:, now]


def store_right(ref, first, value):
    high, low = halves_of(value)
    for start in range(0, value.shape[0], block):
        now, at = slice(start, start + block), 3 * (first + start)
        ref[at : at + block, :] = high[now]
        ref[at + block : at + 2 * block, :] = low[now]
        ref[at + 2 * block : at + 3 * block, :] = high[now]


def kern(crossed, left_half, right_half):
    return jnp.exp2((crossed - left_half) - (right_half - 1.0))


def scale_of(vectors_ref, panel, features):
    return jnp.sqrt(vectors_ref[:, panel : panel + features] * log2_e)


def parts_kernel(
    factor_ref, points_ref, vectors_ref, factor_left_ref, factor_right_ref, pick_ref, left_ref,
    left_half_ref,
):
    factor = factor_ref[...]
    store_left(factor_left_ref, slice(None), 0, factor)
    store_right(factor_right_ref, 0, jnp.transpose(factor))
    panel = factor.shape[0]
    core = lax.axis_index("col") % 2
    place = lax.broadcasted_iota(jnp.int32, (panel, panel), 0) + core * (panel // 2)
    place = jnp.where(place >= panel, place - panel, place).astype(f32)
    hit = jnp.where(place == vectors_ref[:, :panel], 1.0, 0.0).astype(f32)
    pick_ref[...] = jnp.transpose(hit).astype(bf16)
    high, low = halves_of(points_ref[...] * scale_of(vectors_ref, panel, points_ref.shape[1]))
    left_ref[...] = pack_left(high, low)
    left_half_ref[...] = half_square(high, low, 1)


def rows_kernel(
    own_ref, other_ref, vectors_ref, factor_right_ref, pick_ref, left_ref, left_half_ref,
    rows_ref, chosen_ref, chosen_half_ref, kern_ref,
):
    panel = pick_ref.shape[0]
    features = own_ref.shape[1]
    held = jnp.concatenate([own_ref[...], other_ref[...]], axis=0) * scale_of(vectors_ref, panel, features)
    chosen = product(pick_ref[...], jnp.concatenate(halves_of(held), axis=1))
    high, low = chosen[:, :features].astype(bf16), chosen[:, features:].astype(bf16)
    chosen_ref[...] = pack_left(high, low)
    chosen_half_ref[...] = half_square(high, low, 1)
    turned = jnp.transpose(chosen)
    high, low = turned[:features].astype(bf16), turned[features:].astype(bf16)
    right = pack_right(high, low)
    right_half = half_square(high, low, 0)
    chunks = 4
    count = left_ref.shape[0] // chunks
    places = [slice(number * count, (number + 1) * count) for number in range(chunks)]
    crossed = [product(left_ref[place, :], right) for place in places]
    for number, place in enumerate(places):
        store_left(kern_ref, place, 0, kern(crossed[number], left_half_ref[place, :], right_half))
        for first in range(0, panel, block):
            last = first + block
            part = product(kern_ref[place, : 3 * last], factor_right_ref[: 3 * last, first:last])
            store_left(rows_ref, place, first, part)


def update_kernel(
    rows, cols, sent_ref, vectors_ref, factor_left_ref, left_ref, left_half_ref, rows_ref, chosen_ref,
    chosen_half_ref, out_ref, block_ref, kern_ref, cols_ref, sems,
):
    row_place, col_place = lax.axis_index("row"), lax.axis_index("col")
    halves = cols // rows
    count = sent_ref.shape[0]
    part = col_place % halves
    own = row_place == col_place // halves
    panel, features = factor_left_ref.shape[0], sent_ref.shape[1]

    high, low = halves_of(jnp.transpose(sent_ref[...] * scale_of(vectors_ref, panel, features)))
    right = pack_right(high, low)
    right_half = half_square(high, low, 0)
    chunks, chunk = block_ref.shape[:2]
    places = [slice(number * chunk, (number + 1) * chunk) for number in range(chunks)]
    at = pl.multiple_of(panel + features + part * count, 128)
    noise = jnp.where(own, vectors_ref[:, pl.ds(at, count)], 0.0)
    ids = (square, square)
    on_diagonal = lax.broadcasted_iota(jnp.int32, ids, 0) == lax.broadcasted_iota(jnp.int32, ids, 1)

    crossed = product(chosen_ref[...], right)
    tiles = [product(left_ref[place, :], right) for place in places]
    store_right(kern_ref, 0, kern(crossed, chosen_half_ref[...], right_half))
    for first in range(0, panel, block):
        last = first + block
        store_right(cols_ref, first, product(factor_left_ref[first:last, : 3 * last], kern_ref[: 3 * last, :]))
    copies = []
    for number, place in enumerate(places):
        update = product(rows_ref[place, :], cols_ref[...])
        block_ref[number] = kern(tiles[number], left_half_ref[place, :], right_half) - update
        here = jnp.where(part == place.start // count, noise, 0.0)
        for start in range(0, chunk, square):
            first = place.start % count + start
            now, across = slice(start, start + square), slice(first, first + square)
            block_ref[number, now, across] += jnp.where(on_diagonal, here[:, across], 0.0)
        copy = pltpu.make_async_copy(block_ref.at[number], out_ref.at[pl.ds(number * chunk, chunk)], sems.at[number])
        copy.start()
        copies.append(copy)
    for copy in copies:
        copy.wait()


def shape(dims, kind=f32):
    return jax.ShapeDtypeStruct(dims, kind)


def compute_params(flops, moved):
    return dict(
        compiler_params=pltpu.CompilerParams(vmem_limit_bytes=vmem_bytes),
        cost_estimate=pl.CostEstimate(flops=flops, bytes_accessed=moved, transcendentals=0),
    )


def links_of(place, group, target_row, across):
    links = []
    step = 1 if target_row > group else -1
    links += [(0, place, z, step) for z in range(group, target_row, step)]
    (x, y), (end_x, end_y) = (place % across, place // across), (group % across, group // across)
    step = 1 if end_x > x else -1
    links += [(1, target_row, y, at, step) for at in range(x, end_x, step)]
    step = 1 if end_y > y else -1
    links += [(2, target_row, end_x, at, step) for at in range(y, end_y, step)]
    return links


def source_places(rows, halves):
    draw = random.Random(5)
    across = math.isqrt(rows)
    places = {}
    load = collections.Counter()

    def move(key, r, sign):
        change = 0
        for link in links_of(places[key][r], key[1], r, across):
            old = load[link]
            load[link] = old + sign
            change += (old + sign) ** 4 - old**4
        return change

    for h in range(halves):
        for g in range(rows):
            places[h, g] = draw.sample(range(rows), rows)
            for r in range(rows):
                move((h, g), r, 1)
    best, total, kept = 0, 0, {key: list(value) for key, value in places.items()}
    tries = 20000
    for number in range(tries):
        key = draw.randrange(halves), draw.randrange(rows)
        one, two = draw.sample(range(rows), 2)
        own = places[key]
        change = move(key, one, -1) + move(key, two, -1)
        own[one], own[two] = own[two], own[one]
        change += move(key, one, 1) + move(key, two, 1)
        heat = 30.0 * (1 - number / tries) + 0.01
        if change <= 0 or draw.random() < math.exp(-change / heat):
            total += change
            if total < best:
                best, kept = total, {key: list(value) for key, value in places.items()}
        else:
            move(key, one, -1), move(key, two, -1)
            own[one], own[two] = own[two], own[one]
            move(key, one, 1), move(key, two, 1)
    return kept


def column_pairs(rows, cols):
    halves = cols // rows
    places = source_places(rows, halves)
    return [
        (g * cols + places[h, g][r] * halves + h, r * cols + g * halves + halves - 1 - h)
        for h in range(halves)
        for g in range(rows)
        for r in range(rows)
    ]


def swap(value, bit, cols):
    return lax.ppermute(value, "col", [(i, i ^ bit) for i in range(cols)])


def gather_panel(panel_pool, panel_block, cols, beside):
    col_place = lax.axis_index("col")
    core = col_place % 2
    half_rows = panel_pool.shape[0] // 2
    mine = lax.dynamic_slice_in_dim(panel_pool, core * half_rows, half_rows, 0)
    got, mine = lax.optimization_barrier((swap(panel_pool, 1, cols), mine))
    got = lax.dynamic_slice_in_dim(got, core * half_rows, half_rows, 0)
    held = jnp.where(panel_block % 2 == core, mine, got)
    apart = panel_block ^ col_place
    low = 2
    while low < cols:
        high = min(4 * low, cols)
        away = apart & (high - low)
        steps = [(2 * low, low), (3 * low, 2 * low), (low, 3 * low)] if high == 4 * low else [(low, low)]
        received = [
            lax.ppermute(held, "col", [(i, i ^ step[i % 2]) for i in range(cols)]) for step in steps
        ]
        received, beside = lax.optimization_barrier((received, beside))
        for step, value in zip(steps, received):
            held = jnp.where(away == jnp.where(core == 0, step[0], step[1]), value, held)
        low = high
    return [held, swap(held, 1, cols)], beside


def on_device(points, panel_pool, order, panel_index, inv_factor, ard_weights, noise):
    row_count, features = points.shape
    panel = inv_factor.shape[0]
    rows = lax.axis_size("row")
    cols = lax.axis_size("col")
    col_count = row_count * rows // cols
    halves = cols // rows
    col_place = lax.axis_index("col")
    part = halves - 1 - col_place % halves
    own_half = lax.dynamic_slice_in_dim(points, part * col_count, col_count, 0)
    sent = lax.ppermute(own_half, ("row", "col"), column_pairs(rows, cols))
    vectors = jnp.concatenate([order.astype(f32), ard_weights, noise])[None, :]
    pieces, vectors = gather_panel(panel_pool, panel_index[0], cols, vectors)

    packed = 4 * features
    factor_left, factor_right, pick, left, left_half = pl.pallas_call(
        parts_kernel,
        out_shape=[
            shape((panel, 3 * panel), bf16),
            shape((3 * panel, panel), bf16),
            shape((panel, panel), bf16),
            shape((row_count, packed), bf16),
            shape((row_count, 1)),
        ],
        **compute_params(10**8, 4 * 10**6),
    )(inv_factor, points, vectors)

    rows_left, chosen, chosen_half = pl.pallas_call(
        rows_kernel,
        out_shape=[shape((row_count, 3 * panel), bf16), shape((panel, packed), bf16), shape((panel, 1))],
        scratch_shapes=[pltpu.VMEM((row_count, 3 * panel), bf16)],
        **compute_params(1, 1),
    )(*pieces, vectors, factor_right, pick, left, left_half)

    chunks = 8
    return pl.pallas_call(
        functools.partial(update_kernel, rows, cols),
        out_shape=shape((row_count, col_count)),
        out_specs=pl.BlockSpec(memory_space=pl.ANY),
        scratch_shapes=[
            pltpu.VMEM((chunks, row_count // chunks, col_count), f32),
            pltpu.VMEM((3 * panel, col_count), bf16),
            pltpu.VMEM((3 * panel, col_count), bf16),
            pltpu.SemaphoreType.DMA((chunks,)),
        ],
        **compute_params(4 * 10**9, 8 * 10**6),
    )(sent, vectors, factor_left, left, left_half, rows_left, chosen, chosen_half)


def solution(mesh):
    in_specs = (P("row", None), P("col", None), P(), P(), P(), P(), P("row"))
    out_specs = P("row", "col")
    return jax.shard_map(
        on_device, mesh=mesh, in_specs=in_specs, out_specs=out_specs, check_vma=False
    )
```
